32 devices in a mesh: seq: 4 (over z), head: 4 (over x, core), batch: 2 (over y).
Axes of the slice: x: 2, y: 2, z: 4, core: 2. Of those that a mesh axis runs over, the one named last changes fastest.
Arguments:
- tokens: bfloat16 [8, 1024, 1024], P('batch', 'seq'), may hold values from -6 to 6
- cotangent: bfloat16 [8, 1024, 1024], P('batch', 'seq'), may hold values from -6 to 6
- prefix: float32 [2, 64, 1024], P(None, None, 'head'), may hold values from -6 to 6
- first_moment: float32 [2, 64, 1024], P(None, None, 'head'), may hold values from -6 to 6
- second_moment: float32 [2, 64, 1024], P(None, None, 'head'), may hold values from 6.784 to 26.88
- w_qkv: bfloat16 [3, 1024, 1024], P(None, None, 'head'), may hold values from -0.1875 to 0.1875
- proj_bias: float32 [3, 1024], P(None, 'head'), may hold values from -4 to 4
- w_out: bfloat16 [1024, 1024], P('head'), may hold values from -1.5 to 1.5
- w_in: bfloat16 [1024, 4096], P(None, 'head'), may hold values from -0.1875 to 0.1875
- ffn_bias: float32 [4096], P('head'), may hold values from -4 to 4
- w_down: bfloat16 [4096, 1024], P('head'), may hold values from -0.09375 to 0.09375
- gains: float32 [2, 1024], replicated, may hold values from 0.5 to 1.5
- shifts: float32 [4, 1024], replicated, may hold values from -4 to 4
- lengths: int32 [8], P('batch'), may hold values from 32 to 1024, as said below
- key_mask: int32 [8, 1024], P('batch', 'seq'), may hold values 0 or 1
Outputs:
- layer_out: float32 [8, 1024, 1024], P('batch', 'seq')
- input_grad: float32 [8, 1024, 1024], P('batch', 'seq')
- prefix_grad: float32 [2, 64, 1024], P(None, None, 'head')
- new_prefix: float32 [2, 64, 1024], P(None, None, 'head')
- new_first: float32 [2, 64, 1024], P(None, None, 'head')
- new_second: float32 [2, 64, 1024], P(None, None, 'head')
The draws below stay inside these ranges and needn't reach their ends.
Inputs may be any that keep to these rules, and one draw needn't show every extreme that they name: `lengths`: one sequence of every draw has the length 1024.
All inputs are finite; a program needn't handle non-finite values. No bound on the sum of `key_mask` on one device may be relied on, other than what follows from the above.
Results may differ from the reference program's by a relative error of at most 0.029.
Values may be sent and summed in bfloat16 or wider, within the bound.
A program may use at most 128 MiB of HBM per device.

```python
import math
import jax
import jax.numpy as jnp
from jax import lax

D = 1024
HEADS = 16
HEAD_DIM = 64
FF = 4096
PREFIX = 64
STEP = 10
SEQ_LEN = 1024
SEQS = 8


def draw_lengths(key, part):
    first_key = jax.random.fold_in(key, 11)
    second_key = jax.random.fold_in(key, 23)
    drawn = jax.random.randint(first_key, (SEQS,), max(1, SEQ_LEN // 32), SEQ_LEN + 1, dtype=jnp.int32)
    chosen = jax.random.randint(second_key, (), 0, SEQS, dtype=jnp.int32)
    return jnp.where(jnp.arange(SEQS, dtype=jnp.int32) == chosen, SEQ_LEN, drawn).astype(jnp.int32)


def touch_ends(values, key, least, top_value):
    place = [jax.random.randint(jax.random.fold_in(key, axis), (), 0, length) for axis, length in enumerate(values.shape)]
    longest = values.shape.index(max(values.shape))
    next_to = place[:longest] + [(place[longest] + 1) % values.shape[longest]] + place[longest + 1:]
    return values.at[tuple(place)].set(least).at[tuple(next_to)].set(top_value)


def shard_levels(rng, shape, cuts, least, top_value):
    loudness = 1.0
    for position, blocks in cuts:
        draws = jax.random.uniform(jax.random.fold_in(jax.random.fold_in(rng, 6), position), (blocks,), jnp.float32, least / len(cuts), top_value / len(cuts))
        loudness = loudness * jnp.repeat(jnp.exp(draws), shape[position] // blocks).reshape((-1,) + (1,) * (len(shape) - 1 - position))
    return loudness


def noise(stream_key, extent, width, bound, split=(), held_as=jnp.bfloat16):
    entries = jax.random.normal(stream_key, extent, jnp.float32) * width
    if len(split) > 0:
        entries = shard_levels(stream_key, extent, split, -0.22, 0.18) * entries
    return jnp.clip(entries, min=-bound, max=bound).astype(held_as)


def setup_inputs(seed: int = 0) -> dict:
    splits = jax.random.split(jax.random.key(seed), 16)
    tokens = noise(splits[0], (SEQS, SEQ_LEN, D), 1.0, 6.0, ((0, 2), (1, 4)))
    cotangent = noise(splits[1], (SEQS, SEQ_LEN, D), 1.0, 6.0, ((0, 2), (1, 4)))
    prefix = noise(splits[2], (2, PREFIX, D), 1.0, 6.0, ((2, 4),), jnp.float32)
    first_moment = noise(splits[3], (2, PREFIX, D), (0.11 * (SEQS * SEQ_LEN) ** 0.5 / 8), 6.0, ((2, 4),), jnp.float32)
    second_moment = jnp.clip(jnp.exp(math.log(26.88) - 1.3768156 * jax.random.uniform(splits[4], (2, PREFIX, D), jnp.float32) ** shard_levels(splits[4], (2, PREFIX, D), ((2, 4),), -0.2, 0.2)), 6.784, 26.88)
    w_qkv = noise(splits[5], (3, D, D), D ** -0.5, 0.1875, ((2, 4),))
    proj_bias = noise(splits[6], (3, D), 0.3, 4.0, ((1, 4),), jnp.float32)
    w_out = noise(splits[7], (D, D), (max(1, D // 64)) ** -0.5, 1.5, ((0, 4),))
    w_in = noise(splits[8], (D, FF), D ** -0.5, 0.1875, ((1, 4),))
    ffn_bias = noise(splits[9], (FF,), 0.3, 4.0, ((0, 4),), jnp.float32)
    w_down = noise(splits[10], (FF, D), FF ** -0.5, 0.09375, ((0, 4),))
    gains = jnp.clip(1.0 + 0.1 * jax.random.normal(splits[11], (2, D), jnp.float32), 0.5, 1.5)
    shifts = noise(splits[12], (4, D), 0.3, 4.0, (), jnp.float32)
    lengths = draw_lengths(jax.random.fold_in(splits[15], 71), 0)
    key_mask = touch_ends((jax.random.randint(splits[14], (SEQS, SEQ_LEN), 0, 8) < 7).astype(jnp.int32), jax.random.fold_in(splits[14], 1), 0, 1)
    return dict(tokens=tokens, cotangent=cotangent, prefix=prefix, first_moment=first_moment, second_moment=second_moment, w_qkv=w_qkv, proj_bias=proj_bias, w_out=w_out, w_in=w_in, ffn_bias=ffn_bias, w_down=w_down, gains=gains, shifts=shifts, lengths=lengths, key_mask=key_mask)


@jax.custom_vjp
def low(v):
    return lax.optimization_barrier(v.astype(jnp.bfloat16)).astype(jnp.float32)

@jax.custom_vjp
def low_back(v):
    return v

def low_keep(v):
    return (low(v), None)

def low_pass(kept, grad):
    return (grad,)

def back_keep(v):
    return (v, None)

def back_low(kept, grad):
    return (low(grad),)
low.defvjp(low_keep, low_pass)
low_back.defvjp(back_keep, back_low)
NEG_FILL = -1e+30
NORM_EPSILON = 1e-05
BETA_ONE = 0.9
BETA_TWO = 0.95
LEARN_RATE = 0.8
WEIGHT_DECAY = 0.01
ADAM_EPSILON = 1e-08

def layer_norm(values_in, gain_row, shift_row):
    row_mean = lax.optimization_barrier(jnp.mean(values_in, axis=-1, keepdims=True))
    centred = values_in - row_mean
    spread = lax.optimization_barrier(jnp.mean(centred * centred, axis=-1, keepdims=True))
    return centred * lax.rsqrt(spread + NORM_EPSILON) * gain_row + shift_row

def attend(queries, token_keys, token_values, prefix_keys, prefix_values, sequence_live):
    score_scale = HEAD_DIM ** (-0.5)
    block_rows = min(512, SEQ_LEN)
    blocks = queries.reshape(SEQ_LEN // block_rows, block_rows, HEADS, HEAD_DIM)
    all_keys = jnp.concatenate([prefix_keys, token_keys], 0)
    all_values = jnp.concatenate([prefix_values, token_values], 0)
    open_keys = jnp.concatenate([jnp.ones((PREFIX,), dtype=bool), sequence_live])

    def one_block(block_data):
        scores = jnp.einsum('qhd,khd->hqk', block_data, all_keys, precision=lax.Precision.HIGHEST) * score_scale
        scores = jnp.where(open_keys[None, None, :], scores, NEG_FILL)
        scores = low_back(scores)
        probabilities = jax.nn.softmax(scores, axis=-1)
        return jnp.einsum('hqk,khd->qhd', low(probabilities), all_values, precision=lax.Precision.HIGHEST)
    result = lax.map(jax.checkpoint(one_block), blocks)
    return result.reshape(SEQ_LEN, HEADS * HEAD_DIM)

def one_sequence(sequence_rows, sequence_live, prefix_keys, prefix_values, w_qkv, proj_bias, w_out, w_in, ffn_bias, w_down, gains, shifts):
    projected = [jnp.dot(sequence_rows, w_qkv[index], precision=lax.Precision.HIGHEST) + proj_bias[index] for index in range(3)]
    queries, token_keys, token_values = [low_back(low(part)).reshape(SEQ_LEN, HEADS, HEAD_DIM) for part in projected]
    mixed = attend(queries, token_keys, token_values, prefix_keys, prefix_values, sequence_live)
    mixed = low_back(low(mixed))
    attention = low_back(jnp.dot(mixed, w_out, precision=lax.Precision.HIGHEST) + shifts[0])
    normed = layer_norm(sequence_rows + attention, gains[0], shifts[1])
    inner_sum = low_back(jnp.dot(low(normed), w_in, precision=lax.Precision.HIGHEST) + ffn_bias)
    activated = low(jax.nn.gelu(inner_sum, approximate=False))
    feed_forward = low_back(jnp.dot(activated, w_down, precision=lax.Precision.HIGHEST) + shifts[2])
    return layer_norm(normed + feed_forward, gains[1], shifts[3])

def reference(tokens, cotangent, prefix, first_moment, second_moment, w_qkv, proj_bias, w_out, w_in, ffn_bias, w_down, gains, shifts, lengths, key_mask):
    weights = tuple((array.astype(jnp.float32) for array in (w_qkv, proj_bias, w_out, w_in, ffn_bias, w_down, gains, shifts)))
    positions = jnp.arange(SEQ_LEN, dtype=jnp.int32)
    live_keys = (key_mask == 1) & (positions[None, :] < lengths[:, None])

    def forward(inputs, master):
        prefix_low = low(master)
        prefix_keys = prefix_low[0].reshape(PREFIX, HEADS, HEAD_DIM)
        prefix_values = prefix_low[1].reshape(PREFIX, HEADS, HEAD_DIM)

        def scan_step(carried, sequence_item):
            sequence_rows, sequence_live = sequence_item
            return (carried, one_sequence(sequence_rows, sequence_live, prefix_keys, prefix_values, *weights))
        return lax.scan(scan_step, jnp.zeros((), jnp.float32), (inputs, live_keys))[1]
    layer_value, pullback = jax.vjp(forward, tokens.astype(jnp.float32), prefix)
    input_grad, prefix_grad = pullback(cotangent.astype(jnp.float32))
    new_first = BETA_ONE * first_moment + (1.0 - BETA_ONE) * prefix_grad
    new_second = BETA_TWO * second_moment + (1.0 - BETA_TWO) * prefix_grad * prefix_grad
    first_hat = new_first / (1.0 - BETA_ONE ** STEP)
    second_hat = new_second / (1.0 - BETA_TWO ** STEP)
    new_prefix = prefix - LEARN_RATE * (first_hat / (jnp.sqrt(second_hat) + ADAM_EPSILON) + WEIGHT_DECAY * prefix)
    return (layer_value, input_grad, prefix_grad, new_prefix, new_first, new_second)
```

```python
import jax
import jax.numpy as jnp
from jax import lax
from jax.experimental import pallas as pl
from jax.experimental.pallas import tpu as pltpu
from jax.sharding import PartitionSpec as P

HEAD_DIM = 64
STEP = 10


NEG_FILL = -1e30
NORM_EPSILON = 1e-05
BETA_ONE = 0.9
BETA_TWO = 0.95
LEARN_RATE = 0.8
WEIGHT_DECAY = 0.01
ADAM_EPSILON = 1e-08


def shifted(value, axis, steps):
    count = lax.axis_size(axis)
    pairs = [(source, (source + steps) % count) for source in range(count)]
    return lax.ppermute(value, axis, pairs)


def layer_norm(values_in, gain_row, shift_row):
    row_mean = jnp.mean(values_in, axis=-1, keepdims=True)
    centred = values_in - row_mean
    spread = jnp.mean(centred * centred, axis=-1, keepdims=True)
    return centred * lax.rsqrt(spread + NORM_EPSILON) * gain_row + shift_row


def exact_gelu(values_in):
    return jax.nn.gelu(values_in, approximate=False)


def block_scores(queries, block_keys, block_bias, score_scale):
    scores = (
        jnp.einsum("shqd,shkd->shqk", queries, block_keys, preferred_element_type=jnp.float32)
        * score_scale
    )
    return scores + block_bias.astype(jnp.float32)[:, None, None, :]


def absorb(softmax_state, queries, block_keys, block_values, block_bias, score_scale):
    row_max, row_sum, weighted = softmax_state
    scores = block_scores(queries, block_keys, block_bias, score_scale)
    new_max = jnp.maximum(row_max, jnp.max(scores, axis=-1))
    fade_factor = jnp.exp(row_max - new_max)
    exp_scores = jnp.exp(scores - new_max[..., None])
    row_sum = row_sum * fade_factor + jnp.sum(exp_scores, axis=-1)
    weighted = weighted * fade_factor[..., None] + jnp.einsum(
        "shqk,shkd->shqd",
        exp_scores.astype(jnp.bfloat16),
        block_values,
        preferred_element_type=jnp.float32,
    )
    return (new_max, row_sum, weighted)


def back_block(
    queries, grad_att, log_total, row_delta, block_keys, block_values, block_bias, score_scale
):
    scores = block_scores(queries, block_keys, block_bias, score_scale)
    probabilities = jnp.exp(scores - log_total[..., None])
    grad_probs = jnp.einsum(
        "shqd,shkd->shqk", grad_att, block_values, preferred_element_type=jnp.float32
    )
    grad_scores = (probabilities * (grad_probs - row_delta[..., None])).astype(jnp.bfloat16)
    grad_queries = (
        jnp.einsum("shqk,shkd->shqd", grad_scores, block_keys, preferred_element_type=jnp.float32)
        * score_scale
    )
    grad_keys = (
        jnp.einsum("shqk,shqd->shkd", grad_scores, queries, preferred_element_type=jnp.float32)
        * score_scale
    )
    grad_values = jnp.einsum(
        "shqk,shqd->shkd",
        probabilities.astype(jnp.bfloat16),
        grad_att,
        preferred_element_type=jnp.float32,
    )
    return (grad_queries, grad_keys, grad_values)


def general_body(
    tokens,
    cotangent,
    prefix,
    first_moment,
    second_moment,
    w_qkv,
    proj_bias,
    w_out,
    w_in,
    ffn_bias,
    w_down,
    gains,
    shifts,
    lengths,
    key_mask,
):
    seqs_dev, shard_len, model_width = tokens.shape
    row_count = seqs_dev * shard_len
    local_width = w_qkv.shape[2]
    heads_dev = local_width // HEAD_DIM
    prefix_slots = prefix.shape[1]
    score_scale = HEAD_DIM ** (-0.5)
    cycle_size = lax.axis_size("seq")
    cycle_place = lax.axis_index("seq")
    flat_tokens = tokens.reshape(row_count, model_width)
    projected = (
        jnp.einsum("td,ide->ite", flat_tokens, w_qkv, preferred_element_type=jnp.float32)
        + proj_bias[:, None, :]
    )
    by_head = (
        projected.astype(jnp.bfloat16)
        .reshape(3, seqs_dev, shard_len, heads_dev, HEAD_DIM)
        .transpose(0, 1, 3, 2, 4)
    )
    queries = by_head[0]
    own_keys = by_head[1]
    own_values = by_head[2]
    positions = cycle_place * shard_len + lax.broadcasted_iota(jnp.int32, (seqs_dev, shard_len), 1)
    live_keys = (key_mask == 1) & (positions < lengths[:, None])
    own_bias = jnp.where(live_keys, 0.0, NEG_FILL).astype(jnp.bfloat16)
    prefix_low = (
        prefix.astype(jnp.bfloat16)
        .reshape(2, prefix_slots, heads_dev, HEAD_DIM)
        .transpose(0, 2, 1, 3)
    )
    pre_scores = (
        jnp.einsum("shqd,hpd->shqp", queries, prefix_low[0], preferred_element_type=jnp.float32)
        * score_scale
    )
    row_max = jnp.max(pre_scores, axis=-1)
    exp_prefix = jnp.exp(pre_scores - row_max[..., None])
    row_sum = jnp.sum(exp_prefix, axis=-1)
    weighted = jnp.einsum(
        "shqp,hpd->shqd",
        exp_prefix.astype(jnp.bfloat16),
        prefix_low[1],
        preferred_element_type=jnp.float32,
    )

    def visit_keys(softmax_state, block_keys, block_values, block_bias):
        return absorb(softmax_state, queries, block_keys, block_values, block_bias, score_scale)

    def forward_turn(turn_index, carried):
        softmax_state, block_keys, block_values, block_bias = carried
        softmax_state = visit_keys(softmax_state, block_keys, block_values, block_bias)
        block_keys, block_values, block_bias = shifted(
            (block_keys, block_values, block_bias), "seq", 1
        )
        return (softmax_state, block_keys, block_values, block_bias)

    carried = lax.fori_loop(
        0,
        cycle_size - 1,
        forward_turn,
        ((row_max, row_sum, weighted), own_keys, own_values, own_bias),
    )
    row_max, row_sum, weighted = visit_keys(carried[0], carried[1], carried[2], carried[3])
    log_total = row_max + jnp.log(row_sum)
    attended = weighted / row_sum[..., None]
    merged = attended.astype(jnp.bfloat16).transpose(0, 2, 1, 3).reshape(row_count, local_width)
    attention = (
        lax.psum(jnp.dot(merged, w_out, preferred_element_type=jnp.float32), "head") + shifts[0]
    )
    resid_one = flat_tokens.astype(jnp.float32) + attention
    normed, norm_one_back = jax.vjp(
        lambda values_in: layer_norm(values_in, gains[0], shifts[1]), resid_one
    )
    inner_sum = (
        jnp.dot(normed.astype(jnp.bfloat16), w_in, preferred_element_type=jnp.float32) + ffn_bias
    )
    activated, gelu_back = jax.vjp(exact_gelu, inner_sum)
    feed_forward = (
        lax.psum(
            jnp.dot(activated.astype(jnp.bfloat16), w_down, preferred_element_type=jnp.float32),
            "head",
        )
        + shifts[2]
    )
    layer_value, norm_two_back = jax.vjp(
        lambda values_in: layer_norm(values_in, gains[1], shifts[3]), normed + feed_forward
    )
    contract_last = (((1,), (1,)), ((), ()))
    (grad_two,) = norm_two_back(cotangent.reshape(row_count, model_width).astype(jnp.float32))
    grad_act = lax.dot_general(
        grad_two.astype(jnp.bfloat16), w_down, contract_last, preferred_element_type=jnp.float32
    )
    (grad_inner,) = gelu_back(grad_act)
    hidden_part = lax.dot_general(
        grad_inner.astype(jnp.bfloat16), w_in, contract_last, preferred_element_type=jnp.float32
    )
    grad_normed = grad_two + lax.psum(hidden_part, "head")
    (grad_one,) = norm_one_back(grad_normed)
    grad_merged = lax.dot_general(
        grad_one.astype(jnp.bfloat16), w_out, contract_last, preferred_element_type=jnp.float32
    )
    grad_att = (
        grad_merged.astype(jnp.bfloat16)
        .reshape(seqs_dev, shard_len, heads_dev, HEAD_DIM)
        .transpose(0, 2, 1, 3)
    )
    row_delta = jnp.sum(grad_att.astype(jnp.float32) * attended, axis=-1)
    pre_probs = jnp.exp(pre_scores - log_total[..., None])
    grad_pre_probs = jnp.einsum(
        "shqd,hpd->shqp", grad_att, prefix_low[1], preferred_element_type=jnp.float32
    )
    grad_pre_scores = (pre_probs * (grad_pre_probs - row_delta[..., None])).astype(jnp.bfloat16)
    grad_query_pre = (
        jnp.einsum(
            "shqp,hpd->shqd", grad_pre_scores, prefix_low[0], preferred_element_type=jnp.float32
        )
        * score_scale
    )
    grad_pre_keys = (
        jnp.einsum("shqp,shqd->hpd", grad_pre_scores, queries, preferred_element_type=jnp.float32)
        * score_scale
    )
    grad_pre_values = jnp.einsum(
        "shqp,shqd->hpd",
        pre_probs.astype(jnp.bfloat16),
        grad_att,
        preferred_element_type=jnp.float32,
    )
    prefix_terms = (
        jnp.stack([grad_pre_keys, grad_pre_values])
        .transpose(0, 2, 1, 3)
        .reshape(2, prefix_slots, local_width)
    )
    empty_grad = jnp.zeros(queries.shape, jnp.float32)

    def back_visit(query_side, key_side):
        return back_block(
            query_side[0],
            query_side[1],
            query_side[2],
            query_side[3],
            key_side[0],
            key_side[1],
            key_side[2],
            score_scale,
        )

    own_key_side = (own_keys, own_values, own_bias)

    def query_turn(turn_index, carried):
        grad_keys, grad_values, visit_queries, visit_grad, visit_total, visit_delta, visit_sum = (
            carried
        )
        turn_queries, turn_keys, turn_values = back_visit(
            (visit_queries, visit_grad, visit_total, visit_delta), own_key_side
        )
        moved = (
            shifted(visit_queries.astype(jnp.float32), "seq", 1).astype(visit_queries.dtype),
            shifted(visit_grad.astype(jnp.float32), "seq", 1).astype(visit_grad.dtype),
            shifted(visit_total, "seq", 1),
            shifted(visit_delta, "seq", 1),
            shifted(visit_sum + turn_queries, "seq", 1),
        )
        return (grad_keys + turn_keys, grad_values + turn_values) + moved

    carried = lax.fori_loop(
        0,
        cycle_size - 1,
        query_turn,
        (empty_grad, empty_grad, queries, grad_att, log_total, row_delta, grad_query_pre),
    )
    grad_keys, grad_values, visit_queries, visit_grad, visit_total, visit_delta, visit_sum = carried
    turn_queries, turn_keys, turn_values = back_visit(
        (visit_queries, visit_grad, visit_total, visit_delta), own_key_side
    )
    grad_keys = grad_keys + turn_keys
    grad_values = grad_values + turn_values
    grad_queries = shifted(visit_sum + turn_queries, "seq", 1)
    grad_rows = (
        jnp.stack([grad_queries, grad_keys, grad_values])
        .astype(jnp.bfloat16)
        .transpose(0, 1, 3, 2, 4)
        .reshape(3, row_count, local_width)
    )
    input_part = jnp.einsum("ite,ide->td", grad_rows, w_qkv, preferred_element_type=jnp.float32)
    input_grad = grad_one + lax.psum(input_part, "head")
    prefix_grad = lax.psum(prefix_terms, ("seq", "batch"))
    new_first = BETA_ONE * first_moment + (1.0 - BETA_ONE) * prefix_grad
    new_second = BETA_TWO * second_moment + (1.0 - BETA_TWO) * prefix_grad * prefix_grad
    first_hat = new_first / (1.0 - BETA_ONE**STEP)
    second_hat = new_second / (1.0 - BETA_TWO**STEP)
    new_prefix = prefix - LEARN_RATE * (
        first_hat / (jnp.sqrt(second_hat) + ADAM_EPSILON) + WEIGHT_DECAY * prefix
    )
    layer_out = layer_value.reshape(seqs_dev, shard_len, model_width)
    return (
        layer_out,
        input_grad.reshape(seqs_dev, shard_len, model_width),
        prefix_grad,
        new_prefix,
        new_first,
        new_second,
    )


BF = jnp.bfloat16
F32 = jnp.float32
MESH = pl.DeviceIdType.MESH
AHEAD = 3


def nn(left, right):
    return jnp.dot(left, right, preferred_element_type=F32)


def nt(left, right):
    return lax.dot_general(
        left, right, (((1,), (1,)), ((), ())), preferred_element_type=F32
    )


def remote(src, dst, send, recv, device):
    return pltpu.make_async_remote_copy(
        src, dst, send, recv, device_id=device, device_id_type=MESH
    )


def rows_at(start, size, step=64):
    return pl.ds(pl.multiple_of(start, step), size)


def places():
    z = lax.axis_index("seq")
    h = lax.axis_index("head")
    y = lax.axis_index("batch")
    return z, h, y


def member(h, u):
    chip, core = h // 2, lax.rem(h, 2)
    return 2 * lax.rem(chip + u // 2, 2) + lax.rem(core + u % 2, 2)


def z_peers(z):
    return [z + 1 - 2 * lax.rem(z, 2), 3 - z, lax.rem(z + 2, 4)]


def greet(devices):
    barrier = pltpu.get_barrier_semaphore()
    for device in devices:
        pl.semaphore_signal(barrier, inc=1, device_id=device, device_id_type=MESH)
    pl.semaphore_wait(barrier, len(devices))


def lane_masks():
    lane = lax.broadcasted_iota(jnp.int32, (1, 128), 1)
    inside = [lane < HEAD_DIM, lane >= HEAD_DIM]
    spare = [lane == HEAD_DIM, lane == 0]
    return inside, spare


def front_kernel(
    tokens,
    cot,
    w_qkv,
    w_out,
    w_in,
    w_down,
    prefix,
    proj_bias,
    ffn_bias,
    gains,
    shifts,
    lengths,
    key_mask,
    pt_o,
    q_o,
    k_o,
    v_o,
    rl_o,
    att_o,
    lo_o,
    g1_o,
    da_o,
    tok,
    cotg,
    bias_s,
    bias_g,
    wq,
    wo,
    wi,
    wd,
    fb,
    q_s,
    k_s,
    v_s,
    kx,
    vtx,
    pt,
    att_loc,
    att_all,
    rl_s,
    normed_s,
    xhat_s,
    nb_s,
    acc,
    act,
    gp,
    lo_s,
    da_s,
    loc_sem,
    out_sem,
    pt_sem,
    tok_sem,
    cot_sem,
    bias_sem,
    fb_sem,
    att_sem,
    core_sem,
    x_sem,
    y_sem,
    c1_sem,
    c2_sem,
):
    z, h, y = places()
    core = lax.rem(h, 2)
    hc, hx, hd_ = member(h, 1), member(h, 2), member(h, 3)
    dev_core, dev_x, dev_diag, dev_y = (z, hc, y), (z, hx, y), (z, hd_, y), (z, h, 1 - y)
    zs = z_peers(z)
    width = tok.shape[1]
    piece = width // 4
    slots = prefix.shape[1]
    total = 4 * width
    greet([dev_core, dev_x, dev_diag, dev_y] + [(zp, h, y) for zp in zs])

    half = width // 2
    my_half = rows_at(core * half, half)
    tok_copies, tok_forwards = [], []
    for k, zp in enumerate(zs):
        tok_copies.append(
            remote(tokens.at[zp, my_half], tok.at[z, my_half], tok_sem.at[0, k], tok_sem.at[1, k], (zp, h, y))
        )
        tok_forwards.append(
            remote(tok.at[zp, my_half], tok.at[zp, my_half], tok_sem.at[2, k], tok_sem.at[3, k], dev_core)
        )
    for copy in tok_copies:
        copy.start()
    tok_own = pltpu.make_async_copy(tokens.at[z], tok.at[z], loc_sem.at[0])
    tok_own.start()
    wq_own = pltpu.make_async_copy(w_qkv, wq, loc_sem.at[1])
    wq_own.start()

    chunks = [(w_out, wo, w_out.shape[0] // 2, 0, w_out.shape[0] // 2)]
    for src, dst in ((w_in, wi), (w_down, wd)):
        deep = src.shape[0] // 2
        for i in range(4):
            chunks.append((src, dst, deep, i * (deep // 4), deep // 4))
    over_x, over_y, core_x, core_y = [], [], [], []
    for i, (src, dst, deep, offset, size) in enumerate(chunks):
        mine = rows_at(y * deep + offset, size, 128)
        other = rows_at((1 - y) * deep + offset, size, 128)
        over_x.append(remote(src.at[mine], dst.at[h, mine], x_sem.at[0, i], x_sem.at[1, i], dev_x))
        over_y.append(remote(dst.at[hx, mine], dst.at[hx, mine], y_sem.at[0, i], y_sem.at[1, i], dev_y))
        core_x.append(remote(dst.at[hx, mine], dst.at[hx, mine], c1_sem.at[0, i], c1_sem.at[1, i], dev_core))
        core_y.append(remote(dst.at[hx, other], dst.at[hx, other], c2_sem.at[0, i], c2_sem.at[1, i], dev_core))
    n_chunks = len(chunks)
    for copy in over_x[:AHEAD]:
        copy.start()

    def serve_x(i):
        over_x[i].wait_recv()
        over_y[i].start()
        core_x[i].start()
        if i + AHEAD < n_chunks:
            over_x[i + AHEAD].start()

    def serve_y(i):
        over_y[i].wait_recv()
        core_y[i].start()

    own_weights, core_weights = [], []
    for i, (src, dst) in enumerate(((w_out, wo), (w_in, wi), (w_down, wd))):
        own_weights.append(pltpu.make_async_copy(src, dst.at[h], loc_sem.at[2 + i]))
        core_weights.append(remote(src, dst.at[h], core_sem.at[0, i], core_sem.at[1, i], dev_core))

    spot = lax.broadcasted_iota(jnp.int32, (8, width), 1) + z * width
    for s in range(4):
        live = (jnp.broadcast_to(key_mask[s : s + 1, :], (8, width)) == 1) & (spot < lengths[s])
        bias_s[s] = jnp.where(live, 0.0, NEG_FILL)
    bias_g[z] = bias_s[z]
    bias_copies = [
        remote(bias_s.at[zp], bias_g.at[z], bias_sem.at[0, k], bias_sem.at[1, k], (zp, h, y))
        for k, zp in enumerate(zs)
    ]
    fb[h] = jnp.broadcast_to(ffn_bias[...], fb.shape[1:])
    fb_copies = [
        remote(fb.at[h], fb.at[h], fb_sem.at[0, k], fb_sem.at[1, k], device)
        for k, device in enumerate((dev_core, dev_x, dev_diag))
    ]
    for copy in bias_copies + fb_copies:
        copy.start()
    for copy in own_weights + core_weights:
        copy.start()

    my_piece = rows_at(h * piece, piece)
    cot_copies = [
        remote(cot.at[zp, my_piece], cotg.at[z], cot_sem.at[0, k], cot_sem.at[1, k], (zp, h, y))
        for k, zp in enumerate(zs)
    ]
    cot_own = pltpu.make_async_copy(cot.at[z, my_piece], cotg.at[z], loc_sem.at[5])
    cot_own.start()

    inside, spare = lane_masks()

    pk = prefix[0].astype(BF)
    pv = prefix[1].astype(BF)
    k_s[total : total + slots, :] = pk
    v_s[total : total + slots, :] = pv
    for head in range(4):
        pair, par = head // 2, head % 2
        part = pk[:, 128 * pair : 128 * pair + 128].astype(F32)
        kx[head, total : total + slots, :] = jnp.where(inside[par], part, 0.0).astype(BF)
        vtx[head, HEAD_DIM:, :] = jnp.ones((vtx.shape[1] - HEAD_DIM, vtx.shape[2]), BF)

    def project(block):
        rows = tok[block]
        for i, target in enumerate((q_s, k_s, v_s)):
            value = (nn(rows, wq[i]) + proj_bias[i : i + 1, :]).astype(BF)
            if i == 0:
                value = (value.astype(F32) * HEAD_DIM**-0.5).astype(BF)
            for j in range(4):
                target[rows_at(j * width + block * piece, piece), :] = value[piece * j : piece * j + piece]
            if i == 1:
                column = jnp.broadcast_to(bias_g[block][0:1, :], (128, width)).T
                for head in range(4):
                    pair, par = head // 2, head % 2
                    part = value[:, 128 * pair : 128 * pair + 128].astype(F32)
                    ext = jnp.where(inside[par], part, jnp.where(spare[par], column, 0.0)).astype(BF)
                    for j in range(4):
                        kx[head, rows_at(j * width + block * piece, piece), :] = ext[piece * j : piece * j + piece]

    tok_own.wait()
    wq_own.wait()
    project(z)
    serve_x(0)
    for k, zp in enumerate(zs):
        serve_x(k + 1)
        serve_y(k)
        tok_copies[k].wait_recv()
        tok_forwards[k].start()
        bias_copies[k].wait_recv()
        if k == 0:
            for copy in cot_copies:
                copy.start()
        tok_forwards[k].wait_recv()
        project(zp)

    for i in range(4):
        flipped = v_s[i * width : (i + 1) * width, :].astype(F32).T.astype(BF)
        for head in range(4):
            vtx[head, 0:HEAD_DIM, i * width : (i + 1) * width] = flipped[HEAD_DIM * head : HEAD_DIM * (head + 1)]
    flipped = v_s[total : total + slots, :].astype(F32).T.astype(BF)
    for head in range(4):
        vtx[head, 0:HEAD_DIM, total : total + slots] = flipped[HEAD_DIM * head : HEAD_DIM * (head + 1)]

    q_out = pltpu.make_async_copy(q_s, q_o, out_sem.at[0])
    k_out = pltpu.make_async_copy(k_s, k_o, out_sem.at[1])
    v_out = pltpu.make_async_copy(v_s, v_o, out_sem.at[2])
    for copy in (q_out, k_out, v_out):
        copy.start()

    att_copies = []
    pt_out = []
    for step in range(4):
        u = 3 - step
        j = member(h, u) if u else h
        outs, recips = [], []
        for head in range(4):
            pair, par = head // 2, head % 2
            part = q_s[rows_at(j * width, width, width), 128 * pair : 128 * pair + 128].astype(F32)
            ext = jnp.where(inside[par], part, jnp.where(spare[par], 1.0, 0.0)).astype(BF)
            scores = nt(kx[head], ext)
            top = jnp.max(scores, axis=0, keepdims=True)
            weight = jnp.exp(scores - top).astype(BF)
            pt[head, j] = weight
            summed = nn(vtx[head], weight)
            recip = 1.0 / summed[HEAD_DIM : HEAD_DIM + 1]
            outs.append(summed[0:HEAD_DIM] * recip)
            recips.append(jnp.broadcast_to(recip, (32, width)))
            copy = pltpu.make_async_copy(pt.at[head, j], pt_o.at[head, j], pt_sem.at[step, head])
            copy.start()
            pt_out.append(copy)
        att_loc[j] = jnp.concatenate(outs, axis=0).T.astype(BF)
        rl_s[j] = jnp.concatenate(recips, axis=0).T
        if u:
            copy = remote(att_loc.at[j], att_all.at[h], att_sem.at[0, u], att_sem.at[1, u], (z, j, y))
            copy.start()
            att_copies.append(copy)
        else:
            att_all[h] = att_loc[h]
        if step < 2:
            serve_x(4 + step)
            serve_y(3 + step)
    rl_out = pltpu.make_async_copy(rl_s, rl_o, out_sem.at[3])
    att_out = pltpu.make_async_copy(att_loc, att_o, out_sem.at[4])
    rl_out.start()
    att_out.start()

    own_weights[0].wait()
    core_weights[0].wait_recv()
    core_x[0].wait_recv()
    core_y[0].wait_recv()
    for copy in att_copies:
        copy.wait_recv()
    attention = nn(att_all[0], wo[0])
    for j in range(1, 4):
        attention += nn(att_all[j], wo[j])
    mine = jnp.concatenate([tok[b, my_piece, :] for b in range(4)], axis=0).astype(F32)
    resid = mine + attention + shifts[0:1, :]
    centred = resid - jnp.mean(resid, axis=-1, keepdims=True)
    inverse_one = lax.rsqrt(jnp.mean(centred * centred, axis=-1, keepdims=True) + NORM_EPSILON)
    xhat = centred * inverse_one
    xhat_s[...] = xhat
    normed = xhat * gains[0:1, :] + shifts[1:2, :]
    normed_s[...] = normed
    nb_s[...] = normed.astype(BF)

    tile = 256
    tiles = wi.shape[2] // tile

    def ffn_in(quarter):
        @pl.loop(0, tiles)
        def _(n):
            cols = rows_at(n * tile, tile, tile)
            inner = nn(nb_s[...], wi[quarter, :, cols]) + fb[quarter, 0:1, cols]
            cdf = 0.5 * (1.0 + lax.erf(inner * 0.7071067811865476))
            act[quarter, :, cols] = (inner * cdf).astype(BF)
            gp[quarter, :, cols] = cdf + inner * (jnp.exp(-0.5 * inner * inner) * 0.3989422804014327)

    for copy in fb_copies:
        copy.wait_recv()
    own_weights[1].wait()
    core_weights[1].wait_recv()
    ffn_in(h)
    ffn_in(hc)
    serve_x(6)
    serve_y(5)
    for i in range(1, 5):
        core_x[i].wait_recv()
        core_y[i].wait_recv()
    ffn_in(hx)
    ffn_in(hd_)

    acc[...] = jnp.zeros(acc.shape, F32)

    def ffn_out(quarter, start, deep):
        span = rows_at(start, deep, deep)

        @pl.loop(0, tiles)
        def _(n):
            cols = rows_at(n * tile, tile, tile)
            acc[:, cols] += nn(act[quarter, :, span], wd[quarter, span, cols])

    own_weights[2].wait()
    core_weights[2].wait_recv()
    deep = wd.shape[1]
    ffn_out(h, 0, deep)
    serve_x(7)
    serve_y(6)
    ffn_out(hc, 0, deep)
    serve_x(8)
    serve_y(7)
    for i in range(5, 9):
        core_x[i].wait_recv()
    ffn_out(hx, y * (deep // 2), deep // 2)
    ffn_out(hd_, y * (deep // 2), deep // 2)
    serve_y(8)
    ffn_out(hx, (1 - y) * (deep // 2), deep // 2)
    for i in range(5, 9):
        core_y[i].wait_recv()
    ffn_out(hd_, (1 - y) * (deep // 2), deep // 2)

    resid = normed_s[...] + acc[...] + shifts[2:3, :]
    centred = resid - jnp.mean(resid, axis=-1, keepdims=True)
    inverse = lax.rsqrt(jnp.mean(centred * centred, axis=-1, keepdims=True) + NORM_EPSILON)
    xhat = centred * inverse
    lo_s[...] = (xhat * gains[1:2, :] + shifts[3:4, :]).astype(BF)
    lo_out = pltpu.make_async_copy(lo_s, lo_o, out_sem.at[5])
    lo_out.start()
    cot_own.wait()
    for copy in cot_copies:
        copy.wait_recv()
    dy = jnp.concatenate([cotg[b] for b in range(4)], axis=0).astype(F32) * gains[1:2, :]
    g_two = inverse * (
        dy - jnp.mean(dy, axis=-1, keepdims=True) - xhat * jnp.mean(dy * xhat, axis=-1, keepdims=True)
    )
    acc[...] = g_two
    nb_s[...] = g_two.astype(BF)

    @pl.loop(0, 4)
    def _(quarter):
        @pl.loop(0, tiles)
        def _(n):
            cols = rows_at(n * tile, tile, tile)
            d_act = nt(nb_s[...], wd[quarter, cols, :])
            act[quarter, :, cols] = (d_act * gp[quarter, :, cols]).astype(BF)

    @pl.loop(0, 4)
    def _(quarter):
        @pl.loop(0, tiles)
        def _(n):
            cols = rows_at(n * tile, tile, tile)
            acc[:, cols] += nt(act[quarter], wi[quarter, cols, :])

    dy = acc[...] * gains[0:1, :]
    xhat = xhat_s[...]
    g_one = inverse_one * (
        dy - jnp.mean(dy, axis=-1, keepdims=True) - xhat * jnp.mean(dy * xhat, axis=-1, keepdims=True)
    )
    acc[...] = g_one
    g1_out = pltpu.make_async_copy(acc, g1_o, out_sem.at[6])
    g1_out.start()
    low = g_one.astype(BF)
    for j in range(4):
        da_s[j] = nt(low, wo[j]).astype(BF)
    da_out = pltpu.make_async_copy(da_s, da_o, out_sem.at[7])
    da_out.start()

    for copy in [q_out, k_out, v_out, rl_out, att_out, lo_out, g1_out, da_out] + pt_out:
        copy.wait()
    sent = tok_copies + tok_forwards + over_x + over_y + core_x + core_y + core_weights
    for copy in sent + bias_copies + fb_copies + cot_copies + att_copies:
        copy.wait_send()


def front(tokens, cot, w_qkv, w_out, w_in, w_down, prefix, proj_bias, ffn_bias, gains, shifts, lengths, key_mask):
    seqs, width, model = tokens.shape
    local = w_qkv.shape[2]
    hidden = w_in.shape[1]
    slots = prefix.shape[1]
    total = seqs * width
    keys = total + slots
    dma = pltpu.SemaphoreType.DMA
    hbm = pl.BlockSpec(memory_space=pl.ANY)
    vmem = pl.BlockSpec(memory_space=pltpu.VMEM)
    shape = jax.ShapeDtypeStruct
    return pl.pallas_call(
        front_kernel,
        name="front",
        out_shape=(
            shape((4, 4, keys, width), BF),
            shape((total, local), BF),
            shape((keys, local), BF),
            shape((keys, local), BF),
            shape((4, width, 128), F32),
            shape((4, width, local), BF),
            shape((width, model), BF),
            shape((width, model), F32),
            shape((4, width, local), BF),
        ),
        in_specs=[hbm] * 6 + [vmem] * 5 + [pl.BlockSpec(memory_space=pltpu.SMEM), vmem],
        out_specs=(hbm,) * 9,
        scratch_shapes=[
            pltpu.VMEM((4, width, model), BF),
            pltpu.VMEM((4, width // 4, model), BF),
            pltpu.VMEM((4, 8, width), F32),
            pltpu.VMEM((4, 8, width), F32),
            pltpu.VMEM((3, model, local), BF),
            pltpu.VMEM((4, local, model), BF),
            pltpu.VMEM((4, model, hidden), BF),
            pltpu.VMEM((4, hidden, model), BF),
            pltpu.VMEM((4, 8, hidden), F32),
            pltpu.VMEM((total, local), BF),
            pltpu.VMEM((keys, local), BF),
            pltpu.VMEM((keys, local), BF),
            pltpu.VMEM((4, keys, 128), BF),
            pltpu.VMEM((4, HEAD_DIM + 16, keys), BF),
            pltpu.VMEM((4, 4, keys, width), BF),
            pltpu.VMEM((4, width, local), BF),
            pltpu.VMEM((4, width, local), BF),
            pltpu.VMEM((4, width, 128), F32),
            pltpu.VMEM((width, model), F32),
            pltpu.VMEM((width, model), F32),
            pltpu.VMEM((width, model), BF),
            pltpu.VMEM((width, model), F32),
            pltpu.VMEM((4, width, hidden), BF),
            pltpu.VMEM((4, width, hidden), F32),
            pltpu.VMEM((width, model), BF),
            pltpu.VMEM((4, width, local), BF),
            dma((6,)),
            dma((8,)),
            dma((4, 4)),
            dma((4, 3)),
            dma((2, 3)),
            dma((2, 3)),
            dma((2, 3)),
            dma((2, 4)),
            dma((2, 3)),
            dma((2, 9)),
            dma((2, 9)),
            dma((2, 9)),
            dma((2, 9)),
        ],
        compiler_params=pltpu.CompilerParams(
            collective_id=0, has_side_effects=True, vmem_limit_bytes=60 * 2**20
        ),
        cost_estimate=pl.CostEstimate(flops=15 * 10**9, bytes_accessed=40 * 2**20, transcendentals=6 * 10**6),
    )(tokens, cot, w_qkv, w_out, w_in, w_down, prefix, proj_bias, ffn_bias, gains, shifts, lengths, key_mask)


def back_plain(pt, q, k, v, rl, att, lo, g1, da, w_qkv, prefix_slots):
    heads = 4
    total = q.shape[0]
    width = g1.shape[0]
    piece = width // 4
    d_att = lax.all_to_all(da, "head", 0, 0)
    rows = lambda value: value.reshape(4, width, heads, HEAD_DIM).transpose(2, 0, 1, 3)
    d_att_h, att_h = rows(d_att), rows(att)
    q_h = rows(q)
    k_h = k.reshape(-1, heads, HEAD_DIM).transpose(1, 0, 2)
    v_h = v.reshape(-1, heads, HEAD_DIM).transpose(1, 0, 2)
    delta = jnp.sum(d_att_h.astype(F32) * att_h.astype(F32), -1)
    recip = jnp.stack([rl[:, :, 32 * i] for i in range(heads)])
    probs = pt.astype(F32) * recip[:, :, None, :]
    dp = jnp.einsum("hkd,hjrd->hjkr", v_h, d_att_h, preferred_element_type=F32)
    ds = (probs * (dp - delta[:, :, None, :])).astype(BF)
    dq = jnp.einsum("hjkr,hkd->hjrd", ds, k_h, preferred_element_type=F32) * HEAD_DIM**-0.5
    dk = jnp.einsum("hjkr,hjrd->hkd", ds, q_h, preferred_element_type=F32)
    dv = jnp.einsum("hjkr,hjrd->hkd", probs.astype(BF), d_att_h, preferred_element_type=F32)
    flat = lambda value: value.transpose(1, 0, 2).reshape(-1, heads * HEAD_DIM)
    dk, dv = flat(dk), flat(dv)
    dq = dq.transpose(1, 2, 0, 3).reshape(total, heads * HEAD_DIM)
    prefix_terms = jnp.stack([dk[total:], dv[total:]])
    grads = jnp.stack([dq, dk[:total], dv[:total]]).astype(BF)
    part = jnp.einsum("ite,ide->td", grads, w_qkv, preferred_element_type=F32)
    own = lax.psum_scatter(part, "head", scatter_dimension=0, tiled=True) + g1
    both = jnp.stack([own, lo.astype(F32)]).reshape(2, 4, piece, -1)
    moved = lax.all_to_all(both, "seq", 1, 1)
    full = lax.all_gather(moved, "head", axis=2, tiled=True)
    return full[1], full[0], prefix_terms


def body(*args):
    (tokens, cotangent, prefix, first_moment, second_moment, w_qkv, proj_bias, w_out, w_in, ffn_bias) = args[:10]
    w_down, gains, shifts, lengths, key_mask = args[10:]
    fits = (
        lax.axis_size("seq") == 4
        and lax.axis_size("head") == 4
        and lax.axis_size("batch") == 2
        and tokens.shape == (4, 256, 1024)
        and w_qkv.shape == (3, 1024, 256)
        and w_in.shape == (1024, 1024)
        and prefix.shape[1] == 64
    )
    if not fits:
        return general_body(*args)
    parts = front(
        tokens, cotangent, w_qkv, w_out, w_in, w_down, prefix, proj_bias, ffn_bias.reshape(1, -1), gains, shifts,
        lengths, key_mask,
    )
    layer_out, input_grad, prefix_terms = back_plain(*parts, w_qkv, prefix.shape[1])
    prefix_grad = lax.psum(prefix_terms, ("seq", "batch"))
    new_first = BETA_ONE * first_moment + (1.0 - BETA_ONE) * prefix_grad
    new_second = BETA_TWO * second_moment + (1.0 - BETA_TWO) * prefix_grad * prefix_grad
    first_hat = new_first / (1.0 - BETA_ONE**STEP)
    second_hat = new_second / (1.0 - BETA_TWO**STEP)
    new_prefix = prefix - LEARN_RATE * (
        first_hat / (jnp.sqrt(second_hat) + ADAM_EPSILON) + WEIGHT_DECAY * prefix
    )
    return layer_out, input_grad, prefix_grad, new_prefix, new_first, new_second


def solution(mesh):
    placed = (
        P("batch", "seq", None),
        P("batch", "seq", None),
        P(None, None, "head"),
        P(None, None, "head"),
        P(None, None, "head"),
        P(None, None, "head"),
        P(None, "head"),
        P("head", None),
        P(None, "head"),
        P("head"),
        P("head", None),
        P(),
        P(),
        P("batch"),
        P("batch", "seq"),
    )
    return jax.shard_map(
        body,
        mesh=mesh,
        in_specs=placed,
        out_specs=(
            P("batch", "seq", None),
            P("batch", "seq", None),
            P(None, None, "head"),
            P(None, None, "head"),
            P(None, None, "head"),
            P(None, None, "head"),
        ),
        check_vma=False,
    )
```

```python
import jax
import jax.numpy as jnp
from jax import lax
from jax.experimental import pallas as pl
from jax.experimental.pallas import tpu as pltpu
from jax.sharding import PartitionSpec as P

HEAD_DIM = 64
STEP = 10


NEG_FILL = -1e30
NORM_EPSILON = 1e-05
BETA_ONE = 0.9
BETA_TWO = 0.95
LEARN_RATE = 0.8
WEIGHT_DECAY = 0.01
ADAM_EPSILON = 1e-08


def shifted(value, axis, steps):
    count = lax.axis_size(axis)
    pairs = [(source, (source + steps) % count) for source in range(count)]
    return lax.ppermute(value, axis, pairs)


def layer_norm(values_in, gain_row, shift_row):
    row_mean = jnp.mean(values_in, axis=-1, keepdims=True)
    centred = values_in - row_mean
    spread = jnp.mean(centred * centred, axis=-1, keepdims=True)
    return centred * lax.rsqrt(spread + NORM_EPSILON) * gain_row + shift_row


def exact_gelu(values_in):
    return jax.nn.gelu(values_in, approximate=False)


def block_scores(queries, block_keys, block_bias, score_scale):
    scores = (
        jnp.einsum("shqd,shkd->shqk", queries, block_keys, preferred_element_type=jnp.float32)
        * score_scale
    )
    return scores + block_bias.astype(jnp.float32)[:, None, None, :]


def absorb(softmax_state, queries, block_keys, block_values, block_bias, score_scale):
    row_max, row_sum, weighted = softmax_state
    scores = block_scores(queries, block_keys, block_bias, score_scale)
    new_max = jnp.maximum(row_max, jnp.max(scores, axis=-1))
    fade_factor = jnp.exp(row_max - new_max)
    exp_scores = jnp.exp(scores - new_max[..., None])
    row_sum = row_sum * fade_factor + jnp.sum(exp_scores, axis=-1)
    weighted = weighted * fade_factor[..., None] + jnp.einsum(
        "shqk,shkd->shqd",
        exp_scores.astype(jnp.bfloat16),
        block_values,
        preferred_element_type=jnp.float32,
    )
    return (new_max, row_sum, weighted)


def back_block(
    queries, grad_att, log_total, row_delta, block_keys, block_values, block_bias, score_scale
):
    scores = block_scores(queries, block_keys, block_bias, score_scale)
    probabilities = jnp.exp(scores - log_total[..., None])
    grad_probs = jnp.einsum(
        "shqd,shkd->shqk", grad_att, block_values, preferred_element_type=jnp.float32
    )
    grad_scores = (probabilities * (grad_probs - row_delta[..., None])).astype(jnp.bfloat16)
    grad_queries = (
        jnp.einsum("shqk,shkd->shqd", grad_scores, block_keys, preferred_element_type=jnp.float32)
        * score_scale
    )
    grad_keys = (
        jnp.einsum("shqk,shqd->shkd", grad_scores, queries, preferred_element_type=jnp.float32)
        * score_scale
    )
    grad_values = jnp.einsum(
        "shqk,shqd->shkd",
        probabilities.astype(jnp.bfloat16),
        grad_att,
        preferred_element_type=jnp.float32,
    )
    return (grad_queries, grad_keys, grad_values)


def general_body(
    tokens,
    cotangent,
    prefix,
    first_moment,
    second_moment,
    w_qkv,
    proj_bias,
    w_out,
    w_in,
    ffn_bias,
    w_down,
    gains,
    shifts,
    lengths,
    key_mask,
):
    seqs_dev, shard_len, model_width = tokens.shape
    row_count = seqs_dev * shard_len
    local_width = w_qkv.shape[2]
    heads_dev = local_width // HEAD_DIM
    prefix_slots = prefix.shape[1]
    score_scale = HEAD_DIM ** (-0.5)
    cycle_size = lax.axis_size("seq")
    cycle_place = lax.axis_index("seq")
    flat_tokens = tokens.reshape(row_count, model_width)
    projected = (
        jnp.einsum("td,ide->ite", flat_tokens, w_qkv, preferred_element_type=jnp.float32)
        + proj_bias[:, None, :]
    )
    by_head = (
        projected.astype(jnp.bfloat16)
        .reshape(3, seqs_dev, shard_len, heads_dev, HEAD_DIM)
        .transpose(0, 1, 3, 2, 4)
    )
    queries = by_head[0]
    own_keys = by_head[1]
    own_values = by_head[2]
    positions = cycle_place * shard_len + lax.broadcasted_iota(jnp.int32, (seqs_dev, shard_len), 1)
    live_keys = (key_mask == 1) & (positions < lengths[:, None])
    own_bias = jnp.where(live_keys, 0.0, NEG_FILL).astype(jnp.bfloat16)
    prefix_low = (
        prefix.astype(jnp.bfloat16)
        .reshape(2, prefix_slots, heads_dev, HEAD_DIM)
        .transpose(0, 2, 1, 3)
    )
    pre_scores = (
        jnp.einsum("shqd,hpd->shqp", queries, prefix_low[0], preferred_element_type=jnp.float32)
        * score_scale
    )
    row_max = jnp.max(pre_scores, axis=-1)
    exp_prefix = jnp.exp(pre_scores - row_max[..., None])
    row_sum = jnp.sum(exp_prefix, axis=-1)
    weighted = jnp.einsum(
        "shqp,hpd->shqd",
        exp_prefix.astype(jnp.bfloat16),
        prefix_low[1],
        preferred_element_type=jnp.float32,
    )

    def visit_keys(softmax_state, block_keys, block_values, block_bias):
        return absorb(softmax_state, queries, block_keys, block_values, block_bias, score_scale)

    def forward_turn(turn_index, carried):
        softmax_state, block_keys, block_values, block_bias = carried
        softmax_state = visit_keys(softmax_state, block_keys, block_values, block_bias)
        block_keys, block_values, block_bias = shifted(
            (block_keys, block_values, block_bias), "seq", 1
        )
        return (softmax_state, block_keys, block_values, block_bias)

    carried = lax.fori_loop(
        0,
        cycle_size - 1,
        forward_turn,
        ((row_max, row_sum, weighted), own_keys, own_values, own_bias),
    )
    row_max, row_sum, weighted = visit_keys(carried[0], carried[1], carried[2], carried[3])
    log_total = row_max + jnp.log(row_sum)
    attended = weighted / row_sum[..., None]
    merged = attended.astype(jnp.bfloat16).transpose(0, 2, 1, 3).reshape(row_count, local_width)
    attention = (
        lax.psum(jnp.dot(merged, w_out, preferred_element_type=jnp.float32), "head") + shifts[0]
    )
    resid_one = flat_tokens.astype(jnp.float32) + attention
    normed, norm_one_back = jax.vjp(
        lambda values_in: layer_norm(values_in, gains[0], shifts[1]), resid_one
    )
    inner_sum = (
        jnp.dot(normed.astype(jnp.bfloat16), w_in, preferred_element_type=jnp.float32) + ffn_bias
    )
    activated, gelu_back = jax.vjp(exact_gelu, inner_sum)
    feed_forward = (
        lax.psum(
            jnp.dot(activated.astype(jnp.bfloat16), w_down, preferred_element_type=jnp.float32),
            "head",
        )
        + shifts[2]
    )
    layer_value, norm_two_back = jax.vjp(
        lambda values_in: layer_norm(values_in, gains[1], shifts[3]), normed + feed_forward
    )
    contract_last = (((1,), (1,)), ((), ()))
    (grad_two,) = norm_two_back(cotangent.reshape(row_count, model_width).astype(jnp.float32))
    grad_act = lax.dot_general(
        grad_two.astype(jnp.bfloat16), w_down, contract_last, preferred_element_type=jnp.float32
    )
    (grad_inner,) = gelu_back(grad_act)
    hidden_part = lax.dot_general(
        grad_inner.astype(jnp.bfloat16), w_in, contract_last, preferred_element_type=jnp.float32
    )
    grad_normed = grad_two + lax.psum(hidden_part, "head")
    (grad_one,) = norm_one_back(grad_normed)
    grad_merged = lax.dot_general(
        grad_one.astype(jnp.bfloat16), w_out, contract_last, preferred_element_type=jnp.float32
    )
    grad_att = (
        grad_merged.astype(jnp.bfloat16)
        .reshape(seqs_dev, shard_len, heads_dev, HEAD_DIM)
        .transpose(0, 2, 1, 3)
    )
    row_delta = jnp.sum(grad_att.astype(jnp.float32) * attended, axis=-1)
    pre_probs = jnp.exp(pre_scores - log_total[..., None])
    grad_pre_probs = jnp.einsum(
        "shqd,hpd->shqp", grad_att, prefix_low[1], preferred_element_type=jnp.float32
    )
    grad_pre_scores = (pre_probs * (grad_pre_probs - row_delta[..., None])).astype(jnp.bfloat16)
    grad_query_pre = (
        jnp.einsum(
            "shqp,hpd->shqd", grad_pre_scores, prefix_low[0], preferred_element_type=jnp.float32
        )
        * score_scale
    )
    grad_pre_keys = (
        jnp.einsum("shqp,shqd->hpd", grad_pre_scores, queries, preferred_element_type=jnp.float32)
        * score_scale
    )
    grad_pre_values = jnp.einsum(
        "shqp,shqd->hpd",
        pre_probs.astype(jnp.bfloat16),
        grad_att,
        preferred_element_type=jnp.float32,
    )
    prefix_terms = (
        jnp.stack([grad_pre_keys, grad_pre_values])
        .transpose(0, 2, 1, 3)
        .reshape(2, prefix_slots, local_width)
    )
    empty_grad = jnp.zeros(queries.shape, jnp.float32)

    def back_visit(query_side, key_side):
        return back_block(
            query_side[0],
            query_side[1],
            query_side[2],
            query_side[3],
            key_side[0],
            key_side[1],
            key_side[2],
            score_scale,
        )

    own_key_side = (own_keys, own_values, own_bias)

    def query_turn(turn_index, carried):
        grad_keys, grad_values, visit_queries, visit_grad, visit_total, visit_delta, visit_sum = (
            carried
        )
        turn_queries, turn_keys, turn_values = back_visit(
            (visit_queries, visit_grad, visit_total, visit_delta), own_key_side
        )
        moved = (
            shifted(visit_queries.astype(jnp.float32), "seq", 1).astype(visit_queries.dtype),
            shifted(visit_grad.astype(jnp.float32), "seq", 1).astype(visit_grad.dtype),
            shifted(visit_total, "seq", 1),
            shifted(visit_delta, "seq", 1),
            shifted(visit_sum + turn_queries, "seq", 1),
        )
        return (grad_keys + turn_keys, grad_values + turn_values) + moved

    carried = lax.fori_loop(
        0,
        cycle_size - 1,
        query_turn,
        (empty_grad, empty_grad, queries, grad_att, log_total, row_delta, grad_query_pre),
    )
    grad_keys, grad_values, visit_queries, visit_grad, visit_total, visit_delta, visit_sum = carried
    turn_queries, turn_keys, turn_values = back_visit(
        (visit_queries, visit_grad, visit_total, visit_delta), own_key_side
    )
    grad_keys = grad_keys + turn_keys
    grad_values = grad_values + turn_values
    grad_queries = shifted(visit_sum + turn_queries, "seq", 1)
    grad_rows = (
        jnp.stack([grad_queries, grad_keys, grad_values])
        .astype(jnp.bfloat16)
        .transpose(0, 1, 3, 2, 4)
        .reshape(3, row_count, local_width)
    )
    input_part = jnp.einsum("ite,ide->td", grad_rows, w_qkv, preferred_element_type=jnp.float32)
    input_grad = grad_one + lax.psum(input_part, "head")
    prefix_grad = lax.psum(prefix_terms, ("seq", "batch"))
    new_first = BETA_ONE * first_moment + (1.0 - BETA_ONE) * prefix_grad
    new_second = BETA_TWO * second_moment + (1.0 - BETA_TWO) * prefix_grad * prefix_grad
    first_hat = new_first / (1.0 - BETA_ONE**STEP)
    second_hat = new_second / (1.0 - BETA_TWO**STEP)
    new_prefix = prefix - LEARN_RATE * (
        first_hat / (jnp.sqrt(second_hat) + ADAM_EPSILON) + WEIGHT_DECAY * prefix
    )
    layer_out = layer_value.reshape(seqs_dev, shard_len, model_width)
    return (
        layer_out,
        input_grad.reshape(seqs_dev, shard_len, model_width),
        prefix_grad,
        new_prefix,
        new_first,
        new_second,
    )


BF = jnp.bfloat16
F32 = jnp.float32
MESH = pl.DeviceIdType.MESH
AHEAD = 3


def nn(left, right):
    return jnp.dot(left, right, preferred_element_type=F32)


def nt(left, right):
    return lax.dot_general(
        left, right, (((1,), (1,)), ((), ())), preferred_element_type=F32
    )


def remote(src, dst, send, recv, device):
    return pltpu.make_async_remote_copy(
        src, dst, send, recv, device_id=device, device_id_type=MESH
    )


def rows_at(start, size, step=64):
    return pl.ds(pl.multiple_of(start, step), size)


def places():
    z = lax.axis_index("seq")
    h = lax.axis_index("head")
    y = lax.axis_index("batch")
    return z, h, y


def member(h, u):
    chip, core = h // 2, lax.rem(h, 2)
    return 2 * lax.rem(chip + u // 2, 2) + lax.rem(core + u % 2, 2)


def z_peers(z):
    return [z + 1 - 2 * lax.rem(z, 2), 3 - z, lax.rem(z + 2, 4)]


def greet(devices):
    barrier = pltpu.get_barrier_semaphore()
    for device in devices:
        pl.semaphore_signal(barrier, inc=1, device_id=device, device_id_type=MESH)
    pl.semaphore_wait(barrier, len(devices))


def lane_masks():
    lane = lax.broadcasted_iota(jnp.int32, (1, 128), 1)
    inside = [lane < HEAD_DIM, lane >= HEAD_DIM]
    spare = [lane == HEAD_DIM, lane == 0]
    return inside, spare


def front_kernel(
    tokens,
    cot,
    w_qkv,
    w_out,
    w_in,
    w_down,
    prefix,
    proj_bias,
    ffn_bias,
    gains,
    shifts,
    lengths,
    key_mask,
    pt_o,
    q_o,
    k_o,
    v_o,
    rl_o,
    att_o,
    loz_o,
    lox_o,
    g1_o,
    da_o,
    tok,
    cotg,
    bias_s,
    bias_g,
    wq,
    wo,
    wi,
    wd,
    fb,
    q_s,
    k_s,
    v_s,
    kx,
    vtx,
    pt,
    att_loc,
    att_all,
    rl_s,
    normed_s,
    xhat_s,
    nb_s,
    acc,
    act,
    gp,
    lo_s,
    da_s,
    loc_sem,
    out_sem,
    pt_sem,
    tok_sem,
    cot_sem,
    bias_sem,
    fb_sem,
    att_sem,
    core_sem,
    x_sem,
    y_sem,
    c1_sem,
    c2_sem,
    lo_sem,
):
    z, h, y = places()
    core = lax.rem(h, 2)
    hc, hx, hd_ = member(h, 1), member(h, 2), member(h, 3)
    dev_core, dev_x, dev_diag, dev_y = (z, hc, y), (z, hx, y), (z, hd_, y), (z, h, 1 - y)
    zs = z_peers(z)
    width = tok.shape[1]
    piece = width // 4
    slots = prefix.shape[1]
    total = 4 * width
    greet([dev_core, dev_x, dev_diag, dev_y] + [(zp, h, y) for zp in zs])

    half = width // 2
    my_half = rows_at(core * half, half)
    tok_copies, tok_forwards = [], []
    for k, zp in enumerate(zs):
        tok_copies.append(
            remote(tokens.at[zp, my_half], tok.at[z, my_half], tok_sem.at[0, k], tok_sem.at[1, k], (zp, h, y))
        )
        tok_forwards.append(
            remote(tok.at[zp, my_half], tok.at[zp, my_half], tok_sem.at[2, k], tok_sem.at[3, k], dev_core)
        )
    for copy in tok_copies:
        copy.start()
    tok_own = pltpu.make_async_copy(tokens.at[z], tok.at[z], loc_sem.at[0])
    tok_own.start()
    wq_own = pltpu.make_async_copy(w_qkv, wq, loc_sem.at[1])
    wq_own.start()

    chunks = [(w_out, wo, w_out.shape[0] // 2, 0, w_out.shape[0] // 2)]
    for src, dst in ((w_in, wi), (w_down, wd)):
        deep = src.shape[0] // 2
        for i in range(4):
            chunks.append((src, dst, deep, i * (deep // 4), deep // 4))
    over_x, over_y, core_x, core_y = [], [], [], []
    for i, (src, dst, deep, offset, size) in enumerate(chunks):
        mine = rows_at(y * deep + offset, size, 128)
        other = rows_at((1 - y) * deep + offset, size, 128)
        over_x.append(remote(src.at[mine], dst.at[h, mine], x_sem.at[0, i], x_sem.at[1, i], dev_x))
        over_y.append(remote(dst.at[hx, mine], dst.at[hx, mine], y_sem.at[0, i], y_sem.at[1, i], dev_y))
        core_x.append(remote(dst.at[hx, mine], dst.at[hx, mine], c1_sem.at[0, i], c1_sem.at[1, i], dev_core))
        core_y.append(remote(dst.at[hx, other], dst.at[hx, other], c2_sem.at[0, i], c2_sem.at[1, i], dev_core))
    n_chunks = len(chunks)
    for copy in over_x[:AHEAD]:
        copy.start()

    def serve_x(i):
        over_x[i].wait_recv()
        over_y[i].start()
        core_x[i].start()
        if i + AHEAD < n_chunks:
            over_x[i + AHEAD].start()

    def serve_y(i):
        over_y[i].wait_recv()
        core_y[i].start()

    own_weights, core_weights = [], []
    for i, (src, dst) in enumerate(((w_out, wo), (w_in, wi), (w_down, wd))):
        own_weights.append(pltpu.make_async_copy(src, dst.at[h], loc_sem.at[2 + i]))
        core_weights.append(remote(src, dst.at[h], core_sem.at[0, i], core_sem.at[1, i], dev_core))

    spot = lax.broadcasted_iota(jnp.int32, (8, width), 1) + z * width
    for s in range(4):
        live = (jnp.broadcast_to(key_mask[s : s + 1, :], (8, width)) == 1) & (spot < lengths[s])
        bias_s[s] = jnp.where(live, 0.0, NEG_FILL)
    bias_g[z] = bias_s[z]
    bias_copies = [
        remote(bias_s.at[zp], bias_g.at[z], bias_sem.at[0, k], bias_sem.at[1, k], (zp, h, y))
        for k, zp in enumerate(zs)
    ]
    fb[h] = jnp.broadcast_to(ffn_bias[...], fb.shape[1:])
    fb_copies = [
        remote(fb.at[h], fb.at[h], fb_sem.at[0, k], fb_sem.at[1, k], device)
        for k, device in enumerate((dev_core, dev_x, dev_diag))
    ]
    for copy in bias_copies + fb_copies:
        copy.start()
    for copy in own_weights + core_weights:
        copy.start()

    my_piece = rows_at(h * piece, piece)
    cot_copies = [
        remote(cot.at[zp, my_piece], cotg.at[z], cot_sem.at[0, k], cot_sem.at[1, k], (zp, h, y))
        for k, zp in enumerate(zs)
    ]
    cot_own = pltpu.make_async_copy(cot.at[z, my_piece], cotg.at[z], loc_sem.at[5])
    cot_own.start()

    inside, spare = lane_masks()

    pk = prefix[0].astype(BF)
    pv = prefix[1].astype(BF)
    k_s[total : total + slots, :] = pk
    v_s[total : total + slots, :] = pv
    for head in range(4):
        pair, par = head // 2, head % 2
        part = pk[:, 128 * pair : 128 * pair + 128].astype(F32)
        kx[head, total : total + slots, :] = jnp.where(inside[par], part, 0.0).astype(BF)
        vtx[head, HEAD_DIM:, :] = jnp.ones((vtx.shape[1] - HEAD_DIM, vtx.shape[2]), BF)

    def project(block):
        rows = tok[block]
        for i, target in enumerate((q_s, k_s, v_s)):
            value = (nn(rows, wq[i]) + proj_bias[i : i + 1, :]).astype(BF)
            if i == 0:
                value = (value.astype(F32) * HEAD_DIM**-0.5).astype(BF)
            for j in range(4):
                target[rows_at(j * width + block * piece, piece), :] = value[piece * j : piece * j + piece]
            if i == 1:
                column = jnp.broadcast_to(bias_g[block][0:1, :], (128, width)).T
                for head in range(4):
                    pair, par = head // 2, head % 2
                    part = value[:, 128 * pair : 128 * pair + 128].astype(F32)
                    ext = jnp.where(inside[par], part, jnp.where(spare[par], column, 0.0)).astype(BF)
                    for j in range(4):
                        kx[head, rows_at(j * width + block * piece, piece), :] = ext[piece * j : piece * j + piece]

    tok_own.wait()
    wq_own.wait()
    project(z)
    serve_x(0)
    for k, zp in enumerate(zs):
        serve_x(k + 1)
        serve_y(k)
        tok_copies[k].wait_recv()
        tok_forwards[k].start()
        bias_copies[k].wait_recv()
        if k == 0:
            for copy in cot_copies:
                copy.start()
        tok_forwards[k].wait_recv()
        project(zp)

    for i in range(4):
        flipped = v_s[i * width : (i + 1) * width, :].astype(F32).T.astype(BF)
        for head in range(4):
            vtx[head, 0:HEAD_DIM, i * width : (i + 1) * width] = flipped[HEAD_DIM * head : HEAD_DIM * (head + 1)]
    flipped = v_s[total : total + slots, :].astype(F32).T.astype(BF)
    for head in range(4):
        vtx[head, 0:HEAD_DIM, total : total + slots] = flipped[HEAD_DIM * head : HEAD_DIM * (head + 1)]

    q_out = pltpu.make_async_copy(q_s, q_o, out_sem.at[0])
    k_out = pltpu.make_async_copy(k_s, k_o, out_sem.at[1])
    v_out = pltpu.make_async_copy(v_s, v_o, out_sem.at[2])
    for copy in (q_out, k_out, v_out):
        copy.start()

    att_copies = []
    pt_out = []
    for step in range(4):
        u = 3 - step
        j = member(h, u) if u else h
        outs, recips = [], []
        for head in range(4):
            pair, par = head // 2, head % 2
            part = q_s[rows_at(j * width, width, width), 128 * pair : 128 * pair + 128].astype(F32)
            ext = jnp.where(inside[par], part, jnp.where(spare[par], 1.0, 0.0)).astype(BF)
            scores = nt(kx[head], ext)
            top = jnp.max(scores, axis=0, keepdims=True)
            weight = jnp.exp(scores - top).astype(BF)
            pt[head, j] = weight
            summed = nn(vtx[head], weight)
            recip = 1.0 / summed[HEAD_DIM : HEAD_DIM + 1]
            outs.append(summed[0:HEAD_DIM] * recip)
            recips.append(jnp.broadcast_to(recip, (32, width)))
            copy = pltpu.make_async_copy(pt.at[head, j], pt_o.at[head, j], pt_sem.at[step, head])
            copy.start()
            pt_out.append(copy)
        att_loc[j] = jnp.concatenate(outs, axis=0).T.astype(BF)
        rl_s[j] = jnp.concatenate(recips, axis=0).T
        if u:
            copy = remote(att_loc.at[j], att_all.at[h], att_sem.at[0, u], att_sem.at[1, u], (z, j, y))
            copy.start()
            att_copies.append(copy)
        else:
            att_all[h] = att_loc[h]
        if step < 2:
            serve_x(4 + step)
            serve_y(3 + step)
    rl_out = pltpu.make_async_copy(rl_s, rl_o, out_sem.at[3])
    att_out = pltpu.make_async_copy(att_loc, att_o, out_sem.at[4])
    rl_out.start()
    att_out.start()

    own_weights[0].wait()
    core_weights[0].wait_recv()
    core_x[0].wait_recv()
    core_y[0].wait_recv()
    for copy in att_copies:
        copy.wait_recv()
    attention = nn(att_all[0], wo[0])
    for j in range(1, 4):
        attention += nn(att_all[j], wo[j])
    mine = jnp.concatenate([tok[b, my_piece, :] for b in range(4)], axis=0).astype(F32)
    resid = mine + attention + shifts[0:1, :]
    centred = resid - jnp.mean(resid, axis=-1, keepdims=True)
    inverse_one = lax.rsqrt(jnp.mean(centred * centred, axis=-1, keepdims=True) + NORM_EPSILON)
    xhat = centred * inverse_one
    xhat_s[...] = xhat
    normed = xhat * gains[0:1, :] + shifts[1:2, :]
    normed_s[...] = normed
    nb_s[...] = normed.astype(BF)

    tile = 256
    tiles = wi.shape[2] // tile

    def ffn_in(quarter):
        @pl.loop(0, tiles)
        def _(n):
            cols = rows_at(n * tile, tile, tile)
            inner = nn(nb_s[...], wi[quarter, :, cols]) + fb[quarter, 0:1, cols]
            cdf = 0.5 * (1.0 + lax.erf(inner * 0.7071067811865476))
            act[quarter, :, cols] = (inner * cdf).astype(BF)
            gp[quarter, :, cols] = cdf + inner * (jnp.exp(-0.5 * inner * inner) * 0.3989422804014327)

    for copy in fb_copies:
        copy.wait_recv()
    own_weights[1].wait()
    core_weights[1].wait_recv()
    ffn_in(h)
    ffn_in(hc)
    serve_x(6)
    serve_y(5)
    for i in range(1, 5):
        core_x[i].wait_recv()
        core_y[i].wait_recv()
    ffn_in(hx)
    ffn_in(hd_)

    acc[...] = jnp.zeros(acc.shape, F32)

    def ffn_out(quarter, start, deep):
        span = rows_at(start, deep, deep)

        @pl.loop(0, tiles)
        def _(n):
            cols = rows_at(n * tile, tile, tile)
            acc[:, cols] += nn(act[quarter, :, span], wd[quarter, span, cols])

    own_weights[2].wait()
    core_weights[2].wait_recv()
    deep = wd.shape[1]
    ffn_out(h, 0, deep)
    serve_x(7)
    serve_y(6)
    ffn_out(hc, 0, deep)
    serve_x(8)
    serve_y(7)
    for i in range(5, 9):
        core_x[i].wait_recv()
    ffn_out(hx, y * (deep // 2), deep // 2)
    ffn_out(hd_, y * (deep // 2), deep // 2)
    serve_y(8)
    ffn_out(hx, (1 - y) * (deep // 2), deep // 2)
    for i in range(5, 9):
        core_y[i].wait_recv()
    ffn_out(hd_, (1 - y) * (deep // 2), deep // 2)

    resid = normed_s[...] + acc[...] + shifts[2:3, :]
    centred = resid - jnp.mean(resid, axis=-1, keepdims=True)
    inverse = lax.rsqrt(jnp.mean(centred * centred, axis=-1, keepdims=True) + NORM_EPSILON)
    xhat = centred * inverse
    lo_s[...] = (xhat * gains[1:2, :] + shifts[3:4, :]).astype(BF)
    lo_copies = []
    for k, zp in enumerate(zs):
        block = rows_at(zp * piece, piece)
        lo_copies.append(remote(lo_s.at[block], loz_o.at[z], lo_sem.at[0, k], lo_sem.at[1, k], (zp, h, y)))
    for b in range(4):
        block = pl.ds(b * piece, piece)
        lo_copies.append(remote(lo_s.at[block], lox_o.at[b], lo_sem.at[0, 3 + b], lo_sem.at[1, 3 + b], dev_x))
    lo_out = pltpu.make_async_copy(lo_s.at[rows_at(z * piece, piece)], loz_o.at[z], out_sem.at[5])
    for copy in lo_copies + [lo_out]:
        copy.start()
    cot_own.wait()
    for copy in cot_copies:
        copy.wait_recv()
    dy = jnp.concatenate([cotg[b] for b in range(4)], axis=0).astype(F32) * gains[1:2, :]
    g_two = inverse * (
        dy - jnp.mean(dy, axis=-1, keepdims=True) - xhat * jnp.mean(dy * xhat, axis=-1, keepdims=True)
    )
    acc[...] = g_two
    nb_s[...] = g_two.astype(BF)

    @pl.loop(0, 4)
    def _(quarter):
        @pl.loop(0, tiles)
        def _(n):
            cols = rows_at(n * tile, tile, tile)
            d_act = nt(nb_s[...], wd[quarter, cols, :])
            act[quarter, :, cols] = (d_act * gp[quarter, :, cols]).astype(BF)

    @pl.loop(0, 4)
    def _(quarter):
        @pl.loop(0, tiles)
        def _(n):
            cols = rows_at(n * tile, tile, tile)
            acc[:, cols] += nt(act[quarter], wi[quarter, cols, :])

    dy = acc[...] * gains[0:1, :]
    xhat = xhat_s[...]
    g_one = inverse_one * (
        dy - jnp.mean(dy, axis=-1, keepdims=True) - xhat * jnp.mean(dy * xhat, axis=-1, keepdims=True)
    )
    acc[...] = g_one
    g1_out = pltpu.make_async_copy(acc, g1_o, out_sem.at[6])
    g1_out.start()
    low = g_one.astype(BF)
    for j in range(4):
        da_s[j] = nt(low, wo[j]).astype(BF)
    da_out = pltpu.make_async_copy(da_s, da_o, out_sem.at[7])
    da_out.start()

    for copy in [q_out, k_out, v_out, rl_out, att_out, lo_out, g1_out, da_out] + pt_out:
        copy.wait()
    for copy in lo_copies:
        copy.wait()
    sent = tok_copies + tok_forwards + over_x + over_y + core_x + core_y + core_weights
    for copy in sent + bias_copies + fb_copies + cot_copies + att_copies:
        copy.wait_send()


def front(tokens, cot, w_qkv, w_out, w_in, w_down, prefix, proj_bias, ffn_bias, gains, shifts, lengths, key_mask):
    seqs, width, model = tokens.shape
    local = w_qkv.shape[2]
    hidden = w_in.shape[1]
    slots = prefix.shape[1]
    total = seqs * width
    keys = total + slots
    dma = pltpu.SemaphoreType.DMA
    hbm = pl.BlockSpec(memory_space=pl.ANY)
    vmem = pl.BlockSpec(memory_space=pltpu.VMEM)
    shape = jax.ShapeDtypeStruct
    return pl.pallas_call(
        front_kernel,
        name="front",
        out_shape=(
            shape((4, 4, keys, width), BF),
            shape((total, local), BF),
            shape((keys, local), BF),
            shape((keys, local), BF),
            shape((4, width, 128), F32),
            shape((4, width, local), BF),
            shape((4, width // 4, model), BF),
            shape((4, width // 4, model), BF),
            shape((width, model), F32),
            shape((4, width, local), BF),
        ),
        in_specs=[hbm] * 6 + [vmem] * 5 + [pl.BlockSpec(memory_space=pltpu.SMEM), vmem],
        out_specs=(hbm,) * 10,
        scratch_shapes=[
            pltpu.VMEM((4, width, model), BF),
            pltpu.VMEM((4, width // 4, model), BF),
            pltpu.VMEM((4, 8, width), F32),
            pltpu.VMEM((4, 8, width), F32),
            pltpu.VMEM((3, model, local), BF),
            pltpu.VMEM((4, local, model), BF),
            pltpu.VMEM((4, model, hidden), BF),
            pltpu.VMEM((4, hidden, model), BF),
            pltpu.VMEM((4, 8, hidden), F32),
            pltpu.VMEM((total, local), BF),
            pltpu.VMEM((keys, local), BF),
            pltpu.VMEM((keys, local), BF),
            pltpu.VMEM((4, keys, 128), BF),
            pltpu.VMEM((4, HEAD_DIM + 16, keys), BF),
            pltpu.VMEM((4, 4, keys, width), BF),
            pltpu.VMEM((4, width, local), BF),
            pltpu.VMEM((4, width, local), BF),
            pltpu.VMEM((4, width, 128), F32),
            pltpu.VMEM((width, model), F32),
            pltpu.VMEM((width, model), F32),
            pltpu.VMEM((width, model), BF),
            pltpu.VMEM((width, model), F32),
            pltpu.VMEM((4, width, hidden), BF),
            pltpu.VMEM((4, width, hidden), F32),
            pltpu.VMEM((width, model), BF),
            pltpu.VMEM((4, width, local), BF),
            dma((6,)),
            dma((8,)),
            dma((4, 4)),
            dma((4, 3)),
            dma((2, 3)),
            dma((2, 3)),
            dma((2, 3)),
            dma((2, 4)),
            dma((2, 3)),
            dma((2, 9)),
            dma((2, 9)),
            dma((2, 9)),
            dma((2, 9)),
            dma((2, 7)),
        ],
        compiler_params=pltpu.CompilerParams(
            collective_id=0, has_side_effects=True, vmem_limit_bytes=60 * 2**20
        ),
        cost_estimate=pl.CostEstimate(flops=15 * 10**9, bytes_accessed=40 * 2**20, transcendentals=6 * 10**6),
    )(tokens, cot, w_qkv, w_out, w_in, w_down, prefix, proj_bias, ffn_bias, gains, shifts, lengths, key_mask)


def back_kernel(
    pt_i,
    q_i,
    k_i,
    v_i,
    rl_i,
    att_i,
    loz_i,
    lox_i,
    g1_i,
    da_i,
    w_qkv,
    lo_o,
    ig_o,
    pre_o,
    pt,
    ds,
    q_s,
    k_s,
    v_s,
    rl_s,
    att_s,
    g1_s,
    wq,
    da_all,
    vx,
    kt,
    dox,
    dq_s,
    core_out,
    core_in,
    x_out,
    x_in,
    fin,
    pre_part,
    pre_land,
    pre_sum,
    loc_sem,
    pt_sem,
    da_sem,
    loz_sem,
    loc2_sem,
    lo_core_sem,
    part_core_sem,
    part_x_sem,
    igz_sem,
    igx_sem,
    igc_sem,
    igcx_sem,
    pre_sem,
    pre2_sem,
):
    z, h, y = places()
    hc, hx, hd_ = member(h, 1), member(h, 2), member(h, 3)
    dev_core, dev_x, dev_diag = (z, hc, y), (z, hx, y), (z, hd_, y)
    zs = z_peers(z)
    width = g1_s.shape[0]
    piece = width // 4
    slots = pre_part.shape[1]
    total = 4 * width
    group = 2 * z + y
    others = [lax.rem(group + d, 8) for d in range(1, 8)]
    greet([dev_core, dev_x, dev_diag] + [(g // 2, h, lax.rem(g, 2)) for g in others])

    my_piece = rows_at(h * piece, piece)
    x_piece = rows_at(hx * piece, piece)

    da_copies = []
    for u in (2, 3, 1):
        j = member(h, u)
        da_copies.append(remote(da_i.at[j], da_all.at[h], da_sem.at[0, u], da_sem.at[1, u], (z, j, y)))
    for copy in da_copies:
        copy.start()
    da_wait = {2: da_copies[0], 3: da_copies[1], 1: da_copies[2]}

    loads = []
    for i, (src, dst) in enumerate(
        ((da_i.at[h], da_all.at[h]), (v_i, v_s), (k_i, k_s), (rl_i, rl_s), (att_i, att_s), (q_i, q_s), (w_qkv, wq), (g1_i, g1_s))
    ):
        loads.append(pltpu.make_async_copy(src, dst, loc_sem.at[i]))
    for copy in loads[:5]:
        copy.start()
    order = [h, hc, hx, hd_]
    pt_loads = []
    for u, j in enumerate(order):
        copy = pltpu.make_async_copy(pt_i.at[:, j], pt.at[:, j], pt_sem.at[u])
        copy.start()
        pt_loads.append(copy)
    for copy in loads[5:]:
        copy.start()

    loz_copies, lo_forwards = [], []
    for k, zp in enumerate(zs):
        loz_copies.append(remote(lox_i.at[zp], lo_o.at[z, x_piece], loz_sem.at[0, k], loz_sem.at[1, k], (zp, h, y)))
        lo_forwards.append(
            remote(lo_o.at[zp, x_piece], lo_o.at[zp, x_piece], lo_core_sem.at[0, k], lo_core_sem.at[1, k], dev_core)
        )
    for copy in loz_copies:
        copy.start()
    lo_local = [
        pltpu.make_async_copy(loz_i, lo_o.at[:, my_piece], loc2_sem.at[0]),
        pltpu.make_async_copy(lox_i.at[z], lo_o.at[z, x_piece], loc2_sem.at[1]),
    ]
    lo_core = [
        remote(loz_i, lo_o.at[:, my_piece], lo_core_sem.at[0, 3], lo_core_sem.at[1, 3], dev_core),
        remote(lox_i.at[z], lo_o.at[z, x_piece], lo_core_sem.at[0, 4], lo_core_sem.at[1, 4], dev_core),
    ]
    for copy in lo_local + lo_core:
        copy.start()

    lane = lax.broadcasted_iota(jnp.int32, (1, 128), 1)
    inside = [lane < HEAD_DIM, lane >= HEAD_DIM]
    spare_hi = [lane == HEAD_DIM, lane == 0]
    spare_lo = [lane == HEAD_DIM + 1, lane == 1]

    loads[1].wait()
    for head in range(4):
        pair, par = head // 2, head % 2
        part = v_s[:, 128 * pair : 128 * pair + 128].astype(F32)
        ones = jnp.where(spare_hi[par] | spare_lo[par], 1.0, 0.0)
        vx[head] = jnp.where(inside[par], part, ones).astype(BF)
    loads[2].wait()
    for i in range(5):
        low, size = i * width, width if i < 4 else slots
        flipped = k_s[low : low + size, :].astype(F32).T.astype(BF)
        for head in range(4):
            kt[head, :, low : low + size] = flipped[HEAD_DIM * head : HEAD_DIM * (head + 1)]
    loads[0].wait()
    loads[3].wait()
    loads[4].wait()

    for u, j in enumerate(order):
        if u:
            da_wait[u].wait_recv()
        pt_loads[u].wait()
        grads = []
        for head in range(4):
            pair, par = head // 2, head % 2
            lanes = slice(128 * pair, 128 * pair + 128)
            d_out = da_all[j, :, lanes].astype(F32)
            recip = rl_s[j, :, 32 * head : 32 * head + 1]
            delta = recip * jnp.sum(
                jnp.where(inside[par], d_out * att_s[j, :, lanes].astype(F32), 0.0), axis=-1, keepdims=True
            )
            high = delta.astype(BF).astype(F32)
            ext = jnp.where(spare_hi[par], -high, jnp.where(spare_lo[par], high - delta, 0.0))
            ext = jnp.where(inside[par], d_out * recip, ext).astype(BF)
            dox[head, j] = ext
            d_probs = nt(vx[head], ext).astype(BF)
            d_scores = pt[head, j] * d_probs
            ds[head, j] = d_scores
            grads.append(nn(kt[head], d_scores))
        dq_s[j] = (jnp.concatenate(grads, axis=0).T * HEAD_DIM**-0.5).astype(BF)
        if u >= 1:
            loz_copies[u - 1].wait_recv()
            lo_forwards[u - 1].start()

    def key_side(rows, source, right):
        halves = []
        for pair in range(2):
            sides = []
            for par in range(2):
                head = 2 * pair + par
                value = nn(source[head, 0, rows, :], right(head, 0, pair))
                for j in range(1, 4):
                    value += nn(source[head, j, rows, :], right(head, j, pair))
                sides.append(value)
            halves.append(jnp.where(inside[0], sides[0], sides[1]))
        return jnp.concatenate(halves, axis=-1)

    def d_values(rows):
        return key_side(rows, pt, lambda head, j, pair: dox[head, j])

    def d_keys(rows):
        return key_side(
            rows, ds, lambda head, j, pair: q_s[j * width : (j + 1) * width, 128 * pair : 128 * pair + 128]
        )

    for copy in loads[5:]:
        copy.wait()

    def partial(i):
        rows = rows_at(i * width, width, width)
        dk = d_keys(rows).astype(BF)
        dv = d_values(rows).astype(BF)
        return nt(dq_s[i], wq[0]) + nt(dk, wq[1]) + nt(dv, wq[2])

    part_core = [
        remote(core_out.at[i], core_in.at[i], part_core_sem.at[0, i], part_core_sem.at[1, i], dev_core) for i in range(2)
    ]
    blocks = zs + [z]
    part_x = []
    for k, b in enumerate(blocks):
        rows = rows_at(b * piece, piece)
        part_x.append(remote(x_out.at[rows], x_in.at[rows], part_x_sem.at[0, k], part_x_sem.at[1, k], dev_x))

    core_out[0] = partial(hd_).astype(BF)
    part_core[0].start()
    mine = partial(hx)
    part_core[0].wait_recv()
    x_out[...] = (mine + core_in[0].astype(F32)).astype(BF)
    for copy in part_x:
        copy.start()

    edge = pl.ds(total, slots)
    pre_part[0] = d_keys(edge)
    pre_part[1] = d_values(edge)
    few = slots // 8
    pre_copies, pre_back = [], []
    for d, g in enumerate(others):
        device = (g // 2, h, lax.rem(g, 2))
        pre_copies.append(
            remote(pre_part.at[:, rows_at(g * few, few, few)], pre_land.at[d], pre_sem.at[0, d], pre_sem.at[1, d], device)
        )
        mine_rows = rows_at(group * few, few, few)
        pre_back.append(
            remote(pre_sum.at[:, mine_rows], pre_sum.at[:, mine_rows], pre2_sem.at[0, d], pre2_sem.at[1, d], device)
        )
    for copy in pre_copies:
        copy.start()

    core_out[1] = partial(hc).astype(BF)
    part_core[1].start()
    g1_s[...] += partial(h)
    part_core[1].wait_recv()
    g1_s[...] += core_in[1].astype(F32)

    igz, igx, igc, igcx = [], [], [], []
    for k, b in enumerate(blocks):
        rows = rows_at(b * piece, piece)
        source = ig_o.at[b, my_piece]
        if k < 3:
            igz.append(remote(fin.at[rows], ig_o.at[z, my_piece], igz_sem.at[0, k], igz_sem.at[1, k], (b, h, y)))
        else:
            source = fin.at[rows]
        igx.append(remote(source, ig_o.at[b, my_piece], igx_sem.at[0, k], igx_sem.at[1, k], dev_x))
        igc.append(remote(source, ig_o.at[b, my_piece], igc_sem.at[0, k], igc_sem.at[1, k], dev_core))
        igcx.append(
            remote(ig_o.at[b, x_piece], ig_o.at[b, x_piece], igcx_sem.at[0, k], igcx_sem.at[1, k], dev_core)
        )
    ig_local = pltpu.make_async_copy(fin.at[rows_at(z * piece, piece)], ig_o.at[z, my_piece], loc2_sem.at[2])
    for k, b in enumerate(blocks):
        rows = rows_at(b * piece, piece)
        part_x[k].wait_recv()
        fin[rows, :] = (g1_s[rows, :] + x_in[rows, :].astype(F32)).astype(BF)
        if k < 3:
            igz[k].start()
        else:
            ig_local.start()
        if k == 1:
            for copy in pre_copies:
                copy.wait_recv()
            mine_rows = rows_at(group * few, few, few)
            for i in range(2):
                term = pre_part[i, mine_rows, :]
                for d in range(7):
                    term += pre_land[d, i]
                pre_sum[i, mine_rows, :] = term
            for copy in pre_back:
                copy.start()
    for k in range(3):
        igz[k].wait_recv()
        igx[k].start()
        igc[k].start()
        if k == 0:
            igx[3].start()
            igc[3].start()
    for copy in pre_back:
        copy.wait_recv()
    pre_o[...] = pre_sum[...]
    for k in (0, 3, 1, 2):
        igx[k].wait_recv()
        igcx[k].start()
    for copy in igc + igcx + lo_forwards + lo_core:
        copy.wait_recv()
    for copy in lo_local + [ig_local]:
        copy.wait()
    sent = da_copies + loz_copies + lo_forwards + lo_core + part_core + part_x + igz + igx + igc + igcx
    for copy in sent + pre_copies + pre_back:
        copy.wait_send()


def back(pt, q, k, v, rl, att, loz, lox, g1, da, w_qkv):
    width, model = g1.shape
    keys, local = k.shape
    total = 4 * width
    slots = keys - total
    dma = pltpu.SemaphoreType.DMA
    hbm = pl.BlockSpec(memory_space=pl.ANY)
    vmem = pl.BlockSpec(memory_space=pltpu.VMEM)
    shape = jax.ShapeDtypeStruct
    return pl.pallas_call(
        back_kernel,
        name="back",
        out_shape=(
            shape((4, width, model), BF),
            shape((4, width, model), BF),
            shape((2, slots, local), F32),
        ),
        in_specs=[hbm] * 11,
        out_specs=(hbm, hbm, vmem),
        scratch_shapes=[
            pltpu.VMEM((4, 4, keys, width), BF),
            pltpu.VMEM((4, 4, keys, width), BF),
            pltpu.VMEM((total, local), BF),
            pltpu.VMEM((keys, local), BF),
            pltpu.VMEM((keys, local), BF),
            pltpu.VMEM((4, width, 128), F32),
            pltpu.VMEM((4, width, local), BF),
            pltpu.VMEM((width, model), F32),
            pltpu.VMEM((3, model, local), BF),
            pltpu.VMEM((4, width, local), BF),
            pltpu.VMEM((4, keys, 128), BF),
            pltpu.VMEM((4, HEAD_DIM, keys), BF),
            pltpu.VMEM((4, 4, width, 128), BF),
            pltpu.VMEM((4, width, local), BF),
            pltpu.VMEM((2, width, model), BF),
            pltpu.VMEM((2, width, model), BF),
            pltpu.VMEM((width, model), BF),
            pltpu.VMEM((width, model), BF),
            pltpu.VMEM((width, model), BF),
            pltpu.VMEM((2, slots, local), F32),
            pltpu.VMEM((7, 2, slots // 8, local), F32),
            pltpu.VMEM((2, slots, local), F32),
            dma((8,)),
            dma((4,)),
            dma((2, 4)),
            dma((2, 3)),
            dma((3,)),
            dma((2, 5)),
            dma((2, 2)),
            dma((2, 4)),
            dma((2, 3)),
            dma((2, 4)),
            dma((2, 4)),
            dma((2, 4)),
            dma((2, 7)),
            dma((2, 7)),
        ],
        compiler_params=pltpu.CompilerParams(
            collective_id=1, has_side_effects=True, vmem_limit_bytes=60 * 2**20
        ),
        cost_estimate=pl.CostEstimate(flops=8 * 10**9, bytes_accessed=30 * 2**20, transcendentals=0),
    )(pt, q, k, v, rl, att, loz, lox, g1, da, w_qkv)


def body(*args):
    (tokens, cotangent, prefix, first_moment, second_moment, w_qkv, proj_bias, w_out, w_in, ffn_bias) = args[:10]
    w_down, gains, shifts, lengths, key_mask = args[10:]
    fits = (
        lax.axis_size("seq") == 4
        and lax.axis_size("head") == 4
        and lax.axis_size("batch") == 2
        and tokens.shape == (4, 256, 1024)
        and w_qkv.shape == (3, 1024, 256)
        and w_in.shape == (1024, 1024)
        and prefix.shape[1] == 64
    )
    if not fits:
        return general_body(*args)
    parts = front(
        tokens, cotangent, w_qkv, w_out, w_in, w_down, prefix, proj_bias, ffn_bias.reshape(1, -1), gains, shifts,
        lengths, key_mask,
    )
    layer_out, input_grad, prefix_grad = back(*parts, w_qkv)
    layer_out, input_grad = layer_out.astype(F32), input_grad.astype(F32)
    new_first = BETA_ONE * first_moment + (1.0 - BETA_ONE) * prefix_grad
    new_second = BETA_TWO * second_moment + (1.0 - BETA_TWO) * prefix_grad * prefix_grad
    first_hat = new_first / (1.0 - BETA_ONE**STEP)
    second_hat = new_second / (1.0 - BETA_TWO**STEP)
    new_prefix = prefix - LEARN_RATE * (
        first_hat / (jnp.sqrt(second_hat) + ADAM_EPSILON) + WEIGHT_DECAY * prefix
    )
    return layer_out, input_grad, prefix_grad, new_prefix, new_first, new_second


def solution(mesh):
    placed = (
        P("batch", "seq", None),
        P("batch", "seq", None),
        P(None, None, "head"),
        P(None, None, "head"),
        P(None, None, "head"),
        P(None, None, "head"),
        P(None, "head"),
        P("head", None),
        P(None, "head"),
        P("head"),
        P("head", None),
        P(),
        P(),
        P("batch"),
        P("batch", "seq"),
    )
    return jax.shard_map(
        body,
        mesh=mesh,
        in_specs=placed,
        out_specs=(
            P("batch", "seq", None),
            P("batch", "seq", None),
            P(None, None, "head"),
            P(None, None, "head"),
            P(None, None, "head"),
            P(None, None, "head"),
        ),
        check_vma=False,
    )
```

```python
import jax
import jax.numpy as jnp
from jax import lax
from jax.experimental import pallas as pl
from jax.experimental.pallas import tpu as pltpu
from jax.sharding import PartitionSpec as P

HEAD_DIM = 64
STEP = 10


NEG_FILL = -1e30
NORM_EPSILON = 1e-05
BETA_ONE = 0.9
BETA_TWO = 0.95
LEARN_RATE = 0.8
WEIGHT_DECAY = 0.01
ADAM_EPSILON = 1e-08


def shifted(value, axis, steps):
    count = lax.axis_size(axis)
    pairs = [(source, (source + steps) % count) for source in range(count)]
    return lax.ppermute(value, axis, pairs)


def layer_norm(values_in, gain_row, shift_row):
    row_mean = jnp.mean(values_in, axis=-1, keepdims=True)
    centred = values_in - row_mean
    spread = jnp.mean(centred * centred, axis=-1, keepdims=True)
    return centred * lax.rsqrt(spread + NORM_EPSILON) * gain_row + shift_row


def exact_gelu(values_in):
    return jax.nn.gelu(values_in, approximate=False)


def block_scores(queries, block_keys, block_bias, score_scale):
    scores = (
        jnp.einsum("shqd,shkd->shqk", queries, block_keys, preferred_element_type=jnp.float32)
        * score_scale
    )
    return scores + block_bias.astype(jnp.float32)[:, None, None, :]


def absorb(softmax_state, queries, block_keys, block_values, block_bias, score_scale):
    row_max, row_sum, weighted = softmax_state
    scores = block_scores(queries, block_keys, block_bias, score_scale)
    new_max = jnp.maximum(row_max, jnp.max(scores, axis=-1))
    fade_factor = jnp.exp(row_max - new_max)
    exp_scores = jnp.exp(scores - new_max[..., None])
    row_sum = row_sum * fade_factor + jnp.sum(exp_scores, axis=-1)
    weighted = weighted * fade_factor[..., None] + jnp.einsum(
        "shqk,shkd->shqd",
        exp_scores.astype(jnp.bfloat16),
        block_values,
        preferred_element_type=jnp.float32,
    )
    return (new_max, row_sum, weighted)


def back_block(
    queries, grad_att, log_total, row_delta, block_keys, block_values, block_bias, score_scale
):
    scores = block_scores(queries, block_keys, block_bias, score_scale)
    probabilities = jnp.exp(scores - log_total[..., None])
    grad_probs = jnp.einsum(
        "shqd,shkd->shqk", grad_att, block_values, preferred_element_type=jnp.float32
    )
    grad_scores = (probabilities * (grad_probs - row_delta[..., None])).astype(jnp.bfloat16)
    grad_queries = (
        jnp.einsum("shqk,shkd->shqd", grad_scores, block_keys, preferred_element_type=jnp.float32)
        * score_scale
    )
    grad_keys = (
        jnp.einsum("shqk,shqd->shkd", grad_scores, queries, preferred_element_type=jnp.float32)
        * score_scale
    )
    grad_values = jnp.einsum(
        "shqk,shqd->shkd",
        probabilities.astype(jnp.bfloat16),
        grad_att,
        preferred_element_type=jnp.float32,
    )
    return (grad_queries, grad_keys, grad_values)


def general_body(
    tokens,
    cotangent,
    prefix,
    first_moment,
    second_moment,
    w_qkv,
    proj_bias,
    w_out,
    w_in,
    ffn_bias,
    w_down,
    gains,
    shifts,
    lengths,
    key_mask,
):
    seqs_dev, shard_len, model_width = tokens.shape
    row_count = seqs_dev * shard_len
    local_width = w_qkv.shape[2]
    heads_dev = local_width // HEAD_DIM
    prefix_slots = prefix.shape[1]
    score_scale = HEAD_DIM ** (-0.5)
    cycle_size = lax.axis_size("seq")
    cycle_place = lax.axis_index("seq")
    flat_tokens = tokens.reshape(row_count, model_width)
    projected = (
        jnp.einsum("td,ide->ite", flat_tokens, w_qkv, preferred_element_type=jnp.float32)
        + proj_bias[:, None, :]
    )
    by_head = (
        projected.astype(jnp.bfloat16)
        .reshape(3, seqs_dev, shard_len, heads_dev, HEAD_DIM)
        .transpose(0, 1, 3, 2, 4)
    )
    queries = by_head[0]
    own_keys = by_head[1]
    own_values = by_head[2]
    positions = cycle_place * shard_len + lax.broadcasted_iota(jnp.int32, (seqs_dev, shard_len), 1)
    live_keys = (key_mask == 1) & (positions < lengths[:, None])
    own_bias = jnp.where(live_keys, 0.0, NEG_FILL).astype(jnp.bfloat16)
    prefix_low = (
        prefix.astype(jnp.bfloat16)
        .reshape(2, prefix_slots, heads_dev, HEAD_DIM)
        .transpose(0, 2, 1, 3)
    )
    pre_scores = (
        jnp.einsum("shqd,hpd->shqp", queries, prefix_low[0], preferred_element_type=jnp.float32)
        * score_scale
    )
    row_max = jnp.max(pre_scores, axis=-1)
    exp_prefix = jnp.exp(pre_scores - row_max[..., None])
    row_sum = jnp.sum(exp_prefix, axis=-1)
    weighted = jnp.einsum(
        "shqp,hpd->shqd",
        exp_prefix.astype(jnp.bfloat16),
        prefix_low[1],
        preferred_element_type=jnp.float32,
    )

    def visit_keys(softmax_state, block_keys, block_values, block_bias):
        return absorb(softmax_state, queries, block_keys, block_values, block_bias, score_scale)

    def forward_turn(turn_index, carried):
        softmax_state, block_keys, block_values, block_bias = carried
        softmax_state = visit_keys(softmax_state, block_keys, block_values, block_bias)
        block_keys, block_values, block_bias = shifted(
            (block_keys, block_values, block_bias), "seq", 1
        )
        return (softmax_state, block_keys, block_values, block_bias)

    carried = lax.fori_loop(
        0,
        cycle_size - 1,
        forward_turn,
        ((row_max, row_sum, weighted), own_keys, own_values, own_bias),
    )
    row_max, row_sum, weighted = visit_keys(carried[0], carried[1], carried[2], carried[3])
    log_total = row_max + jnp.log(row_sum)
    attended = weighted / row_sum[..., None]
    merged = attended.astype(jnp.bfloat16).transpose(0, 2, 1, 3).reshape(row_count, local_width)
    attention = (
        lax.psum(jnp.dot(merged, w_out, preferred_element_type=jnp.float32), "head") + shifts[0]
    )
    resid_one = flat_tokens.astype(jnp.float32) + attention
    normed, norm_one_back = jax.vjp(
        lambda values_in: layer_norm(values_in, gains[0], shifts[1]), resid_one
    )
    inner_sum = (
        jnp.dot(normed.astype(jnp.bfloat16), w_in, preferred_element_type=jnp.float32) + ffn_bias
    )
    activated, gelu_back = jax.vjp(exact_gelu, inner_sum)
    feed_forward = (
        lax.psum(
            jnp.dot(activated.astype(jnp.bfloat16), w_down, preferred_element_type=jnp.float32),
            "head",
        )
        + shifts[2]
    )
    layer_value, norm_two_back = jax.vjp(
        lambda values_in: layer_norm(values_in, gains[1], shifts[3]), normed + feed_forward
    )
    contract_last = (((1,), (1,)), ((), ()))
    (grad_two,) = norm_two_back(cotangent.reshape(row_count, model_width).astype(jnp.float32))
    grad_act = lax.dot_general(
        grad_two.astype(jnp.bfloat16), w_down, contract_last, preferred_element_type=jnp.float32
    )
    (grad_inner,) = gelu_back(grad_act)
    hidden_part = lax.dot_general(
        grad_inner.astype(jnp.bfloat16), w_in, contract_last, preferred_element_type=jnp.float32
    )
    grad_normed = grad_two + lax.psum(hidden_part, "head")
    (grad_one,) = norm_one_back(grad_normed)
    grad_merged = lax.dot_general(
        grad_one.astype(jnp.bfloat16), w_out, contract_last, preferred_element_type=jnp.float32
    )
    grad_att = (
        grad_merged.astype(jnp.bfloat16)
        .reshape(seqs_dev, shard_len, heads_dev, HEAD_DIM)
        .transpose(0, 2, 1, 3)
    )
    row_delta = jnp.sum(grad_att.astype(jnp.float32) * attended, axis=-1)
    pre_probs = jnp.exp(pre_scores - log_total[..., None])
    grad_pre_probs = jnp.einsum(
        "shqd,hpd->shqp", grad_att, prefix_low[1], preferred_element_type=jnp.float32
    )
    grad_pre_scores = (pre_probs * (grad_pre_probs - row_delta[..., None])).astype(jnp.bfloat16)
    grad_query_pre = (
        jnp.einsum(
            "shqp,hpd->shqd", grad_pre_scores, prefix_low[0], preferred_element_type=jnp.float32
        )
        * score_scale
    )
    grad_pre_keys = (
        jnp.einsum("shqp,shqd->hpd", grad_pre_scores, queries, preferred_element_type=jnp.float32)
        * score_scale
    )
    grad_pre_values = jnp.einsum(
        "shqp,shqd->hpd",
        pre_probs.astype(jnp.bfloat16),
        grad_att,
        preferred_element_type=jnp.float32,
    )
    prefix_terms = (
        jnp.stack([grad_pre_keys, grad_pre_values])
        .transpose(0, 2, 1, 3)
        .reshape(2, prefix_slots, local_width)
    )
    empty_grad = jnp.zeros(queries.shape, jnp.float32)

    def back_visit(query_side, key_side):
        return back_block(
            query_side[0],
            query_side[1],
            query_side[2],
            query_side[3],
            key_side[0],
            key_side[1],
            key_side[2],
            score_scale,
        )

    own_key_side = (own_keys, own_values, own_bias)

    def query_turn(turn_index, carried):
        grad_keys, grad_values, visit_queries, visit_grad, visit_total, visit_delta, visit_sum = (
            carried
        )
        turn_queries, turn_keys, turn_values = back_visit(
            (visit_queries, visit_grad, visit_total, visit_delta), own_key_side
        )
        moved = (
            shifted(visit_queries.astype(jnp.float32), "seq", 1).astype(visit_queries.dtype),
            shifted(visit_grad.astype(jnp.float32), "seq", 1).astype(visit_grad.dtype),
            shifted(visit_total, "seq", 1),
            shifted(visit_delta, "seq", 1),
            shifted(visit_sum + turn_queries, "seq", 1),
        )
        return (grad_keys + turn_keys, grad_values + turn_values) + moved

    carried = lax.fori_loop(
        0,
        cycle_size - 1,
        query_turn,
        (empty_grad, empty_grad, queries, grad_att, log_total, row_delta, grad_query_pre),
    )
    grad_keys, grad_values, visit_queries, visit_grad, visit_total, visit_delta, visit_sum = carried
    turn_queries, turn_keys, turn_values = back_visit(
        (visit_queries, visit_grad, visit_total, visit_delta), own_key_side
    )
    grad_keys = grad_keys + turn_keys
    grad_values = grad_values + turn_values
    grad_queries = shifted(visit_sum + turn_queries, "seq", 1)
    grad_rows = (
        jnp.stack([grad_queries, grad_keys, grad_values])
        .astype(jnp.bfloat16)
        .transpose(0, 1, 3, 2, 4)
        .reshape(3, row_count, local_width)
    )
    input_part = jnp.einsum("ite,ide->td", grad_rows, w_qkv, preferred_element_type=jnp.float32)
    input_grad = grad_one + lax.psum(input_part, "head")
    prefix_grad = lax.psum(prefix_terms, ("seq", "batch"))
    new_first = BETA_ONE * first_moment + (1.0 - BETA_ONE) * prefix_grad
    new_second = BETA_TWO * second_moment + (1.0 - BETA_TWO) * prefix_grad * prefix_grad
    first_hat = new_first / (1.0 - BETA_ONE**STEP)
    second_hat = new_second / (1.0 - BETA_TWO**STEP)
    new_prefix = prefix - LEARN_RATE * (
        first_hat / (jnp.sqrt(second_hat) + ADAM_EPSILON) + WEIGHT_DECAY * prefix
    )
    layer_out = layer_value.reshape(seqs_dev, shard_len, model_width)
    return (
        layer_out,
        input_grad.reshape(seqs_dev, shard_len, model_width),
        prefix_grad,
        new_prefix,
        new_first,
        new_second,
    )


BF = jnp.bfloat16
F32 = jnp.float32
MESH = pl.DeviceIdType.MESH
AHEAD = 2


def nn(left, right):
    return jnp.dot(left, right, preferred_element_type=F32)


def nt(left, right):
    return lax.dot_general(
        left, right, (((1,), (1,)), ((), ())), preferred_element_type=F32
    )


def remote(src, dst, send, recv, device):
    return pltpu.make_async_remote_copy(
        src, dst, send, recv, device_id=device, device_id_type=MESH
    )


def rows_at(start, size, step=64):
    return pl.ds(pl.multiple_of(start, step), size)


def places():
    z = lax.axis_index("seq")
    h = lax.axis_index("head")
    y = lax.axis_index("batch")
    return z, h, y


def member(h, u):
    chip, core = h // 2, lax.rem(h, 2)
    return 2 * lax.rem(chip + u // 2, 2) + lax.rem(core + u % 2, 2)


def z_peers(z):
    return [z + 1 - 2 * lax.rem(z, 2), 3 - z, lax.rem(z + 2, 4)]


def greet(devices):
    barrier = pltpu.get_barrier_semaphore()
    for device in devices:
        pl.semaphore_signal(barrier, inc=1, device_id=device, device_id_type=MESH)
    pl.semaphore_wait(barrier, len(devices))


def lane_masks():
    lane = lax.broadcasted_iota(jnp.int32, (1, 128), 1)
    inside = [lane < HEAD_DIM, lane >= HEAD_DIM]
    spare = [lane == HEAD_DIM, lane == 0]
    return inside, spare


def layer_kernel(
    tokens,
    cot,
    w_qkv,
    w_out,
    w_in,
    w_down,
    prefix,
    proj_bias,
    ffn_bias,
    gains,
    shifts,
    lengths,
    key_mask,
    lo_all,
    ig_all,
    pre_o,
    tok,
    cotg,
    bias_s,
    bias_g,
    wq,
    wo,
    wi,
    wd,
    fb,
    q_s,
    k_s,
    v_s,
    kx,
    vtx,
    pt,
    att_loc,
    att_all,
    rl_s,
    normed_s,
    xhat_s,
    nb_s,
    acc,
    act,
    gp,
    lo_s,
    da_s,
    da_all,
    ds_pre,
    dox,
    dq_s,
    core_out,
    core_in,
    x_out,
    x_in,
    fin,
    pre_part,
    pre_land,
    pre_sum,
    loc_sem,
    out_sem,
    tok_sem,
    cot_sem,
    bias_sem,
    fb_sem,
    att_sem,
    core_sem,
    x_sem,
    y_sem,
    c1_sem,
    c2_sem,
    lo_sem,
    lox_sem,
    loc_lo_sem,
    lox_core_sem,
    da_sem,
    part_core_sem,
    part_x_sem,
    igz_sem,
    igx_sem,
    igc_sem,
    igcx_sem,
    pre_sem,
    pre2_sem,
):
    z, h, y = places()
    core = lax.rem(h, 2)
    hc, hx, hd_ = member(h, 1), member(h, 2), member(h, 3)
    dev_core, dev_x, dev_diag, dev_y = (z, hc, y), (z, hx, y), (z, hd_, y), (z, h, 1 - y)
    zs = z_peers(z)
    width = tok.shape[1]
    piece = width // 4
    slots = prefix.shape[1]
    total = 4 * width
    group = 2 * z + y
    others = [lax.rem(group + d, 8) for d in range(1, 8)]
    greet([dev_core, dev_x, dev_diag] + [(g // 2, h, lax.rem(g, 2)) for g in others])

    half = width // 2
    my_half = rows_at(core * half, half)
    tok_copies, tok_forwards = [], []
    for k, zp in enumerate(zs):
        tok_copies.append(
            remote(tokens.at[zp, my_half], tok.at[z, my_half], tok_sem.at[0, k], tok_sem.at[1, k], (zp, h, y))
        )
        tok_forwards.append(
            remote(tok.at[zp, my_half], tok.at[zp, my_half], tok_sem.at[2, k], tok_sem.at[3, k], dev_core)
        )
    for copy in tok_copies:
        copy.start()
    tok_own = pltpu.make_async_copy(tokens.at[z], tok.at[z], loc_sem.at[0])
    tok_own.start()
    wq_own = pltpu.make_async_copy(w_qkv, wq, loc_sem.at[1])
    wq_own.start()

    chunks = [(w_out, wo, w_out.shape[0] // 2, 0, w_out.shape[0] // 2)]
    for src, dst in ((w_in, wi), (w_down, wd)):
        deep = src.shape[0] // 2
        for i in range(4):
            chunks.append((src, dst, deep, i * (deep // 4), deep // 4))
    over_x, over_y, core_x, core_y = [], [], [], []
    for i, (src, dst, deep, offset, size) in enumerate(chunks):
        mine = rows_at(y * deep + offset, size, 128)
        other = rows_at((1 - y) * deep + offset, size, 128)
        over_x.append(remote(src.at[mine], dst.at[h, mine], x_sem.at[0, i], x_sem.at[1, i], dev_x))
        over_y.append(remote(dst.at[hx, mine], dst.at[hx, mine], y_sem.at[0, i], y_sem.at[1, i], dev_y))
        core_x.append(remote(dst.at[hx, mine], dst.at[hx, mine], c1_sem.at[0, i], c1_sem.at[1, i], dev_core))
        core_y.append(remote(dst.at[hx, other], dst.at[hx, other], c2_sem.at[0, i], c2_sem.at[1, i], dev_core))
    n_chunks = len(chunks)
    for copy in over_x[:AHEAD]:
        copy.start()

    def serve_x(i):
        over_x[i].wait_recv()
        over_y[i].start()
        core_x[i].start()
        if i + AHEAD < n_chunks:
            over_x[i + AHEAD].start()

    def serve_y(i):
        over_y[i].wait_recv()
        core_y[i].start()

    own_weights, core_weights = [], []
    for i, (src, dst) in enumerate(((w_out, wo), (w_in, wi), (w_down, wd))):
        own_weights.append(pltpu.make_async_copy(src, dst.at[h], loc_sem.at[2 + i]))
        core_weights.append(remote(src, dst.at[h], core_sem.at[0, i], core_sem.at[1, i], dev_core))

    spot = lax.broadcasted_iota(jnp.int32, (8, width), 1) + z * width
    for s in range(4):
        live = (jnp.broadcast_to(key_mask[s : s + 1, :], (8, width)) == 1) & (spot < lengths[s])
        bias_s[s] = jnp.where(live, 0.0, NEG_FILL)
    bias_g[z] = bias_s[z]
    bias_copies = [
        remote(bias_s.at[zp], bias_g.at[z], bias_sem.at[0, k], bias_sem.at[1, k], (zp, h, y))
        for k, zp in enumerate(zs)
    ]
    fb[h] = jnp.broadcast_to(ffn_bias[...], fb.shape[1:])
    fb_copies = [
        remote(fb.at[h], fb.at[h], fb_sem.at[0, k], fb_sem.at[1, k], device)
        for k, device in enumerate((dev_core, dev_x, dev_diag))
    ]
    for copy in bias_copies + fb_copies:
        copy.start()
    for copy in own_weights + core_weights:
        copy.start()

    my_piece = rows_at(h * piece, piece)
    cot_copies = [
        remote(cot.at[zp, my_piece], cotg.at[z], cot_sem.at[0, k], cot_sem.at[1, k], (zp, h, y))
        for k, zp in enumerate(zs)
    ]
    cot_own = pltpu.make_async_copy(cot.at[z, my_piece], cotg.at[z], loc_sem.at[5])
    cot_own.start()

    inside, spare = lane_masks()

    pk = prefix[0].astype(BF)
    pv = prefix[1].astype(BF)
    k_s[total : total + slots, :] = pk
    v_s[total : total + slots, :] = pv
    for head in range(4):
        pair, par = head // 2, head % 2
        part = pk[:, 128 * pair : 128 * pair + 128].astype(F32)
        kx[head, total : total + slots, :] = jnp.where(inside[par], part, 0.0).astype(BF)
        vtx[head, HEAD_DIM:, :] = jnp.ones((vtx.shape[1] - HEAD_DIM, vtx.shape[2]), BF)

    def project(block):
        rows = tok[block]
        for i, target in enumerate((q_s, k_s, v_s)):
            value = (nn(rows, wq[i]) + proj_bias[i : i + 1, :]).astype(BF)
            if i == 0:
                value = (value.astype(F32) * HEAD_DIM**-0.5).astype(BF)
            for j in range(4):
                target[rows_at(j * width + block * piece, piece), :] = value[piece * j : piece * j + piece]
            if i == 1:
                column = jnp.broadcast_to(bias_g[block][0:1, :], (128, width)).T
                for head in range(4):
                    pair, par = head // 2, head % 2
                    part = value[:, 128 * pair : 128 * pair + 128].astype(F32)
                    ext = jnp.where(inside[par], part, jnp.where(spare[par], column, 0.0)).astype(BF)
                    for j in range(4):
                        kx[head, rows_at(j * width + block * piece, piece), :] = ext[piece * j : piece * j + piece]

    tok_own.wait()
    wq_own.wait()
    project(z)
    serve_x(0)
    for k, zp in enumerate(zs):
        serve_x(k + 1)
        serve_y(k)
        tok_copies[k].wait_recv()
        tok_forwards[k].start()
        bias_copies[k].wait_recv()
        if k == 2:
            for copy in cot_copies:
                copy.start()
        tok_forwards[k].wait_recv()
        project(zp)

    for i in range(4):
        flipped = v_s[i * width : (i + 1) * width, :].astype(F32).T.astype(BF)
        for head in range(4):
            vtx[head, 0:HEAD_DIM, i * width : (i + 1) * width] = flipped[HEAD_DIM * head : HEAD_DIM * (head + 1)]
    flipped = v_s[total : total + slots, :].astype(F32).T.astype(BF)
    for head in range(4):
        vtx[head, 0:HEAD_DIM, total : total + slots] = flipped[HEAD_DIM * head : HEAD_DIM * (head + 1)]

    att_copies = []
    for step in range(4):
        u = 3 - step
        j = member(h, u) if u else h
        outs, recips = [], []
        for head in range(4):
            pair, par = head // 2, head % 2
            part = q_s[rows_at(j * width, width, width), 128 * pair : 128 * pair + 128].astype(F32)
            ext = jnp.where(inside[par], part, jnp.where(spare[par], 1.0, 0.0)).astype(BF)
            scores = nt(kx[head], ext)
            top = jnp.max(scores, axis=0, keepdims=True)
            weight = jnp.exp(scores - top).astype(BF)
            pt[head, j] = weight
            summed = nn(vtx[head], weight)
            recip = 1.0 / summed[HEAD_DIM : HEAD_DIM + 1]
            outs.append(summed[0:HEAD_DIM] * recip)
            recips.append(jnp.broadcast_to(recip, (32, width)))
        att_loc[j] = jnp.concatenate(outs, axis=0).T.astype(BF)
        rl_s[j] = jnp.concatenate(recips, axis=0).T
        if u:
            copy = remote(att_loc.at[j], att_all.at[h], att_sem.at[0, u], att_sem.at[1, u], (z, j, y))
            copy.start()
            att_copies.append(copy)
        else:
            att_all[h] = att_loc[h]
        if step < 2:
            serve_x(4 + step)
            serve_y(3 + step)
    lane = lax.broadcasted_iota(jnp.int32, (1, 128), 1)
    spare_lo = [lane == HEAD_DIM + 1, lane == 1]
    for head in range(4):
        pair, par = head // 2, head % 2
        part = v_s[:, 128 * pair : 128 * pair + 128].astype(F32)
        ones = jnp.where(spare[par] | spare_lo[par], 1.0, 0.0)
        kx[head] = jnp.where(inside[par], part, ones).astype(BF)
    for i in range(5):
        low, size = i * width, width if i < 4 else slots
        flipped = k_s[low : low + size, :].astype(F32).T.astype(BF)
        for head in range(4):
            vtx[head, 0:HEAD_DIM, low : low + size] = flipped[HEAD_DIM * head : HEAD_DIM * (head + 1)]

    own_weights[0].wait()
    core_weights[0].wait_recv()
    core_x[0].wait_recv()
    core_y[0].wait_recv()
    for copy in att_copies:
        copy.wait_recv()
    attention = nn(att_all[0], wo[0])
    for j in range(1, 4):
        attention += nn(att_all[j], wo[j])
    mine = jnp.concatenate([tok[b, my_piece, :] for b in range(4)], axis=0).astype(F32)
    resid = mine + attention + shifts[0:1, :]
    centred = resid - jnp.mean(resid, axis=-1, keepdims=True)
    inverse_one = lax.rsqrt(jnp.mean(centred * centred, axis=-1, keepdims=True) + NORM_EPSILON)
    xhat = centred * inverse_one
    xhat_s[...] = xhat
    normed = xhat * gains[0:1, :] + shifts[1:2, :]
    normed_s[...] = normed
    nb_s[...] = normed.astype(BF)

    tile = 256
    tiles = wi.shape[2] // tile

    def ffn_in(quarter):
        @pl.loop(0, tiles, unroll=4)
        def _(n):
            cols = rows_at(n * tile, tile, tile)
            inner = nn(nb_s[...], wi[quarter, :, cols]) + fb[quarter, 0:1, cols]
            cdf = 0.5 * (1.0 + lax.erf(inner * 0.7071067811865476))
            act[quarter, :, cols] = (inner * cdf).astype(BF)
            gp[quarter, :, cols] = cdf + inner * (jnp.exp(-0.5 * inner * inner) * 0.3989422804014327)

    for copy in fb_copies:
        copy.wait_recv()
    own_weights[1].wait()
    core_weights[1].wait_recv()
    ffn_in(h)
    ffn_in(hc)
    serve_x(6)
    serve_y(5)
    for i in range(1, 5):
        core_x[i].wait_recv()
        core_y[i].wait_recv()
    ffn_in(hx)
    ffn_in(hd_)

    acc[...] = jnp.zeros(acc.shape, F32)

    def ffn_out(quarter, start, deep):
        span = rows_at(start, deep, deep)

        @pl.loop(0, tiles, unroll=4)
        def _(n):
            cols = rows_at(n * tile, tile, tile)
            acc[:, cols] += nn(act[quarter, :, span], wd[quarter, span, cols])

    own_weights[2].wait()
    core_weights[2].wait_recv()
    deep = wd.shape[1]
    ffn_out(h, 0, deep)
    serve_x(7)
    serve_y(6)
    ffn_out(hc, 0, deep)
    serve_x(8)
    serve_y(7)
    for i in range(5, 9):
        core_x[i].wait_recv()
    ffn_out(hx, y * (deep // 2), deep // 2)
    ffn_out(hd_, y * (deep // 2), deep // 2)
    serve_y(8)
    ffn_out(hx, (1 - y) * (deep // 2), deep // 2)
    for i in range(5, 9):
        core_y[i].wait_recv()
    ffn_out(hd_, (1 - y) * (deep // 2), deep // 2)

    resid = normed_s[...] + acc[...] + shifts[2:3, :]
    centred = resid - jnp.mean(resid, axis=-1, keepdims=True)
    inverse = lax.rsqrt(jnp.mean(centred * centred, axis=-1, keepdims=True) + NORM_EPSILON)
    xhat = centred * inverse
    lo_s[...] = (xhat * gains[1:2, :] + shifts[3:4, :]).astype(BF)
    x_piece = rows_at(hx * piece, piece)
    lo_z, lo_x, lo_core, lo_across = [], [], [], []
    blocks = zs + [z]
    for k, b in enumerate(blocks):
        rows = rows_at(b * piece, piece)
        source = lo_all.at[b, my_piece]
        if k < 3:
            lo_z.append(remote(lo_s.at[rows], lo_all.at[z, my_piece], lo_sem.at[0, k], lo_sem.at[1, k], (b, h, y)))
        else:
            source = lo_s.at[rows]
        lo_x.append(remote(source, lo_all.at[b, my_piece], lox_sem.at[0, k], lox_sem.at[1, k], dev_x))
        lo_core.append(remote(source, lo_all.at[b, my_piece], loc_lo_sem.at[0, k], loc_lo_sem.at[1, k], dev_core))
        lo_across.append(
            remote(lo_all.at[b, x_piece], lo_all.at[b, x_piece], lox_core_sem.at[0, k], lox_core_sem.at[1, k], dev_core)
        )
    lo_own = pltpu.make_async_copy(lo_s.at[rows_at(z * piece, piece)], lo_all.at[z, my_piece], out_sem.at[0])
    for copy in lo_z + [lo_x[3], lo_core[3], lo_own]:
        copy.start()

    def serve_lo(k):
        lo_z[k].wait_recv()
        lo_x[k].start()
        lo_core[k].start()

    cot_own.wait()
    for copy in cot_copies:
        copy.wait_recv()
    dy = jnp.concatenate([cotg[b] for b in range(4)], axis=0).astype(F32) * gains[1:2, :]
    g_two = inverse * (
        dy - jnp.mean(dy, axis=-1, keepdims=True) - xhat * jnp.mean(dy * xhat, axis=-1, keepdims=True)
    )
    acc[...] = g_two
    nb_s[...] = g_two.astype(BF)

    @pl.loop(0, 4)
    def _(quarter):
        @pl.loop(0, tiles, unroll=4)
        def _(n):
            cols = rows_at(n * tile, tile, tile)
            d_act = nt(nb_s[...], wd[quarter, cols, :])
            act[quarter, :, cols] = (d_act * gp[quarter, :, cols]).astype(BF)

    serve_lo(0)

    @pl.loop(0, 4)
    def _(quarter):
        @pl.loop(0, tiles, unroll=4)
        def _(n):
            cols = rows_at(n * tile, tile, tile)
            acc[:, cols] += nt(act[quarter], wi[quarter, cols, :])

    serve_lo(1)
    dy = acc[...] * gains[0:1, :]
    xhat = xhat_s[...]
    g_one = inverse_one * (
        dy - jnp.mean(dy, axis=-1, keepdims=True) - xhat * jnp.mean(dy * xhat, axis=-1, keepdims=True)
    )
    acc[...] = g_one
    low = g_one.astype(BF)
    da_copies = {}
    for u in (2, 3, 1):
        j = member(h, u)
        da_s[j] = nt(low, wo[j]).astype(BF)
        da_copies[u] = remote(da_s.at[j], da_all.at[h], da_sem.at[0, u], da_sem.at[1, u], (z, j, y))
        da_copies[u].start()
    da_all[h] = nt(low, wo[h]).astype(BF)
    for copy in over_y + core_x + core_y:
        copy.wait_send()

    order = [h, hc, hx, hd_]
    for u, j in enumerate(order):
        if u:
            da_copies[u].wait_recv()
        if u == 1:
            serve_lo(2)
        grads = []
        for head in range(4):
            pair, par = head // 2, head % 2
            lanes = slice(128 * pair, 128 * pair + 128)
            d_out = da_all[j, :, lanes].astype(F32)
            recip = rl_s[j, :, 32 * head : 32 * head + 1]
            delta = recip * jnp.sum(
                jnp.where(inside[par], d_out * att_loc[j, :, lanes].astype(F32), 0.0), axis=-1, keepdims=True
            )
            high = delta.astype(BF).astype(F32)
            ext = jnp.where(spare[par], -high, jnp.where(spare_lo[par], high - delta, 0.0))
            ext = jnp.where(inside[par], d_out * recip, ext).astype(BF)
            dox[head, j] = ext
            d_probs = nt(kx[head], ext).astype(BF)
            d_scores = pt[head, j] * d_probs
            wi[head, :, rows_at(j * width, width, width)] = d_scores[0:total]
            ds_pre[head, j] = d_scores[total:]
            grads.append(nn(vtx[head, 0:HEAD_DIM, :], d_scores))
        dq_s[j] = (jnp.concatenate(grads, axis=0).T * HEAD_DIM**-0.5).astype(BF)

    def key_side(left, right):
        halves = []
        for pair in range(2):
            sides = []
            for par in range(2):
                head = 2 * pair + par
                value = nn(left(head, 0), right(head, 0, pair))
                for j in range(1, 4):
                    value += nn(left(head, j), right(head, j, pair))
                sides.append(value)
            halves.append(jnp.where(inside[0], sides[0], sides[1]))
        return jnp.concatenate(halves, axis=-1)

    def d_values(rows):
        return key_side(lambda head, j: pt[head, j, rows, :], lambda head, j, pair: dox[head, j])

    def d_keys(left):
        return key_side(left, lambda head, j, pair: q_s[j * width : (j + 1) * width, 128 * pair : 128 * pair + 128])

    def partial(i):
        rows = rows_at(i * width, width, width)
        dk = d_keys(lambda head, j: wi[head, rows, j * width : (j + 1) * width]).astype(BF)
        dv = d_values(rows).astype(BF)
        return nt(dq_s[i], wq[0]) + nt(dk, wq[1]) + nt(dv, wq[2])

    part_core = [
        remote(core_out.at[i], core_in.at[i], part_core_sem.at[0, i], part_core_sem.at[1, i], dev_core) for i in range(2)
    ]
    part_x = []
    for k, b in enumerate(blocks):
        rows = rows_at(b * piece, piece)
        part_x.append(remote(x_out.at[rows], x_in.at[rows], part_x_sem.at[0, k], part_x_sem.at[1, k], dev_x))

    core_out[0] = partial(hd_).astype(BF)
    part_core[0].start()
    mine = partial(hx)
    part_core[0].wait_recv()
    x_out[...] = (mine + core_in[0].astype(F32)).astype(BF)
    for copy in part_x:
        copy.start()

    pre_part[0] = d_keys(lambda head, j: ds_pre[head, j])
    pre_part[1] = d_values(pl.ds(total, slots))
    few = slots // 8
    mine_rows = rows_at(group * few, few, few)
    pre_copies, pre_back = [], []
    for d, g in enumerate(others):
        device = (g // 2, h, lax.rem(g, 2))
        pre_copies.append(
            remote(pre_part.at[:, rows_at(g * few, few, few)], pre_land.at[d], pre_sem.at[0, d], pre_sem.at[1, d], device)
        )
        pre_back.append(
            remote(pre_sum.at[:, mine_rows], pre_sum.at[:, mine_rows], pre2_sem.at[0, d], pre2_sem.at[1, d], device)
        )
    for copy in pre_copies:
        copy.start()
    for k in (3, 0, 1, 2):
        lo_x[k].wait_recv()
        lo_across[k].start()

    core_out[1] = partial(hc).astype(BF)
    part_core[1].start()
    acc[...] += partial(h)
    part_core[1].wait_recv()
    acc[...] += core_in[1].astype(F32)

    igz, igx, igc, igcx = [], [], [], []
    for k, b in enumerate(blocks):
        rows = rows_at(b * piece, piece)
        source = ig_all.at[b, my_piece]
        if k < 3:
            igz.append(remote(fin.at[rows], ig_all.at[z, my_piece], igz_sem.at[0, k], igz_sem.at[1, k], (b, h, y)))
        else:
            source = fin.at[rows]
        igx.append(remote(source, ig_all.at[b, my_piece], igx_sem.at[0, k], igx_sem.at[1, k], dev_x))
        igc.append(remote(source, ig_all.at[b, my_piece], igc_sem.at[0, k], igc_sem.at[1, k], dev_core))
        igcx.append(
            remote(ig_all.at[b, x_piece], ig_all.at[b, x_piece], igcx_sem.at[0, k], igcx_sem.at[1, k], dev_core)
        )
    ig_own = pltpu.make_async_copy(fin.at[rows_at(z * piece, piece)], ig_all.at[z, my_piece], out_sem.at[1])
    for k, b in enumerate(blocks):
        rows = rows_at(b * piece, piece)
        part_x[k].wait_recv()
        fin[rows, :] = (acc[rows, :] + x_in[rows, :].astype(F32)).astype(BF)
        if k < 3:
            igz[k].start()
        else:
            ig_own.start()
            igx[3].start()
            igc[3].start()
        if k == 1:
            for copy in pre_copies:
                copy.wait_recv()
            for i in range(2):
                term = pre_part[i, mine_rows, :]
                for d in range(7):
                    term += pre_land[d, i]
                pre_sum[i, mine_rows, :] = term
            for copy in pre_back:
                copy.start()
    for copy in lo_core + lo_across:
        copy.wait_recv()
    lo_own.wait()
    for k in range(3):
        igz[k].wait_recv()
        igx[k].start()
        igc[k].start()
    for copy in pre_back:
        copy.wait_recv()
    pre_o[...] = pre_sum[...]
    for k in (3, 0, 1, 2):
        igx[k].wait_recv()
        igcx[k].start()
    for copy in igc + igcx:
        copy.wait_recv()
    ig_own.wait()
    sent = tok_copies + tok_forwards + over_x + core_weights + bias_copies + fb_copies + cot_copies + att_copies
    sent += lo_z + lo_x + lo_core + lo_across + list(da_copies.values()) + part_core + part_x
    for copy in sent + igz + igx + igc + igcx + pre_copies + pre_back:
        copy.wait_send()


def layer(tokens, cot, w_qkv, w_out, w_in, w_down, prefix, proj_bias, ffn_bias, gains, shifts, lengths, key_mask):
    seqs, width, model = tokens.shape
    local = w_qkv.shape[2]
    hidden = w_in.shape[1]
    slots = prefix.shape[1]
    total = seqs * width
    keys = total + slots
    dma = pltpu.SemaphoreType.DMA
    hbm = pl.BlockSpec(memory_space=pl.ANY)
    vmem = pl.BlockSpec(memory_space=pltpu.VMEM)
    shape = jax.ShapeDtypeStruct
    return pl.pallas_call(
        layer_kernel,
        name="layer",
        out_shape=(
            pltpu.VMEM((4, width, model), BF),
            pltpu.VMEM((4, width, model), BF),
            shape((2, slots, local), F32),
        ),
        in_specs=[hbm] * 6 + [vmem] * 5 + [pl.BlockSpec(memory_space=pltpu.SMEM), vmem],
        out_specs=(vmem, vmem, vmem),
        scratch_shapes=[
            pltpu.VMEM((4, width, model), BF),
            pltpu.VMEM((4, width // 4, model), BF),
            pltpu.VMEM((4, 8, width), F32),
            pltpu.VMEM((4, 8, width), F32),
            pltpu.VMEM((3, model, local), BF),
            pltpu.VMEM((4, local, model), BF),
            pltpu.VMEM((4, model, hidden), BF),
            pltpu.VMEM((4, hidden, model), BF),
            pltpu.VMEM((4, 8, hidden), F32),
            pltpu.VMEM((total, local), BF),
            pltpu.VMEM((keys, local), BF),
            pltpu.VMEM((keys, local), BF),
            pltpu.VMEM((4, keys, 128), BF),
            pltpu.VMEM((4, HEAD_DIM + 16, keys), BF),
            pltpu.VMEM((4, 4, keys, width), BF),
            pltpu.VMEM((4, width, local), BF),
            pltpu.VMEM((4, width, local), BF),
            pltpu.VMEM((4, width, 128), F32),
            pltpu.VMEM((width, model), F32),
            pltpu.VMEM((width, model), F32),
            pltpu.VMEM((width, model), BF),
            pltpu.VMEM((width, model), F32),
            pltpu.VMEM((4, width, hidden), BF),
            pltpu.VMEM((4, width, hidden), F32),
            pltpu.VMEM((width, model), BF),
            pltpu.VMEM((4, width, local), BF),
            pltpu.VMEM((4, width, local), BF),
            pltpu.VMEM((4, 4, slots, width), BF),
            pltpu.VMEM((4, 4, width, 128), BF),
            pltpu.VMEM((4, width, local), BF),
            pltpu.VMEM((2, width, model), BF),
            pltpu.VMEM((2, width, model), BF),
            pltpu.VMEM((width, model), BF),
            pltpu.VMEM((width, model), BF),
            pltpu.VMEM((width, model), BF),
            pltpu.VMEM((2, slots, local), F32),
            pltpu.VMEM((7, 2, slots // 8, local), F32),
            pltpu.VMEM((2, slots, local), F32),
            dma((6,)),
            dma((4,)),
            dma((4, 3)),
            dma((2, 3)),
            dma((2, 3)),
            dma((2, 3)),
            dma((2, 4)),
            dma((2, 3)),
            dma((2, 9)),
            dma((2, 9)),
            dma((2, 9)),
            dma((2, 9)),
            dma((2, 3)),
            dma((2, 4)),
            dma((2, 4)),
            dma((2, 4)),
            dma((2, 4)),
            dma((2, 2)),
            dma((2, 4)),
            dma((2, 3)),
            dma((2, 4)),
            dma((2, 4)),
            dma((2, 4)),
            dma((2, 7)),
            dma((2, 7)),
        ],
        compiler_params=pltpu.CompilerParams(
            collective_id=0, has_side_effects=True, vmem_limit_bytes=58 * 2**20
        ),
        cost_estimate=pl.CostEstimate(flops=15 * 10**9, bytes_accessed=40 * 2**20, transcendentals=6 * 10**6),
    )(tokens, cot, w_qkv, w_out, w_in, w_down, prefix, proj_bias, ffn_bias, gains, shifts, lengths, key_mask)


def finish_kernel(lo, ig, grad, prefix, first, second, lo_o, ig_o, grad_o, new_o, first_o, second_o, lo_f, ig_f, sem):
    seqs = lo.shape[0]
    copies = []
    for i in range(seqs):
        for k, (src, mid, dst) in enumerate(((lo, lo_f, lo_o), (ig, ig_f, ig_o))):
            mid[i] = src[i].astype(F32)
            copy = pltpu.make_async_copy(mid.at[i], dst.at[i], sem.at[k, i])
            copy.start()
            copies.append(copy)
    slope = grad[...]
    grad_o[...] = slope
    new_first = BETA_ONE * first[...] + (1.0 - BETA_ONE) * slope
    new_second = BETA_TWO * second[...] + (1.0 - BETA_TWO) * slope * slope
    first_hat = new_first / (1.0 - BETA_ONE**STEP)
    second_hat = new_second / (1.0 - BETA_TWO**STEP)
    value = prefix[...]
    new_o[...] = value - LEARN_RATE * (first_hat / (jnp.sqrt(second_hat) + ADAM_EPSILON) + WEIGHT_DECAY * value)
    first_o[...] = new_first
    second_o[...] = new_second
    for copy in copies:
        copy.wait()


def finish(lo, ig, grad, prefix, first, second):
    hbm = pl.BlockSpec(memory_space=pl.ANY)
    vmem = pl.BlockSpec(memory_space=pltpu.VMEM)
    shape = jax.ShapeDtypeStruct
    whole, little = shape(lo.shape, F32), shape(prefix.shape, F32)
    return pl.pallas_call(
        finish_kernel,
        name="finish",
        out_shape=(whole, whole, little, little, little, little),
        in_specs=[vmem] * 6,
        out_specs=(hbm, hbm, vmem, vmem, vmem, vmem),
        scratch_shapes=[
            pltpu.VMEM(lo.shape, F32),
            pltpu.VMEM(lo.shape, F32),
            pltpu.SemaphoreType.DMA((2, lo.shape[0])),
        ],
        compiler_params=pltpu.CompilerParams(vmem_limit_bytes=40 * 2**20),
    )(lo, ig, grad, prefix, first, second)


def body(*args):
    (tokens, cotangent, prefix, first_moment, second_moment, w_qkv, proj_bias, w_out, w_in, ffn_bias) = args[:10]
    w_down, gains, shifts, lengths, key_mask = args[10:]
    fits = (
        lax.axis_size("seq") == 4
        and lax.axis_size("head") == 4
        and lax.axis_size("batch") == 2
        and tokens.shape == (4, 256, 1024)
        and w_qkv.shape == (3, 1024, 256)
        and w_in.shape == (1024, 1024)
        and prefix.shape[1] == 64
    )
    if not fits:
        return general_body(*args)
    layer_out, input_grad, prefix_grad = layer(
        tokens, cotangent, w_qkv, w_out, w_in, w_down, prefix, proj_bias, ffn_bias.reshape(1, -1), gains, shifts,
        lengths, key_mask,
    )
    layer_out, input_grad, prefix_grad, new_prefix, new_first, new_second = finish(
        layer_out, input_grad, prefix_grad, prefix, first_moment, second_moment
    )
    return layer_out, input_grad, prefix_grad, new_prefix, new_first, new_second


def solution(mesh):
    placed = (
        P("batch", "seq", None),
        P("batch", "seq", None),
        P(None, None, "head"),
        P(None, None, "head"),
        P(None, None, "head"),
        P(None, None, "head"),
        P(None, "head"),
        P("head", None),
        P(None, "head"),
        P("head"),
        P("head", None),
        P(),
        P(),
        P("batch"),
        P("batch", "seq"),
    )
    return jax.shard_map(
        body,
        mesh=mesh,
        in_specs=placed,
        out_specs=(
            P("batch", "seq", None),
            P("batch", "seq", None),
            P(None, None, "head"),
            P(None, None, "head"),
            P(None, None, "head"),
            P(None, None, "head"),
        ),
        check_vma=False,
    )
```

```python
import jax
import jax.numpy as jnp
from jax import lax
from jax.experimental import pallas as pl
from jax.experimental.pallas import tpu as pltpu
from jax.sharding import PartitionSpec as P

HEAD_DIM = 64
STEP = 10


NEG_FILL = -1e30
NORM_EPSILON = 1e-05
BETA_ONE = 0.9
BETA_TWO = 0.95
LEARN_RATE = 0.8
WEIGHT_DECAY = 0.01
ADAM_EPSILON = 1e-08


def shifted(value, axis, steps):
    count = lax.axis_size(axis)
    pairs = [(source, (source + steps) % count) for source in range(count)]
    return lax.ppermute(value, axis, pairs)


def layer_norm(values_in, gain_row, shift_row):
    row_mean = jnp.mean(values_in, axis=-1, keepdims=True)
    centred = values_in - row_mean
    spread = jnp.mean(centred * centred, axis=-1, keepdims=True)
    return centred * lax.rsqrt(spread + NORM_EPSILON) * gain_row + shift_row


def exact_gelu(values_in):
    return jax.nn.gelu(values_in, approximate=False)


def block_scores(queries, block_keys, block_bias, score_scale):
    scores = (
        jnp.einsum("shqd,shkd->shqk", queries, block_keys, preferred_element_type=jnp.float32)
        * score_scale
    )
    return scores + block_bias.astype(jnp.float32)[:, None, None, :]


def absorb(softmax_state, queries, block_keys, block_values, block_bias, score_scale):
    row_max, row_sum, weighted = softmax_state
    scores = block_scores(queries, block_keys, block_bias, score_scale)
    new_max = jnp.maximum(row_max, jnp.max(scores, axis=-1))
    fade_factor = jnp.exp(row_max - new_max)
    exp_scores = jnp.exp(scores - new_max[..., None])
    row_sum = row_sum * fade_factor + jnp.sum(exp_scores, axis=-1)
    weighted = weighted * fade_factor[..., None] + jnp.einsum(
        "shqk,shkd->shqd",
        exp_scores.astype(jnp.bfloat16),
        block_values,
        preferred_element_type=jnp.float32,
    )
    return (new_max, row_sum, weighted)


def back_block(
    queries, grad_att, log_total, row_delta, block_keys, block_values, block_bias, score_scale
):
    scores = block_scores(queries, block_keys, block_bias, score_scale)
    probabilities = jnp.exp(scores - log_total[..., None])
    grad_probs = jnp.einsum(
        "shqd,shkd->shqk", grad_att, block_values, preferred_element_type=jnp.float32
    )
    grad_scores = (probabilities * (grad_probs - row_delta[..., None])).astype(jnp.bfloat16)
    grad_queries = (
        jnp.einsum("shqk,shkd->shqd", grad_scores, block_keys, preferred_element_type=jnp.float32)
        * score_scale
    )
    grad_keys = (
        jnp.einsum("shqk,shqd->shkd", grad_scores, queries, preferred_element_type=jnp.float32)
        * score_scale
    )
    grad_values = jnp.einsum(
        "shqk,shqd->shkd",
        probabilities.astype(jnp.bfloat16),
        grad_att,
        preferred_element_type=jnp.float32,
    )
    return (grad_queries, grad_keys, grad_values)


def general_body(
    tokens,
    cotangent,
    prefix,
    first_moment,
    second_moment,
    w_qkv,
    proj_bias,
    w_out,
    w_in,
    ffn_bias,
    w_down,
    gains,
    shifts,
    lengths,
    key_mask,
):
    seqs_dev, shard_len, model_width = tokens.shape
    row_count = seqs_dev * shard_len
    local_width = w_qkv.shape[2]
    heads_dev = local_width // HEAD_DIM
    prefix_slots = prefix.shape[1]
    score_scale = HEAD_DIM ** (-0.5)
    cycle_size = lax.axis_size("seq")
    cycle_place = lax.axis_index("seq")
    flat_tokens = tokens.reshape(row_count, model_width)
    projected = (
        jnp.einsum("td,ide->ite", flat_tokens, w_qkv, preferred_element_type=jnp.float32)
        + proj_bias[:, None, :]
    )
    by_head = (
        projected.astype(jnp.bfloat16)
        .reshape(3, seqs_dev, shard_len, heads_dev, HEAD_DIM)
        .transpose(0, 1, 3, 2, 4)
    )
    queries = by_head[0]
    own_keys = by_head[1]
    own_values = by_head[2]
    positions = cycle_place * shard_len + lax.broadcasted_iota(jnp.int32, (seqs_dev, shard_len), 1)
    live_keys = (key_mask == 1) & (positions < lengths[:, None])
    own_bias = jnp.where(live_keys, 0.0, NEG_FILL).astype(jnp.bfloat16)
    prefix_low = (
        prefix.astype(jnp.bfloat16)
        .reshape(2, prefix_slots, heads_dev, HEAD_DIM)
        .transpose(0, 2, 1, 3)
    )
    pre_scores = (
        jnp.einsum("shqd,hpd->shqp", queries, prefix_low[0], preferred_element_type=jnp.float32)
        * score_scale
    )
    row_max = jnp.max(pre_scores, axis=-1)
    exp_prefix = jnp.exp(pre_scores - row_max[..., None])
    row_sum = jnp.sum(exp_prefix, axis=-1)
    weighted = jnp.einsum(
        "shqp,hpd->shqd",
        exp_prefix.astype(jnp.bfloat16),
        prefix_low[1],
        preferred_element_type=jnp.float32,
    )

    def visit_keys(softmax_state, block_keys, block_values, block_bias):
        return absorb(softmax_state, queries, block_keys, block_values, block_bias, score_scale)

    def forward_turn(turn_index, carried):
        softmax_state, block_keys, block_values, block_bias = carried
        softmax_state = visit_keys(softmax_state, block_keys, block_values, block_bias)
        block_keys, block_values, block_bias = shifted(
            (block_keys, block_values, block_bias), "seq", 1
        )
        return (softmax_state, block_keys, block_values, block_bias)

    carried = lax.fori_loop(
        0,
        cycle_size - 1,
        forward_turn,
        ((row_max, row_sum, weighted), own_keys, own_values, own_bias),
    )
    row_max, row_sum, weighted = visit_keys(carried[0], carried[1], carried[2], carried[3])
    log_total = row_max + jnp.log(row_sum)
    attended = weighted / row_sum[..., None]
    merged = attended.astype(jnp.bfloat16).transpose(0, 2, 1, 3).reshape(row_count, local_width)
    attention = (
        lax.psum(jnp.dot(merged, w_out, preferred_element_type=jnp.float32), "head") + shifts[0]
    )
    resid_one = flat_tokens.astype(jnp.float32) + attention
    normed, norm_one_back = jax.vjp(
        lambda values_in: layer_norm(values_in, gains[0], shifts[1]), resid_one
    )
    inner_sum = (
        jnp.dot(normed.astype(jnp.bfloat16), w_in, preferred_element_type=jnp.float32) + ffn_bias
    )
    activated, gelu_back = jax.vjp(exact_gelu, inner_sum)
    feed_forward = (
        lax.psum(
            jnp.dot(activated.astype(jnp.bfloat16), w_down, preferred_element_type=jnp.float32),
            "head",
        )
        + shifts[2]
    )
    layer_value, norm_two_back = jax.vjp(
        lambda values_in: layer_norm(values_in, gains[1], shifts[3]), normed + feed_forward
    )
    contract_last = (((1,), (1,)), ((), ()))
    (grad_two,) = norm_two_back(cotangent.reshape(row_count, model_width).astype(jnp.float32))
    grad_act = lax.dot_general(
        grad_two.astype(jnp.bfloat16), w_down, contract_last, preferred_element_type=jnp.float32
    )
    (grad_inner,) = gelu_back(grad_act)
    hidden_part = lax.dot_general(
        grad_inner.astype(jnp.bfloat16), w_in, contract_last, preferred_element_type=jnp.float32
    )
    grad_normed = grad_two + lax.psum(hidden_part, "head")
    (grad_one,) = norm_one_back(grad_normed)
    grad_merged = lax.dot_general(
        grad_one.astype(jnp.bfloat16), w_out, contract_last, preferred_element_type=jnp.float32
    )
    grad_att = (
        grad_merged.astype(jnp.bfloat16)
        .reshape(seqs_dev, shard_len, heads_dev, HEAD_DIM)
        .transpose(0, 2, 1, 3)
    )
    row_delta = jnp.sum(grad_att.astype(jnp.float32) * attended, axis=-1)
    pre_probs = jnp.exp(pre_scores - log_total[..., None])
    grad_pre_probs = jnp.einsum(
        "shqd,hpd->shqp", grad_att, prefix_low[1], preferred_element_type=jnp.float32
    )
    grad_pre_scores = (pre_probs * (grad_pre_probs - row_delta[..., None])).astype(jnp.bfloat16)
    grad_query_pre = (
        jnp.einsum(
            "shqp,hpd->shqd", grad_pre_scores, prefix_low[0], preferred_element_type=jnp.float32
        )
        * score_scale
    )
    grad_pre_keys = (
        jnp.einsum("shqp,shqd->hpd", grad_pre_scores, queries, preferred_element_type=jnp.float32)
        * score_scale
    )
    grad_pre_values = jnp.einsum(
        "shqp,shqd->hpd",
        pre_probs.astype(jnp.bfloat16),
        grad_att,
        preferred_element_type=jnp.float32,
    )
    prefix_terms = (
        jnp.stack([grad_pre_keys, grad_pre_values])
        .transpose(0, 2, 1, 3)
        .reshape(2, prefix_slots, local_width)
    )
    empty_grad = jnp.zeros(queries.shape, jnp.float32)

    def back_visit(query_side, key_side):
        return back_block(
            query_side[0],
            query_side[1],
            query_side[2],
            query_side[3],
            key_side[0],
            key_side[1],
            key_side[2],
            score_scale,
        )

    own_key_side = (own_keys, own_values, own_bias)

    def query_turn(turn_index, carried):
        grad_keys, grad_values, visit_queries, visit_grad, visit_total, visit_delta, visit_sum = (
            carried
        )
        turn_queries, turn_keys, turn_values = back_visit(
            (visit_queries, visit_grad, visit_total, visit_delta), own_key_side
        )
        moved = (
            shifted(visit_queries.astype(jnp.float32), "seq", 1).astype(visit_queries.dtype),
            shifted(visit_grad.astype(jnp.float32), "seq", 1).astype(visit_grad.dtype),
            shifted(visit_total, "seq", 1),
            shifted(visit_delta, "seq", 1),
            shifted(visit_sum + turn_queries, "seq", 1),
        )
        return (grad_keys + turn_keys, grad_values + turn_values) + moved

    carried = lax.fori_loop(
        0,
        cycle_size - 1,
        query_turn,
        (empty_grad, empty_grad, queries, grad_att, log_total, row_delta, grad_query_pre),
    )
    grad_keys, grad_values, visit_queries, visit_grad, visit_total, visit_delta, visit_sum = carried
    turn_queries, turn_keys, turn_values = back_visit(
        (visit_queries, visit_grad, visit_total, visit_delta), own_key_side
    )
    grad_keys = grad_keys + turn_keys
    grad_values = grad_values + turn_values
    grad_queries = shifted(visit_sum + turn_queries, "seq", 1)
    grad_rows = (
        jnp.stack([grad_queries, grad_keys, grad_values])
        .astype(jnp.bfloat16)
        .transpose(0, 1, 3, 2, 4)
        .reshape(3, row_count, local_width)
    )
    input_part = jnp.einsum("ite,ide->td", grad_rows, w_qkv, preferred_element_type=jnp.float32)
    input_grad = grad_one + lax.psum(input_part, "head")
    prefix_grad = lax.psum(prefix_terms, ("seq", "batch"))
    new_first = BETA_ONE * first_moment + (1.0 - BETA_ONE) * prefix_grad
    new_second = BETA_TWO * second_moment + (1.0 - BETA_TWO) * prefix_grad * prefix_grad
    first_hat = new_first / (1.0 - BETA_ONE**STEP)
    second_hat = new_second / (1.0 - BETA_TWO**STEP)
    new_prefix = prefix - LEARN_RATE * (
        first_hat / (jnp.sqrt(second_hat) + ADAM_EPSILON) + WEIGHT_DECAY * prefix
    )
    layer_out = layer_value.reshape(seqs_dev, shard_len, model_width)
    return (
        layer_out,
        input_grad.reshape(seqs_dev, shard_len, model_width),
        prefix_grad,
        new_prefix,
        new_first,
        new_second,
    )


BF = jnp.bfloat16
F32 = jnp.float32
MESH = pl.DeviceIdType.MESH
AHEAD = 2


def nn(left, right):
    return jnp.dot(left, right, preferred_element_type=F32)


def nt(left, right):
    return lax.dot_general(
        left, right, (((1,), (1,)), ((), ())), preferred_element_type=F32
    )


def remote(src, dst, send, recv, device):
    return pltpu.make_async_remote_copy(
        src, dst, send, recv, device_id=device, device_id_type=MESH
    )


def rows_at(start, size, step=64):
    return pl.ds(pl.multiple_of(start, step), size)


def places():
    z = lax.axis_index("seq")
    h = lax.axis_index("head")
    y = lax.axis_index("batch")
    return z, h, y


def member(h, u):
    chip, core = h // 2, lax.rem(h, 2)
    return 2 * lax.rem(chip + u // 2, 2) + lax.rem(core + u % 2, 2)


def z_peers(z):
    return [z + 1 - 2 * lax.rem(z, 2), 3 - z, lax.rem(z + 2, 4)]


def greet(devices):
    barrier = pltpu.get_barrier_semaphore()
    for device in devices:
        pl.semaphore_signal(barrier, inc=1, device_id=device, device_id_type=MESH)
    pl.semaphore_wait(barrier, len(devices))


def lane_masks():
    lane = lax.broadcasted_iota(jnp.int32, (1, 128), 1)
    inside = [lane < HEAD_DIM, lane >= HEAD_DIM]
    spare = [lane == HEAD_DIM, lane == 0]
    return inside, spare


def layer_kernel(
    tokens,
    cot,
    w_qkv,
    w_out,
    w_in,
    w_down,
    prefix,
    proj_bias,
    ffn_bias,
    gains,
    shifts,
    lengths,
    key_mask,
    lo_all,
    ig_all,
    pre_o,
    tok,
    cotg,
    bias_s,
    bias_g,
    wq,
    wo,
    wi,
    wd,
    fb,
    q_s,
    k_s,
    v_s,
    kx,
    vtx,
    pt,
    att_loc,
    att_all,
    rl_s,
    normed_s,
    xhat_s,
    nb_s,
    acc,
    act,
    gp,
    lo_s,
    da_s,
    da_all,
    ds_pre,
    dox,
    dq_s,
    core_out,
    core_in,
    x_out,
    x_in,
    fin,
    pre_part,
    pre_land,
    pre_sum,
    loc_sem,
    out_sem,
    tok_sem,
    cot_sem,
    bias_sem,
    fb_sem,
    att_sem,
    core_sem,
    x_sem,
    y_sem,
    c1_sem,
    c2_sem,
    lower_sem,
    lo_sem,
    lox_sem,
    loc_lo_sem,
    lox_core_sem,
    da_sem,
    part_core_sem,
    part_x_sem,
    igz_sem,
    igx_sem,
    igc_sem,
    igcx_sem,
    pre_sem,
    pre2_sem,
):
    z, h, y = places()
    core = lax.rem(h, 2)
    hc, hx, hd_ = member(h, 1), member(h, 2), member(h, 3)
    dev_core, dev_x, dev_diag, dev_y = (z, hc, y), (z, hx, y), (z, hd_, y), (z, h, 1 - y)
    zs = z_peers(z)
    width = tok.shape[1]
    piece = width // 4
    slots = prefix.shape[1]
    total = 4 * width
    group = 2 * z + y
    others = [lax.rem(group + d, 8) for d in range(1, 8)]
    greet([dev_core, dev_x, dev_diag] + [(g // 2, h, lax.rem(g, 2)) for g in others])

    half = width // 2
    my_half = rows_at(core * half, half)
    tok_copies, tok_forwards = [], []
    for k, zp in enumerate(zs):
        tok_copies.append(
            remote(tokens.at[zp, my_half], tok.at[z, my_half], tok_sem.at[0, k], tok_sem.at[1, k], (zp, h, y))
        )
        tok_forwards.append(
            remote(tok.at[zp, my_half], tok.at[zp, my_half], tok_sem.at[2, k], tok_sem.at[3, k], dev_core)
        )
    for copy in tok_copies:
        copy.start()
    tok_own = pltpu.make_async_copy(tokens.at[z], tok.at[z], loc_sem.at[0])
    tok_own.start()
    wq_own = pltpu.make_async_copy(w_qkv, wq, loc_sem.at[1])
    wq_own.start()

    chunks = [(w_out, wo, w_out.shape[0] // 2, 0, w_out.shape[0] // 2)]
    deep = w_in.shape[0] // 2
    for i in range(4):
        chunks.append((w_in, wi, deep, i * (deep // 4), deep // 4))
    deep = w_down.shape[0] // 4
    for i in range(2):
        chunks.append((w_down, wd, deep, i * (deep // 2), deep // 2))
    over_x, over_y, core_x, core_y = [], [], [], []
    for i, (src, dst, deep, offset, size) in enumerate(chunks):
        mine = rows_at(y * deep + offset, size, 128)
        other = rows_at((1 - y) * deep + offset, size, 128)
        over_x.append(remote(src.at[mine], dst.at[h, mine], x_sem.at[0, i], x_sem.at[1, i], dev_x))
        over_y.append(remote(dst.at[hx, mine], dst.at[hx, mine], y_sem.at[0, i], y_sem.at[1, i], dev_y))
        core_x.append(remote(dst.at[hx, mine], dst.at[hx, mine], c1_sem.at[0, i], c1_sem.at[1, i], dev_core))
        core_y.append(remote(dst.at[hx, other], dst.at[hx, other], c2_sem.at[0, i], c2_sem.at[1, i], dev_core))
    n_chunks = len(chunks)
    base, size = w_down.shape[0] // 2, w_down.shape[0] // 8
    lower = rows_at(base + z * size, size, 128)
    lower_x = remote(w_down.at[lower], wd.at[h, lower], x_sem.at[0, 7], x_sem.at[1, 7], dev_x)
    lower_core = [remote(wd.at[hx, lower], wd.at[hx, lower], c1_sem.at[0, 7], c1_sem.at[1, 7], dev_core)]
    lower_z = []
    for k, zp in enumerate(zs):
        theirs = rows_at(base + zp * size, size, 128)
        lower_z.append(
            remote(wd.at[hx, lower], wd.at[hx, lower], lower_sem.at[0, k], lower_sem.at[1, k], (zp, h, y))
        )
        lower_core.append(
            remote(wd.at[hx, theirs], wd.at[hx, theirs], lower_sem.at[2, k], lower_sem.at[3, k], dev_core)
        )
    x_queue = [over_x[0], lower_x] + over_x[1:]
    for copy in x_queue[:AHEAD]:
        copy.start()

    def serve_x(place):
        x_queue[place].wait_recv()
        if place == 1:
            lower_core[0].start()
        else:
            i = place - 1 if place else 0
            over_y[i].start()
            core_x[i].start()
        if place + AHEAD < len(x_queue):
            x_queue[place + AHEAD].start()

    def serve_y(i):
        over_y[i].wait_recv()
        core_y[i].start()

    own_weights, core_weights = [], []
    for i, (src, dst) in enumerate(((w_out, wo), (w_in, wi), (w_down, wd))):
        own_weights.append(pltpu.make_async_copy(src, dst.at[h], loc_sem.at[2 + i]))
        core_weights.append(remote(src, dst.at[h], core_sem.at[0, i], core_sem.at[1, i], dev_core))

    spot = lax.broadcasted_iota(jnp.int32, (8, width), 1) + z * width
    for s in range(4):
        live = (jnp.broadcast_to(key_mask[s : s + 1, :], (8, width)) == 1) & (spot < lengths[s])
        bias_s[s] = jnp.where(live, 0.0, NEG_FILL)
    bias_g[z] = bias_s[z]
    bias_copies = [
        remote(bias_s.at[zp], bias_g.at[z], bias_sem.at[0, k], bias_sem.at[1, k], (zp, h, y))
        for k, zp in enumerate(zs)
    ]
    fb[h] = jnp.broadcast_to(ffn_bias[...], fb.shape[1:])
    fb_copies = [
        remote(fb.at[h], fb.at[h], fb_sem.at[0, k], fb_sem.at[1, k], device)
        for k, device in enumerate((dev_core, dev_x, dev_diag))
    ]
    for copy in bias_copies + fb_copies:
        copy.start()
    for copy in own_weights + core_weights:
        copy.start()

    my_piece = rows_at(h * piece, piece)
    cot_copies = [
        remote(cot.at[zp, my_piece], cotg.at[z], cot_sem.at[0, k], cot_sem.at[1, k], (zp, h, y))
        for k, zp in enumerate(zs)
    ]
    cot_own = pltpu.make_async_copy(cot.at[z, my_piece], cotg.at[z], loc_sem.at[5])
    cot_own.start()

    inside, spare = lane_masks()

    pk = prefix[0].astype(BF)
    pv = prefix[1].astype(BF)
    k_s[total : total + slots, :] = pk
    v_s[total : total + slots, :] = pv
    for head in range(4):
        pair, par = head // 2, head % 2
        part = pk[:, 128 * pair : 128 * pair + 128].astype(F32)
        kx[head, total : total + slots, :] = jnp.where(inside[par], part, 0.0).astype(BF)
        vtx[head, HEAD_DIM:, :] = jnp.ones((vtx.shape[1] - HEAD_DIM, vtx.shape[2]), BF)

    def project(block):
        rows = tok[block]
        for i, target in enumerate((q_s, k_s, v_s)):
            value = (nn(rows, wq[i]) + proj_bias[i : i + 1, :]).astype(BF)
            if i == 0:
                value = (value.astype(F32) * HEAD_DIM**-0.5).astype(BF)
            for j in range(4):
                target[rows_at(j * width + block * piece, piece), :] = value[piece * j : piece * j + piece]
            if i == 1:
                column = jnp.broadcast_to(bias_g[block][0:1, :], (128, width)).T
                for head in range(4):
                    pair, par = head // 2, head % 2
                    part = value[:, 128 * pair : 128 * pair + 128].astype(F32)
                    ext = jnp.where(inside[par], part, jnp.where(spare[par], column, 0.0)).astype(BF)
                    for j in range(4):
                        kx[head, rows_at(j * width + block * piece, piece), :] = ext[piece * j : piece * j + piece]

    tok_own.wait()
    wq_own.wait()
    project(z)
    serve_x(0)
    for k, zp in enumerate(zs):
        serve_x(k + 1)
        if k != 1:
            serve_y(k // 2)
        tok_copies[k].wait_recv()
        tok_forwards[k].start()
        bias_copies[k].wait_recv()
        if k == 2:
            for copy in lower_z + cot_copies:
                copy.start()
        tok_forwards[k].wait_recv()
        project(zp)

    for i in range(4):
        flipped = v_s[i * width : (i + 1) * width, :].astype(F32).T.astype(BF)
        for head in range(4):
            vtx[head, 0:HEAD_DIM, i * width : (i + 1) * width] = flipped[HEAD_DIM * head : HEAD_DIM * (head + 1)]
    flipped = v_s[total : total + slots, :].astype(F32).T.astype(BF)
    for head in range(4):
        vtx[head, 0:HEAD_DIM, total : total + slots] = flipped[HEAD_DIM * head : HEAD_DIM * (head + 1)]

    def att_copy(u):
        j = member(h, u)
        return remote(att_loc.at[j], att_all.at[h], att_sem.at[0, u], att_sem.at[1, u], (z, j, y))

    def attend(step):
        u = 3 - step
        j = member(h, u)
        outs, recips = [], []
        for head in range(4):
            pair, par = head // 2, head % 2
            part = q_s[rows_at(j * width, width, width), 128 * pair : 128 * pair + 128].astype(F32)
            ext = jnp.where(inside[par], part, jnp.where(spare[par], 1.0, 0.0)).astype(BF)
            scores = nt(kx[head], ext)
            top = jnp.max(scores, axis=0, keepdims=True)
            weight = jnp.exp(scores - top).astype(BF)
            pt[head, j] = weight
            summed = nn(vtx[head], weight)
            recip = 1.0 / summed[HEAD_DIM : HEAD_DIM + 1]
            outs.append(summed[0:HEAD_DIM] * recip)
            recips.append(jnp.broadcast_to(recip, (32, width)))
        att_loc[j] = jnp.concatenate(outs, axis=0).T.astype(BF)
        rl_s[j] = jnp.concatenate(recips, axis=0).T

        @pl.when(u > 0)
        def _():
            att_copy(u).start()

        @pl.when(u == 0)
        def _():
            att_all[h] = att_loc[h]

    pl.loop(0, 2)(attend)
    serve_x(4)
    serve_y(2)
    pl.loop(2, 4)(attend)
    serve_x(5)
    serve_y(3)
    att_copies = [att_copy(u) for u in (1, 2, 3)]

    lane = lax.broadcasted_iota(jnp.int32, (1, 128), 1)
    spare_lo = [lane == HEAD_DIM + 1, lane == 1]
    for head in range(4):
        pair, par = head // 2, head % 2
        part = v_s[:, 128 * pair : 128 * pair + 128].astype(F32)
        ones = jnp.where(spare[par] | spare_lo[par], 1.0, 0.0)
        kx[head] = jnp.where(inside[par], part, ones).astype(BF)
    for i in range(5):
        low, size = i * width, width if i < 4 else slots
        flipped = k_s[low : low + size, :].astype(F32).T.astype(BF)
        for head in range(4):
            vtx[head, 0:HEAD_DIM, low : low + size] = flipped[HEAD_DIM * head : HEAD_DIM * (head + 1)]

    own_weights[0].wait()
    core_weights[0].wait_recv()
    core_x[0].wait_recv()
    core_y[0].wait_recv()
    for copy in att_copies:
        copy.wait_recv()
    attention = nn(att_all[0], wo[0])
    for j in range(1, 4):
        attention += nn(att_all[j], wo[j])
    mine = jnp.concatenate([tok[b, my_piece, :] for b in range(4)], axis=0).astype(F32)
    resid = mine + attention + shifts[0:1, :]
    centred = resid - jnp.mean(resid, axis=-1, keepdims=True)
    inverse_one = lax.rsqrt(jnp.mean(centred * centred, axis=-1, keepdims=True) + NORM_EPSILON)
    xhat = centred * inverse_one
    xhat_s[...] = xhat
    normed = xhat * gains[0:1, :] + shifts[1:2, :]
    normed_s[...] = normed
    nb_s[...] = normed.astype(BF)

    tile = 256
    tiles = wi.shape[2] // tile

    def ffn_in(quarter):
        @pl.loop(0, tiles, unroll=4)
        def _(n):
            cols = rows_at(n * tile, tile, tile)
            inner = nn(nb_s[...], wi[quarter, :, cols]) + fb[quarter, 0:1, cols]
            cdf = 0.5 * (1.0 + lax.erf(inner * 0.7071067811865476))
            act[quarter, :, cols] = (inner * cdf).astype(BF)
            gp[quarter, :, cols] = cdf + inner * (jnp.exp(-0.5 * inner * inner) * 0.3989422804014327)

    for copy in fb_copies:
        copy.wait_recv()
    own_weights[1].wait()
    core_weights[1].wait_recv()
    ffn_in(h)
    ffn_in(hc)
    serve_x(6)
    serve_y(4)
    for i in range(1, 5):
        core_x[i].wait_recv()
        core_y[i].wait_recv()
    ffn_in(hx)
    ffn_in(hd_)

    acc[...] = jnp.zeros(acc.shape, F32)

    def ffn_out(quarter, start, deep):
        span = rows_at(start, deep, deep)

        @pl.loop(0, tiles, unroll=4)
        def _(n):
            cols = rows_at(n * tile, tile, tile)
            acc[:, cols] += nn(act[quarter, :, span], wd[quarter, span, cols])

    own_weights[2].wait()
    core_weights[2].wait_recv()
    deep = wd.shape[1]
    for k in range(3):
        lower_z[k].wait_recv()
        lower_core[k + 1].start()
    ffn_out(h, 0, deep)
    serve_x(7)
    serve_y(5)
    ffn_out(hc, 0, deep)
    ffn_out(hx, base, deep // 2)
    for copy in lower_core:
        copy.wait_recv()
    ffn_out(hd_, base, deep // 2)
    for i in (5, 6):
        core_x[i].wait_recv()
    ffn_out(hx, y * (deep // 4), deep // 4)
    ffn_out(hd_, y * (deep // 4), deep // 4)
    serve_y(6)
    ffn_out(hx, (1 - y) * (deep // 4), deep // 4)
    for i in (5, 6):
        core_y[i].wait_recv()
    ffn_out(hd_, (1 - y) * (deep // 4), deep // 4)

    resid = normed_s[...] + acc[...] + shifts[2:3, :]
    centred = resid - jnp.mean(resid, axis=-1, keepdims=True)
    inverse = lax.rsqrt(jnp.mean(centred * centred, axis=-1, keepdims=True) + NORM_EPSILON)
    xhat = centred * inverse
    lo_s[...] = (xhat * gains[1:2, :] + shifts[3:4, :]).astype(BF)
    x_piece = rows_at(hx * piece, piece)
    lo_z, lo_x, lo_core, lo_across = [], [], [], []
    blocks = zs + [z]
    for k, b in enumerate(blocks):
        rows = rows_at(b * piece, piece)
        source = lo_all.at[b, my_piece]
        if k < 3:
            lo_z.append(remote(lo_s.at[rows], lo_all.at[z, my_piece], lo_sem.at[0, k], lo_sem.at[1, k], (b, h, y)))
        else:
            source = lo_s.at[rows]
        lo_x.append(remote(source, lo_all.at[b, my_piece], lox_sem.at[0, k], lox_sem.at[1, k], dev_x))
        lo_core.append(remote(source, lo_all.at[b, my_piece], loc_lo_sem.at[0, k], loc_lo_sem.at[1, k], dev_core))
        lo_across.append(
            remote(lo_all.at[b, x_piece], lo_all.at[b, x_piece], lox_core_sem.at[0, k], lox_core_sem.at[1, k], dev_core)
        )
    lo_own = pltpu.make_async_copy(lo_s.at[rows_at(z * piece, piece)], lo_all.at[z, my_piece], out_sem.at[0])
    for copy in lo_z + [lo_x[3], lo_core[3], lo_own]:
        copy.start()

    def serve_lo(k):
        lo_z[k].wait_recv()
        lo_x[k].start()
        lo_core[k].start()

    cot_own.wait()
    for copy in cot_copies:
        copy.wait_recv()
    dy = jnp.concatenate([cotg[b] for b in range(4)], axis=0).astype(F32) * gains[1:2, :]
    g_two = inverse * (
        dy - jnp.mean(dy, axis=-1, keepdims=True) - xhat * jnp.mean(dy * xhat, axis=-1, keepdims=True)
    )
    acc[...] = g_two
    nb_s[...] = g_two.astype(BF)

    @pl.loop(0, 4)
    def _(quarter):
        @pl.loop(0, tiles, unroll=4)
        def _(n):
            cols = rows_at(n * tile, tile, tile)
            d_act = nt(nb_s[...], wd[quarter, cols, :])
            act[quarter, :, cols] = (d_act * gp[quarter, :, cols]).astype(BF)

    serve_lo(0)

    @pl.loop(0, 4)
    def _(quarter):
        @pl.loop(0, tiles, unroll=4)
        def _(n):
            cols = rows_at(n * tile, tile, tile)
            acc[:, cols] += nt(act[quarter], wi[quarter, cols, :])

    serve_lo(1)
    dy = acc[...] * gains[0:1, :]
    xhat = xhat_s[...]
    g_one = inverse_one * (
        dy - jnp.mean(dy, axis=-1, keepdims=True) - xhat * jnp.mean(dy * xhat, axis=-1, keepdims=True)
    )
    acc[...] = g_one
    low = g_one.astype(BF)
    da_copies = {}
    for u in (2, 3, 1):
        j = member(h, u)
        da_s[j] = nt(low, wo[j]).astype(BF)
        da_copies[u] = remote(da_s.at[j], da_all.at[h], da_sem.at[0, u], da_sem.at[1, u], (z, j, y))
        da_copies[u].start()
    da_all[h] = nt(low, wo[h]).astype(BF)
    for copy in over_y + core_x + core_y + lower_z + lower_core:
        copy.wait_send()

    @pl.loop(0, 4)
    def _(u):
        j = member(h, u)

        @pl.when(u > 0)
        def _():
            remote(da_s.at[j], da_all.at[h], da_sem.at[0, u], da_sem.at[1, u], (z, j, y)).wait_recv()

        grads = []
        for head in range(4):
            pair, par = head // 2, head % 2
            lanes = slice(128 * pair, 128 * pair + 128)
            d_out = da_all[j, :, lanes].astype(F32)
            recip = rl_s[j, :, 32 * head : 32 * head + 1]
            delta = recip * jnp.sum(
                jnp.where(inside[par], d_out * att_loc[j, :, lanes].astype(F32), 0.0), axis=-1, keepdims=True
            )
            high = delta.astype(BF).astype(F32)
            ext = jnp.where(spare[par], -high, jnp.where(spare_lo[par], high - delta, 0.0))
            ext = jnp.where(inside[par], d_out * recip, ext).astype(BF)
            dox[head, j] = ext
            d_probs = nt(kx[head], ext).astype(BF)
            d_scores = pt[head, j] * d_probs
            wi[head, :, rows_at(j * width, width, width)] = d_scores[0:total]
            ds_pre[head, j] = d_scores[total:]
            grads.append(nn(vtx[head, 0:HEAD_DIM, :], d_scores))
        dq_s[j] = (jnp.concatenate(grads, axis=0).T * HEAD_DIM**-0.5).astype(BF)

    serve_lo(2)

    def key_side(left, right):
        halves = []
        for pair in range(2):
            sides = []
            for par in range(2):
                head = 2 * pair + par
                value = nn(left(head, 0), right(head, 0, pair))
                for j in range(1, 4):
                    value += nn(left(head, j), right(head, j, pair))
                sides.append(value)
            halves.append(jnp.where(inside[0], sides[0], sides[1]))
        return jnp.concatenate(halves, axis=-1)

    def d_values(rows):
        return key_side(lambda head, j: pt[head, j, rows, :], lambda head, j, pair: dox[head, j])

    def d_keys(left):
        return key_side(left, lambda head, j, pair: q_s[j * width : (j + 1) * width, 128 * pair : 128 * pair + 128])

    def partial(i):
        rows = rows_at(i * width, width, width)
        dk = d_keys(lambda head, j: wi[head, rows, j * width : (j + 1) * width]).astype(BF)
        dv = d_values(rows).astype(BF)
        return nt(dq_s[i], wq[0]) + nt(dk, wq[1]) + nt(dv, wq[2])

    part_core = [
        remote(core_out.at[i], core_in.at[i], part_core_sem.at[0, i], part_core_sem.at[1, i], dev_core) for i in range(2)
    ]
    part_x = []
    for k, b in enumerate(blocks):
        rows = rows_at(b * piece, piece)
        part_x.append(remote(x_out.at[rows], x_in.at[rows], part_x_sem.at[0, k], part_x_sem.at[1, k], dev_x))

    core_out[0] = partial(hd_).astype(BF)
    part_core[0].start()
    mine = partial(hx)
    part_core[0].wait_recv()
    x_out[...] = (mine + core_in[0].astype(F32)).astype(BF)
    for copy in part_x:
        copy.start()

    pre_part[0] = d_keys(lambda head, j: ds_pre[head, j])
    pre_part[1] = d_values(pl.ds(total, slots))
    few = slots // 8
    mine_rows = rows_at(group * few, few, few)
    pre_copies, pre_back = [], []
    for d, g in enumerate(others):
        device = (g // 2, h, lax.rem(g, 2))
        pre_copies.append(
            remote(pre_part.at[:, rows_at(g * few, few, few)], pre_land.at[d], pre_sem.at[0, d], pre_sem.at[1, d], device)
        )
        pre_back.append(
            remote(pre_sum.at[:, mine_rows], pre_sum.at[:, mine_rows], pre2_sem.at[0, d], pre2_sem.at[1, d], device)
        )
    for copy in pre_copies:
        copy.start()
    for k in (3, 0, 1, 2):
        lo_x[k].wait_recv()
        lo_across[k].start()

    core_out[1] = partial(hc).astype(BF)
    part_core[1].start()
    acc[...] += partial(h)
    part_core[1].wait_recv()
    acc[...] += core_in[1].astype(F32)

    igz, igx, igc, igcx = [], [], [], []
    for k, b in enumerate(blocks):
        rows = rows_at(b * piece, piece)
        source = ig_all.at[b, my_piece]
        if k < 3:
            igz.append(remote(fin.at[rows], ig_all.at[z, my_piece], igz_sem.at[0, k], igz_sem.at[1, k], (b, h, y)))
        else:
            source = fin.at[rows]
        igx.append(remote(source, ig_all.at[b, my_piece], igx_sem.at[0, k], igx_sem.at[1, k], dev_x))
        igc.append(remote(source, ig_all.at[b, my_piece], igc_sem.at[0, k], igc_sem.at[1, k], dev_core))
        igcx.append(
            remote(ig_all.at[b, x_piece], ig_all.at[b, x_piece], igcx_sem.at[0, k], igcx_sem.at[1, k], dev_core)
        )
    ig_own = pltpu.make_async_copy(fin.at[rows_at(z * piece, piece)], ig_all.at[z, my_piece], out_sem.at[1])
    for k, b in enumerate(blocks):
        rows = rows_at(b * piece, piece)
        part_x[k].wait_recv()
        fin[rows, :] = (acc[rows, :] + x_in[rows, :].astype(F32)).astype(BF)
        if k < 3:
            igz[k].start()
        else:
            ig_own.start()
            igx[3].start()
            igc[3].start()
        if k == 1:
            for copy in pre_copies:
                copy.wait_recv()
            for i in range(2):
                term = pre_part[i, mine_rows, :]
                for d in range(7):
                    term += pre_land[d, i]
                pre_sum[i, mine_rows, :] = term
            for copy in pre_back:
                copy.start()
    for copy in lo_core + lo_across:
        copy.wait_recv()
    lo_own.wait()
    for k in range(3):
        igz[k].wait_recv()
        igx[k].start()
        igc[k].start()
    for copy in pre_back:
        copy.wait_recv()
    pre_o[...] = pre_sum[...]
    for k in (3, 0, 1, 2):
        igx[k].wait_recv()
        igcx[k].start()
    for copy in igc + igcx:
        copy.wait_recv()
    ig_own.wait()
    sent = tok_copies + tok_forwards + x_queue + core_weights + bias_copies + fb_copies + cot_copies + att_copies
    sent += lo_z + lo_x + lo_core + lo_across + list(da_copies.values()) + part_core + part_x
    for copy in sent + igz + igx + igc + igcx + pre_copies + pre_back:
        copy.wait_send()


def layer(tokens, cot, w_qkv, w_out, w_in, w_down, prefix, proj_bias, ffn_bias, gains, shifts, lengths, key_mask):
    seqs, width, model = tokens.shape
    local = w_qkv.shape[2]
    hidden = w_in.shape[1]
    slots = prefix.shape[1]
    total = seqs * width
    keys = total + slots
    dma = pltpu.SemaphoreType.DMA
    hbm = pl.BlockSpec(memory_space=pl.ANY)
    vmem = pl.BlockSpec(memory_space=pltpu.VMEM)
    shape = jax.ShapeDtypeStruct
    return pl.pallas_call(
        layer_kernel,
        name="layer",
        out_shape=(
            pltpu.VMEM((4, width, model), BF),
            pltpu.VMEM((4, width, model), BF),
            shape((2, slots, local), F32),
        ),
        in_specs=[hbm] * 6 + [vmem] * 5 + [pl.BlockSpec(memory_space=pltpu.SMEM), vmem],
        out_specs=(vmem, vmem, vmem),
        scratch_shapes=[
            pltpu.VMEM((4, width, model), BF),
            pltpu.VMEM((4, width // 4, model), BF),
            pltpu.VMEM((4, 8, width), F32),
            pltpu.VMEM((4, 8, width), F32),
            pltpu.VMEM((3, model, local), BF),
            pltpu.VMEM((4, local, model), BF),
            pltpu.VMEM((4, model, hidden), BF),
            pltpu.VMEM((4, hidden, model), BF),
            pltpu.VMEM((4, 8, hidden), F32),
            pltpu.VMEM((total, local), BF),
            pltpu.VMEM((keys, local), BF),
            pltpu.VMEM((keys, local), BF),
            pltpu.VMEM((4, keys, 128), BF),
            pltpu.VMEM((4, HEAD_DIM + 16, keys), BF),
            pltpu.VMEM((4, 4, keys, width), BF),
            pltpu.VMEM((4, width, local), BF),
            pltpu.VMEM((4, width, local), BF),
            pltpu.VMEM((4, width, 128), F32),
            pltpu.VMEM((width, model), F32),
            pltpu.VMEM((width, model), F32),
            pltpu.VMEM((width, model), BF),
            pltpu.VMEM((width, model), F32),
            pltpu.VMEM((4, width, hidden), BF),
            pltpu.VMEM((4, width, hidden), F32),
            pltpu.VMEM((width, model), BF),
            pltpu.VMEM((4, width, local), BF),
            pltpu.VMEM((4, width, local), BF),
            pltpu.VMEM((4, 4, slots, width), BF),
            pltpu.VMEM((4, 4, width, 128), BF),
            pltpu.VMEM((4, width, local), BF),
            pltpu.VMEM((2, width, model), BF),
            pltpu.VMEM((2, width, model), BF),
            pltpu.VMEM((width, model), BF),
            pltpu.VMEM((width, model), BF),
            pltpu.VMEM((width, model), BF),
            pltpu.VMEM((2, slots, local), F32),
            pltpu.VMEM((7, 2, slots // 8, local), F32),
            pltpu.VMEM((2, slots, local), F32),
            dma((6,)),
            dma((4,)),
            dma((4, 3)),
            dma((2, 3)),
            dma((2, 3)),
            dma((2, 3)),
            dma((2, 4)),
            dma((2, 3)),
            dma((2, 9)),
            dma((2, 9)),
            dma((2, 9)),
            dma((2, 9)),
            dma((4, 3)),
            dma((2, 3)),
            dma((2, 4)),
            dma((2, 4)),
            dma((2, 4)),
            dma((2, 4)),
            dma((2, 2)),
            dma((2, 4)),
            dma((2, 3)),
            dma((2, 4)),
            dma((2, 4)),
            dma((2, 4)),
            dma((2, 7)),
            dma((2, 7)),
        ],
        compiler_params=pltpu.CompilerParams(
            collective_id=0, has_side_effects=True, vmem_limit_bytes=58 * 2**20
        ),
        cost_estimate=pl.CostEstimate(flops=15 * 10**9, bytes_accessed=40 * 2**20, transcendentals=6 * 10**6),
    )(tokens, cot, w_qkv, w_out, w_in, w_down, prefix, proj_bias, ffn_bias, gains, shifts, lengths, key_mask)


def finish_kernel(lo, ig, grad, prefix, first, second, lo_o, ig_o, grad_o, new_o, first_o, second_o, lo_f, ig_f, sem):
    seqs = lo.shape[0]
    copies = []
    for i in range(seqs):
        for k, (src, mid, dst) in enumerate(((lo, lo_f, lo_o), (ig, ig_f, ig_o))):
            mid[i] = src[i].astype(F32)
            copy = pltpu.make_async_copy(mid.at[i], dst.at[i], sem.at[k, i])
            copy.start()
            copies.append(copy)
    slope = grad[...]
    grad_o[...] = slope
    new_first = BETA_ONE * first[...] + (1.0 - BETA_ONE) * slope
    new_second = BETA_TWO * second[...] + (1.0 - BETA_TWO) * slope * slope
    first_hat = new_first / (1.0 - BETA_ONE**STEP)
    second_hat = new_second / (1.0 - BETA_TWO**STEP)
    value = prefix[...]
    new_o[...] = value - LEARN_RATE * (first_hat / (jnp.sqrt(second_hat) + ADAM_EPSILON) + WEIGHT_DECAY * value)
    first_o[...] = new_first
    second_o[...] = new_second
    for copy in copies:
        copy.wait()


def finish(lo, ig, grad, prefix, first, second):
    hbm = pl.BlockSpec(memory_space=pl.ANY)
    vmem = pl.BlockSpec(memory_space=pltpu.VMEM)
    shape = jax.ShapeDtypeStruct
    whole, little = shape(lo.shape, F32), shape(prefix.shape, F32)
    return pl.pallas_call(
        finish_kernel,
        name="finish",
        out_shape=(whole, whole, little, little, little, little),
        in_specs=[vmem] * 6,
        out_specs=(hbm, hbm, vmem, vmem, vmem, vmem),
        scratch_shapes=[
            pltpu.VMEM(lo.shape, F32),
            pltpu.VMEM(lo.shape, F32),
            pltpu.SemaphoreType.DMA((2, lo.shape[0])),
        ],
        compiler_params=pltpu.CompilerParams(vmem_limit_bytes=40 * 2**20),
    )(lo, ig, grad, prefix, first, second)


def body(*args):
    (tokens, cotangent, prefix, first_moment, second_moment, w_qkv, proj_bias, w_out, w_in, ffn_bias) = args[:10]
    w_down, gains, shifts, lengths, key_mask = args[10:]
    fits = (
        lax.axis_size("seq") == 4
        and lax.axis_size("head") == 4
        and lax.axis_size("batch") == 2
        and tokens.shape == (4, 256, 1024)
        and w_qkv.shape == (3, 1024, 256)
        and w_in.shape == (1024, 1024)
        and prefix.shape[1] == 64
    )
    if not fits:
        return general_body(*args)
    layer_out, input_grad, prefix_grad = layer(
        tokens, cotangent, w_qkv, w_out, w_in, w_down, prefix, proj_bias, ffn_bias.reshape(1, -1), gains, shifts,
        lengths, key_mask,
    )
    layer_out, input_grad, prefix_grad, new_prefix, new_first, new_second = finish(
        layer_out, input_grad, prefix_grad, prefix, first_moment, second_moment
    )
    return layer_out, input_grad, prefix_grad, new_prefix, new_first, new_second


def solution(mesh):
    placed = (
        P("batch", "seq", None),
        P("batch", "seq", None),
        P(None, None, "head"),
        P(None, None, "head"),
        P(None, None, "head"),
        P(None, None, "head"),
        P(None, "head"),
        P("head", None),
        P(None, "head"),
        P("head"),
        P("head", None),
        P(),
        P(),
        P("batch"),
        P("batch", "seq"),
    )
    return jax.shard_map(
        body,
        mesh=mesh,
        in_specs=placed,
        out_specs=(
            P("batch", "seq", None),
            P("batch", "seq", None),
            P(None, None, "head"),
            P(None, None, "head"),
            P(None, None, "head"),
            P(None, None, "head"),
        ),
        check_vma=False,
    )
```

```python
import jax
import jax.numpy as jnp
from jax import lax
from jax.experimental import pallas as pl
from jax.experimental.pallas import tpu as pltpu
from jax.sharding import PartitionSpec as P

HEAD_DIM = 64
STEP = 10


NEG_FILL = -1e30
NORM_EPSILON = 1e-05
BETA_ONE = 0.9
BETA_TWO = 0.95
LEARN_RATE = 0.8
WEIGHT_DECAY = 0.01
ADAM_EPSILON = 1e-08


def shifted(value, axis, steps):
    count = lax.axis_size(axis)
    pairs = [(source, (source + steps) % count) for source in range(count)]
    return lax.ppermute(value, axis, pairs)


def layer_norm(values_in, gain_row, shift_row):
    row_mean = jnp.mean(values_in, axis=-1, keepdims=True)
    centred = values_in - row_mean
    spread = jnp.mean(centred * centred, axis=-1, keepdims=True)
    return centred * lax.rsqrt(spread + NORM_EPSILON) * gain_row + shift_row


def exact_gelu(values_in):
    return jax.nn.gelu(values_in, approximate=False)


def block_scores(queries, block_keys, block_bias, score_scale):
    scores = (
        jnp.einsum("shqd,shkd->shqk", queries, block_keys, preferred_element_type=jnp.float32)
        * score_scale
    )
    return scores + block_bias.astype(jnp.float32)[:, None, None, :]


def absorb(softmax_state, queries, block_keys, block_values, block_bias, score_scale):
    row_max, row_sum, weighted = softmax_state
    scores = block_scores(queries, block_keys, block_bias, score_scale)
    new_max = jnp.maximum(row_max, jnp.max(scores, axis=-1))
    fade_factor = jnp.exp(row_max - new_max)
    exp_scores = jnp.exp(scores - new_max[..., None])
    row_sum = row_sum * fade_factor + jnp.sum(exp_scores, axis=-1)
    weighted = weighted * fade_factor[..., None] + jnp.einsum(
        "shqk,shkd->shqd",
        exp_scores.astype(jnp.bfloat16),
        block_values,
        preferred_element_type=jnp.float32,
    )
    return (new_max, row_sum, weighted)


def back_block(
    queries, grad_att, log_total, row_delta, block_keys, block_values, block_bias, score_scale
):
    scores = block_scores(queries, block_keys, block_bias, score_scale)
    probabilities = jnp.exp(scores - log_total[..., None])
    grad_probs = jnp.einsum(
        "shqd,shkd->shqk", grad_att, block_values, preferred_element_type=jnp.float32
    )
    grad_scores = (probabilities * (grad_probs - row_delta[..., None])).astype(jnp.bfloat16)
    grad_queries = (
        jnp.einsum("shqk,shkd->shqd", grad_scores, block_keys, preferred_element_type=jnp.float32)
        * score_scale
    )
    grad_keys = (
        jnp.einsum("shqk,shqd->shkd", grad_scores, queries, preferred_element_type=jnp.float32)
        * score_scale
    )
    grad_values = jnp.einsum(
        "shqk,shqd->shkd",
        probabilities.astype(jnp.bfloat16),
        grad_att,
        preferred_element_type=jnp.float32,
    )
    return (grad_queries, grad_keys, grad_values)


def general_body(
    tokens,
    cotangent,
    prefix,
    first_moment,
    second_moment,
    w_qkv,
    proj_bias,
    w_out,
    w_in,
    ffn_bias,
    w_down,
    gains,
    shifts,
    lengths,
    key_mask,
):
    seqs_dev, shard_len, model_width = tokens.shape
    row_count = seqs_dev * shard_len
    local_width = w_qkv.shape[2]
    heads_dev = local_width // HEAD_DIM
    prefix_slots = prefix.shape[1]
    score_scale = HEAD_DIM ** (-0.5)
    cycle_size = lax.axis_size("seq")
    cycle_place = lax.axis_index("seq")
    flat_tokens = tokens.reshape(row_count, model_width)
    projected = (
        jnp.einsum("td,ide->ite", flat_tokens, w_qkv, preferred_element_type=jnp.float32)
        + proj_bias[:, None, :]
    )
    by_head = (
        projected.astype(jnp.bfloat16)
        .reshape(3, seqs_dev, shard_len, heads_dev, HEAD_DIM)
        .transpose(0, 1, 3, 2, 4)
    )
    queries = by_head[0]
    own_keys = by_head[1]
    own_values = by_head[2]
    positions = cycle_place * shard_len + lax.broadcasted_iota(jnp.int32, (seqs_dev, shard_len), 1)
    live_keys = (key_mask == 1) & (positions < lengths[:, None])
    own_bias = jnp.where(live_keys, 0.0, NEG_FILL).astype(jnp.bfloat16)
    prefix_low = (
        prefix.astype(jnp.bfloat16)
        .reshape(2, prefix_slots, heads_dev, HEAD_DIM)
        .transpose(0, 2, 1, 3)
    )
    pre_scores = (
        jnp.einsum("shqd,hpd->shqp", queries, prefix_low[0], preferred_element_type=jnp.float32)
        * score_scale
    )
    row_max = jnp.max(pre_scores, axis=-1)
    exp_prefix = jnp.exp(pre_scores - row_max[..., None])
    row_sum = jnp.sum(exp_prefix, axis=-1)
    weighted = jnp.einsum(
        "shqp,hpd->shqd",
        exp_prefix.astype(jnp.bfloat16),
        prefix_low[1],
        preferred_element_type=jnp.float32,
    )

    def visit_keys(softmax_state, block_keys, block_values, block_bias):
        return absorb(softmax_state, queries, block_keys, block_values, block_bias, score_scale)

    def forward_turn(turn_index, carried):
        softmax_state, block_keys, block_values, block_bias = carried
        softmax_state = visit_keys(softmax_state, block_keys, block_values, block_bias)
        block_keys, block_values, block_bias = shifted(
            (block_keys, block_values, block_bias), "seq", 1
        )
        return (softmax_state, block_keys, block_values, block_bias)

    carried = lax.fori_loop(
        0,
        cycle_size - 1,
        forward_turn,
        ((row_max, row_sum, weighted), own_keys, own_values, own_bias),
    )
    row_max, row_sum, weighted = visit_keys(carried[0], carried[1], carried[2], carried[3])
    log_total = row_max + jnp.log(row_sum)
    attended = weighted / row_sum[..., None]
    merged = attended.astype(jnp.bfloat16).transpose(0, 2, 1, 3).reshape(row_count, local_width)
    attention = (
        lax.psum(jnp.dot(merged, w_out, preferred_element_type=jnp.float32), "head") + shifts[0]
    )
    resid_one = flat_tokens.astype(jnp.float32) + attention
    normed, norm_one_back = jax.vjp(
        lambda values_in: layer_norm(values_in, gains[0], shifts[1]), resid_one
    )
    inner_sum = (
        jnp.dot(normed.astype(jnp.bfloat16), w_in, preferred_element_type=jnp.float32) + ffn_bias
    )
    activated, gelu_back = jax.vjp(exact_gelu, inner_sum)
    feed_forward = (
        lax.psum(
            jnp.dot(activated.astype(jnp.bfloat16), w_down, preferred_element_type=jnp.float32),
            "head",
        )
        + shifts[2]
    )
    layer_value, norm_two_back = jax.vjp(
        lambda values_in: layer_norm(values_in, gains[1], shifts[3]), normed + feed_forward
    )
    contract_last = (((1,), (1,)), ((), ()))
    (grad_two,) = norm_two_back(cotangent.reshape(row_count, model_width).astype(jnp.float32))
    grad_act = lax.dot_general(
        grad_two.astype(jnp.bfloat16), w_down, contract_last, preferred_element_type=jnp.float32
    )
    (grad_inner,) = gelu_back(grad_act)
    hidden_part = lax.dot_general(
        grad_inner.astype(jnp.bfloat16), w_in, contract_last, preferred_element_type=jnp.float32
    )
    grad_normed = grad_two + lax.psum(hidden_part, "head")
    (grad_one,) = norm_one_back(grad_normed)
    grad_merged = lax.dot_general(
        grad_one.astype(jnp.bfloat16), w_out, contract_last, preferred_element_type=jnp.float32
    )
    grad_att = (
        grad_merged.astype(jnp.bfloat16)
        .reshape(seqs_dev, shard_len, heads_dev, HEAD_DIM)
        .transpose(0, 2, 1, 3)
    )
    row_delta = jnp.sum(grad_att.astype(jnp.float32) * attended, axis=-1)
    pre_probs = jnp.exp(pre_scores - log_total[..., None])
    grad_pre_probs = jnp.einsum(
        "shqd,hpd->shqp", grad_att, prefix_low[1], preferred_element_type=jnp.float32
    )
    grad_pre_scores = (pre_probs * (grad_pre_probs - row_delta[..., None])).astype(jnp.bfloat16)
    grad_query_pre = (
        jnp.einsum(
            "shqp,hpd->shqd", grad_pre_scores, prefix_low[0], preferred_element_type=jnp.float32
        )
        * score_scale
    )
    grad_pre_keys = (
        jnp.einsum("shqp,shqd->hpd", grad_pre_scores, queries, preferred_element_type=jnp.float32)
        * score_scale
    )
    grad_pre_values = jnp.einsum(
        "shqp,shqd->hpd",
        pre_probs.astype(jnp.bfloat16),
        grad_att,
        preferred_element_type=jnp.float32,
    )
    prefix_terms = (
        jnp.stack([grad_pre_keys, grad_pre_values])
        .transpose(0, 2, 1, 3)
        .reshape(2, prefix_slots, local_width)
    )
    empty_grad = jnp.zeros(queries.shape, jnp.float32)

    def back_visit(query_side, key_side):
        return back_block(
            query_side[0],
            query_side[1],
            query_side[2],
            query_side[3],
            key_side[0],
            key_side[1],
            key_side[2],
            score_scale,
        )

    own_key_side = (own_keys, own_values, own_bias)

    def query_turn(turn_index, carried):
        grad_keys, grad_values, visit_queries, visit_grad, visit_total, visit_delta, visit_sum = (
            carried
        )
        turn_queries, turn_keys, turn_values = back_visit(
            (visit_queries, visit_grad, visit_total, visit_delta), own_key_side
        )
        moved = (
            shifted(visit_queries.astype(jnp.float32), "seq", 1).astype(visit_queries.dtype),
            shifted(visit_grad.astype(jnp.float32), "seq", 1).astype(visit_grad.dtype),
            shifted(visit_total, "seq", 1),
            shifted(visit_delta, "seq", 1),
            shifted(visit_sum + turn_queries, "seq", 1),
        )
        return (grad_keys + turn_keys, grad_values + turn_values) + moved

    carried = lax.fori_loop(
        0,
        cycle_size - 1,
        query_turn,
        (empty_grad, empty_grad, queries, grad_att, log_total, row_delta, grad_query_pre),
    )
    grad_keys, grad_values, visit_queries, visit_grad, visit_total, visit_delta, visit_sum = carried
    turn_queries, turn_keys, turn_values = back_visit(
        (visit_queries, visit_grad, visit_total, visit_delta), own_key_side
    )
    grad_keys = grad_keys + turn_keys
    grad_values = grad_values + turn_values
    grad_queries = shifted(visit_sum + turn_queries, "seq", 1)
    grad_rows = (
        jnp.stack([grad_queries, grad_keys, grad_values])
        .astype(jnp.bfloat16)
        .transpose(0, 1, 3, 2, 4)
        .reshape(3, row_count, local_width)
    )
    input_part = jnp.einsum("ite,ide->td", grad_rows, w_qkv, preferred_element_type=jnp.float32)
    input_grad = grad_one + lax.psum(input_part, "head")
    prefix_grad = lax.psum(prefix_terms, ("seq", "batch"))
    new_first = BETA_ONE * first_moment + (1.0 - BETA_ONE) * prefix_grad
    new_second = BETA_TWO * second_moment + (1.0 - BETA_TWO) * prefix_grad * prefix_grad
    first_hat = new_first / (1.0 - BETA_ONE**STEP)
    second_hat = new_second / (1.0 - BETA_TWO**STEP)
    new_prefix = prefix - LEARN_RATE * (
        first_hat / (jnp.sqrt(second_hat) + ADAM_EPSILON) + WEIGHT_DECAY * prefix
    )
    layer_out = layer_value.reshape(seqs_dev, shard_len, model_width)
    return (
        layer_out,
        input_grad.reshape(seqs_dev, shard_len, model_width),
        prefix_grad,
        new_prefix,
        new_first,
        new_second,
    )


BF = jnp.bfloat16
F32 = jnp.float32
MESH = pl.DeviceIdType.MESH
AHEAD = 2


def nn(left, right):
    return jnp.dot(left, right, preferred_element_type=F32)


def nt(left, right):
    return lax.dot_general(
        left, right, (((1,), (1,)), ((), ())), preferred_element_type=F32
    )


def remote(src, dst, send, recv, device):
    return pltpu.make_async_remote_copy(
        src, dst, send, recv, device_id=device, device_id_type=MESH
    )


def rows_at(start, size, step=64):
    return pl.ds(pl.multiple_of(start, step), size)


def places():
    z = lax.axis_index("seq")
    h = lax.axis_index("head")
    y = lax.axis_index("batch")
    return z, h, y


def member(h, u):
    chip, core = h // 2, lax.rem(h, 2)
    return 2 * lax.rem(chip + u // 2, 2) + lax.rem(core + u % 2, 2)


def z_peers(z):
    return [z + 1 - 2 * lax.rem(z, 2), 3 - z, lax.rem(z + 2, 4)]


def greet(devices):
    barrier = pltpu.get_barrier_semaphore()
    for device in devices:
        pl.semaphore_signal(barrier, inc=1, device_id=device, device_id_type=MESH)
    pl.semaphore_wait(barrier, len(devices))


def lane_masks():
    lane = lax.broadcasted_iota(jnp.int32, (1, 128), 1)
    inside = [lane < HEAD_DIM, lane >= HEAD_DIM]
    spare = [lane == HEAD_DIM, lane == 0]
    return inside, spare


def layer_kernel(
    tokens,
    cot,
    w_qkv,
    w_out,
    w_in,
    w_down,
    prefix,
    proj_bias,
    ffn_bias,
    gains,
    shifts,
    lengths,
    key_mask,
    lo_all,
    ig_all,
    pre_o,
    tok,
    cotg,
    bias_s,
    bias_g,
    wq,
    wo,
    wi,
    wd,
    fb,
    q_s,
    k_s,
    v_s,
    kx,
    vtx,
    pt,
    att_loc,
    att_all,
    rl_s,
    normed_s,
    xhat_s,
    nb_s,
    acc,
    act,
    gp,
    lo_s,
    da_s,
    da_all,
    ds_pre,
    dox,
    dq_s,
    core_out,
    core_in,
    x_out,
    x_in,
    fin,
    pre_part,
    pre_land,
    pre_sum,
    loc_sem,
    out_sem,
    tok_sem,
    cot_sem,
    bias_sem,
    fb_sem,
    att_sem,
    core_sem,
    x_sem,
    y_sem,
    c1_sem,
    c2_sem,
    lower_sem,
    lo_sem,
    lox_sem,
    loc_lo_sem,
    lox_core_sem,
    da_sem,
    part_core_sem,
    part_x_sem,
    igz_sem,
    igx_sem,
    igc_sem,
    igcx_sem,
    pre_sem,
    pre2_sem,
):
    z, h, y = places()
    core = lax.rem(h, 2)
    hc, hx, hd_ = member(h, 1), member(h, 2), member(h, 3)
    dev_core, dev_x, dev_diag, dev_y = (z, hc, y), (z, hx, y), (z, hd_, y), (z, h, 1 - y)
    zs = z_peers(z)
    width = tok.shape[1]
    piece = width // 4
    slots = prefix.shape[1]
    total = 4 * width
    group = 2 * z + y
    others = [lax.rem(group + d, 8) for d in range(1, 8)]
    greet([dev_core, dev_x, dev_diag] + [(g // 2, h, lax.rem(g, 2)) for g in others])

    half = width // 2
    my_half = rows_at(core * half, half)
    tok_copies, tok_forwards = [], []
    for k, zp in enumerate(zs):
        tok_copies.append(
            remote(tokens.at[zp, my_half], tok.at[z, my_half], tok_sem.at[0, k], tok_sem.at[1, k], (zp, h, y))
        )
        tok_forwards.append(
            remote(tok.at[zp, my_half], tok.at[zp, my_half], tok_sem.at[2, k], tok_sem.at[3, k], dev_core)
        )
    for copy in tok_copies:
        copy.start()
    tok_own = pltpu.make_async_copy(tokens.at[z], tok.at[z], loc_sem.at[0])
    tok_own.start()
    wq_own = pltpu.make_async_copy(w_qkv, wq, loc_sem.at[1])
    wq_own.start()

    chunks = [(w_out, wo, w_out.shape[0] // 2, 0, w_out.shape[0] // 2)]
    deep = w_in.shape[0] // 2
    for i in range(4):
        chunks.append((w_in, wi, deep, i * (deep // 4), deep // 4))
    deep = w_down.shape[0] // 4
    for i in range(2):
        chunks.append((w_down, wd, deep, i * (deep // 2), deep // 2))
    over_x, over_y, core_x, core_y = [], [], [], []
    for i, (src, dst, deep, offset, size) in enumerate(chunks):
        mine = rows_at(y * deep + offset, size, 128)
        other = rows_at((1 - y) * deep + offset, size, 128)
        over_x.append(remote(src.at[mine], dst.at[h, mine], x_sem.at[0, i], x_sem.at[1, i], dev_x))
        over_y.append(remote(dst.at[hx, mine], dst.at[hx, mine], y_sem.at[0, i], y_sem.at[1, i], dev_y))
        core_x.append(remote(dst.at[hx, mine], dst.at[hx, mine], c1_sem.at[0, i], c1_sem.at[1, i], dev_core))
        core_y.append(remote(dst.at[hx, other], dst.at[hx, other], c2_sem.at[0, i], c2_sem.at[1, i], dev_core))
    n_chunks = len(chunks)
    base, size = w_down.shape[0] // 2, w_down.shape[0] // 8
    lower = rows_at(base + z * size, size, 128)
    lower_x = remote(w_down.at[lower], wd.at[h, lower], x_sem.at[0, 7], x_sem.at[1, 7], dev_x)
    lower_core = [remote(wd.at[hx, lower], wd.at[hx, lower], c1_sem.at[0, 7], c1_sem.at[1, 7], dev_core)]
    lower_z = []
    for k, zp in enumerate(zs):
        theirs = rows_at(base + zp * size, size, 128)
        lower_z.append(
            remote(wd.at[hx, lower], wd.at[hx, lower], lower_sem.at[0, k], lower_sem.at[1, k], (zp, h, y))
        )
        lower_core.append(
            remote(wd.at[hx, theirs], wd.at[hx, theirs], lower_sem.at[2, k], lower_sem.at[3, k], dev_core)
        )
    x_queue = [over_x[0], lower_x] + over_x[1:]
    for copy in x_queue[:AHEAD]:
        copy.start()

    def serve_x(place):
        x_queue[place].wait_recv()
        if place == 1:
            lower_core[0].start()
        else:
            i = place - 1 if place else 0
            over_y[i].start()
            core_x[i].start()
        if place + AHEAD < len(x_queue):
            x_queue[place + AHEAD].start()

    def serve_y(i):
        over_y[i].wait_recv()
        core_y[i].start()

    own_weights, core_weights = [], []
    for i, (src, dst) in enumerate(((w_out, wo), (w_in, wi), (w_down, wd))):
        own_weights.append(pltpu.make_async_copy(src, dst.at[h], loc_sem.at[2 + i]))
        core_weights.append(remote(src, dst.at[h], core_sem.at[0, i], core_sem.at[1, i], dev_core))

    spot = lax.broadcasted_iota(jnp.int32, (8, width), 1) + z * width
    for s in range(4):
        live = (jnp.broadcast_to(key_mask[s : s + 1, :], (8, width)) == 1) & (spot < lengths[s])
        bias_s[s] = jnp.where(live, 0.0, NEG_FILL)
    bias_g[z] = bias_s[z]
    bias_copies = [
        remote(bias_s.at[zp], bias_g.at[z], bias_sem.at[0, k], bias_sem.at[1, k], (zp, h, y))
        for k, zp in enumerate(zs)
    ]
    fb[h] = jnp.broadcast_to(ffn_bias[...], fb.shape[1:])
    fb_copies = [
        remote(fb.at[h], fb.at[h], fb_sem.at[0, k], fb_sem.at[1, k], device)
        for k, device in enumerate((dev_core, dev_x, dev_diag))
    ]
    for copy in bias_copies + fb_copies:
        copy.start()
    for copy in own_weights + core_weights:
        copy.start()

    my_piece = rows_at(h * piece, piece)
    cot_copies = [
        remote(cot.at[zp, my_piece], cotg.at[z], cot_sem.at[0, k], cot_sem.at[1, k], (zp, h, y))
        for k, zp in enumerate(zs)
    ]
    cot_own = pltpu.make_async_copy(cot.at[z, my_piece], cotg.at[z], loc_sem.at[5])
    cot_own.start()

    inside, spare = lane_masks()

    pk = prefix[0].astype(BF)
    pv = prefix[1].astype(BF)
    k_s[total : total + slots, :] = pk
    v_s[total : total + slots, :] = pv
    for head in range(4):
        pair, par = head // 2, head % 2
        part = pk[:, 128 * pair : 128 * pair + 128].astype(F32)
        kx[head, total : total + slots, :] = jnp.where(inside[par], part, 0.0).astype(BF)
        vtx[head, HEAD_DIM:, :] = jnp.ones((vtx.shape[1] - HEAD_DIM, vtx.shape[2]), BF)

    def project(block):
        rows = tok[block]
        for i, target in enumerate((q_s, k_s, v_s)):
            value = (nn(rows, wq[i]) + proj_bias[i : i + 1, :]).astype(BF)
            if i == 0:
                value = (value.astype(F32) * HEAD_DIM**-0.5).astype(BF)
            for j in range(4):
                target[rows_at(j * width + block * piece, piece), :] = value[piece * j : piece * j + piece]
            if i == 1:
                column = jnp.broadcast_to(bias_g[block][0:1, :], (128, width)).T
                for head in range(4):
                    pair, par = head // 2, head % 2
                    part = value[:, 128 * pair : 128 * pair + 128].astype(F32)
                    ext = jnp.where(inside[par], part, jnp.where(spare[par], column, 0.0)).astype(BF)
                    for j in range(4):
                        kx[head, rows_at(j * width + block * piece, piece), :] = ext[piece * j : piece * j + piece]

    tok_own.wait()
    wq_own.wait()
    project(z)
    serve_x(0)
    for k, zp in enumerate(zs):
        serve_x(k + 1)
        if k != 1:
            serve_y(k // 2)
        tok_copies[k].wait_recv()
        tok_forwards[k].start()
        bias_copies[k].wait_recv()
        if k == 2:
            for copy in lower_z + cot_copies:
                copy.start()
        tok_forwards[k].wait_recv()
        project(zp)

    for i in range(4):
        flipped = v_s[i * width : (i + 1) * width, :].astype(F32).T.astype(BF)
        for head in range(4):
            vtx[head, 0:HEAD_DIM, i * width : (i + 1) * width] = flipped[HEAD_DIM * head : HEAD_DIM * (head + 1)]
    flipped = v_s[total : total + slots, :].astype(F32).T.astype(BF)
    for head in range(4):
        vtx[head, 0:HEAD_DIM, total : total + slots] = flipped[HEAD_DIM * head : HEAD_DIM * (head + 1)]

    def att_copy(u):
        j = member(h, u)
        return remote(att_loc.at[j], att_all.at[h], att_sem.at[0, u], att_sem.at[1, u], (z, j, y))

    def attend(step):
        u = 3 - step
        j = member(h, u)
        outs, recips = [], []
        for head in range(4):
            pair, par = head // 2, head % 2
            part = q_s[rows_at(j * width, width, width), 128 * pair : 128 * pair + 128].astype(F32)
            ext = jnp.where(inside[par], part, jnp.where(spare[par], 1.0, 0.0)).astype(BF)
            scores = nt(kx[head], ext)
            top = jnp.max(scores, axis=0, keepdims=True)
            weight = jnp.exp(scores - top).astype(BF)
            pt[head, j] = weight
            summed = nn(vtx[head], weight)
            recip = 1.0 / summed[HEAD_DIM : HEAD_DIM + 1]
            outs.append(summed[0:HEAD_DIM] * recip)
            recips.append(jnp.broadcast_to(recip, (32, width)))
        att_loc[j] = jnp.concatenate(outs, axis=0).T.astype(BF)
        rl_s[j] = jnp.concatenate(recips, axis=0).T

        @pl.when(u > 0)
        def _():
            att_copy(u).start()

        @pl.when(u == 0)
        def _():
            att_all[h] = att_loc[h]

    pl.loop(0, 2)(attend)
    serve_x(4)
    serve_y(2)
    pl.loop(2, 4)(attend)
    serve_x(5)
    serve_y(3)
    att_copies = [att_copy(u) for u in (1, 2, 3)]

    lane = lax.broadcasted_iota(jnp.int32, (1, 128), 1)
    spare_lo = [lane == HEAD_DIM + 1, lane == 1]
    for head in range(4):
        pair, par = head // 2, head % 2
        part = v_s[:, 128 * pair : 128 * pair + 128].astype(F32)
        ones = jnp.where(spare[par] | spare_lo[par], 1.0, 0.0)
        kx[head] = jnp.where(inside[par], part, ones).astype(BF)
    for i in range(5):
        low, size = i * width, width if i < 4 else slots
        flipped = k_s[low : low + size, :].astype(F32).T.astype(BF)
        for head in range(4):
            vtx[head, 0:HEAD_DIM, low : low + size] = flipped[HEAD_DIM * head : HEAD_DIM * (head + 1)]

    own_weights[0].wait()
    core_weights[0].wait_recv()
    core_x[0].wait_recv()
    core_y[0].wait_recv()
    for copy in att_copies:
        copy.wait_recv()
    attention = nn(att_all[0], wo[0])
    for j in range(1, 4):
        attention += nn(att_all[j], wo[j])
    mine = jnp.concatenate([tok[b, my_piece, :] for b in range(4)], axis=0).astype(F32)
    resid = mine + attention + shifts[0:1, :]
    centred = resid - jnp.mean(resid, axis=-1, keepdims=True)
    inverse_one = lax.rsqrt(jnp.mean(centred * centred, axis=-1, keepdims=True) + NORM_EPSILON)
    xhat = centred * inverse_one
    xhat_s[...] = xhat
    normed = xhat * gains[0:1, :] + shifts[1:2, :]
    normed_s[...] = normed
    nb_s[...] = normed.astype(BF)

    tile = 256
    tiles = wi.shape[2] // tile

    def ffn_in(quarter):
        @pl.loop(0, tiles, unroll=4)
        def _(n):
            cols = rows_at(n * tile, tile, tile)
            inner = nn(nb_s[...], wi[quarter, :, cols]) + fb[quarter, 0:1, cols]
            cdf = 0.5 * (1.0 + lax.erf(inner * 0.7071067811865476))
            act[quarter, :, cols] = (inner * cdf).astype(BF)
            gp[quarter, :, cols] = cdf + inner * (jnp.exp(-0.5 * inner * inner) * 0.3989422804014327)

    for copy in fb_copies:
        copy.wait_recv()
    own_weights[1].wait()
    core_weights[1].wait_recv()
    ffn_in(h)
    ffn_in(hc)
    serve_x(6)
    serve_y(4)
    for i in range(1, 5):
        core_x[i].wait_recv()
        core_y[i].wait_recv()
    ffn_in(hx)
    ffn_in(hd_)

    acc[...] = jnp.zeros(acc.shape, F32)

    def ffn_out(quarter, start, deep):
        span = rows_at(start, deep, deep)

        @pl.loop(0, tiles, unroll=4)
        def _(n):
            cols = rows_at(n * tile, tile, tile)
            acc[:, cols] += nn(act[quarter, :, span], wd[quarter, span, cols])

    own_weights[2].wait()
    core_weights[2].wait_recv()
    deep = wd.shape[1]
    for k in range(3):
        lower_z[k].wait_recv()
        lower_core[k + 1].start()
    ffn_out(h, 0, deep)
    serve_x(7)
    serve_y(5)
    ffn_out(hc, 0, deep)
    ffn_out(hx, base, deep // 2)
    for copy in lower_core:
        copy.wait_recv()
    ffn_out(hd_, base, deep // 2)
    for i in (5, 6):
        core_x[i].wait_recv()
    ffn_out(hx, y * (deep // 4), deep // 4)
    ffn_out(hd_, y * (deep // 4), deep // 4)
    serve_y(6)
    ffn_out(hx, (1 - y) * (deep // 4), deep // 4)
    for i in (5, 6):
        core_y[i].wait_recv()
    ffn_out(hd_, (1 - y) * (deep // 4), deep // 4)

    resid = normed_s[...] + acc[...] + shifts[2:3, :]
    centred = resid - jnp.mean(resid, axis=-1, keepdims=True)
    inverse = lax.rsqrt(jnp.mean(centred * centred, axis=-1, keepdims=True) + NORM_EPSILON)
    xhat = centred * inverse
    lo_s[...] = (xhat * gains[1:2, :] + shifts[3:4, :]).astype(BF)
    x_piece = rows_at(hx * piece, piece)
    lo_z, lo_x, lo_core, lo_across = [], [], [], []
    blocks = zs + [z]
    for k, b in enumerate(blocks):
        rows = rows_at(b * piece, piece)
        source = lo_all.at[b, my_piece]
        if k < 3:
            lo_z.append(remote(lo_s.at[rows], lo_all.at[z, my_piece], lo_sem.at[0, k], lo_sem.at[1, k], (b, h, y)))
        else:
            source = lo_s.at[rows]
        lo_x.append(remote(source, lo_all.at[b, my_piece], lox_sem.at[0, k], lox_sem.at[1, k], dev_x))
        lo_core.append(remote(source, lo_all.at[b, my_piece], loc_lo_sem.at[0, k], loc_lo_sem.at[1, k], dev_core))
        lo_across.append(
            remote(lo_all.at[b, x_piece], lo_all.at[b, x_piece], lox_core_sem.at[0, k], lox_core_sem.at[1, k], dev_core)
        )
    lo_own = pltpu.make_async_copy(lo_s.at[rows_at(z * piece, piece)], lo_all.at[z, my_piece], out_sem.at[0])
    for copy in lo_z + [lo_x[3], lo_core[3], lo_own]:
        copy.start()

    def serve_lo(k):
        lo_z[k].wait_recv()
        lo_x[k].start()
        lo_core[k].start()

    cot_own.wait()
    for copy in cot_copies:
        copy.wait_recv()
    dy = jnp.concatenate([cotg[b] for b in range(4)], axis=0).astype(F32) * gains[1:2, :]
    g_two = inverse * (
        dy - jnp.mean(dy, axis=-1, keepdims=True) - xhat * jnp.mean(dy * xhat, axis=-1, keepdims=True)
    )
    acc[...] = g_two
    nb_s[...] = g_two.astype(BF)

    @pl.loop(0, 4)
    def _(quarter):
        @pl.loop(0, tiles, unroll=4)
        def _(n):
            cols = rows_at(n * tile, tile, tile)
            d_act = nt(nb_s[...], wd[quarter, cols, :])
            act[quarter, :, cols] = (d_act * gp[quarter, :, cols]).astype(BF)

    @pl.loop(0, 4)
    def _(quarter):
        @pl.loop(0, tiles, unroll=4)
        def _(n):
            cols = rows_at(n * tile, tile, tile)
            acc[:, cols] += nt(act[quarter], wi[quarter, cols, :])

    dy = acc[...] * gains[0:1, :]
    xhat = xhat_s[...]
    g_one = inverse_one * (
        dy - jnp.mean(dy, axis=-1, keepdims=True) - xhat * jnp.mean(dy * xhat, axis=-1, keepdims=True)
    )
    acc[...] = g_one
    low = g_one.astype(BF)
    da_copies = {}
    for u in (2, 3, 1):
        j = member(h, u)
        da_s[j] = nt(low, wo[j]).astype(BF)
        da_copies[u] = remote(da_s.at[j], da_all.at[h], da_sem.at[0, u], da_sem.at[1, u], (z, j, y))
        da_copies[u].start()
    da_all[h] = nt(low, wo[h]).astype(BF)
    for copy in over_y + core_x + core_y + lower_z + lower_core:
        copy.wait_send()

    def score_grads(u):
        j = member(h, u)

        @pl.when(u > 0)
        def _():
            remote(da_s.at[j], da_all.at[h], da_sem.at[0, u], da_sem.at[1, u], (z, j, y)).wait_recv()

        grads = []
        for head in range(4):
            pair, par = head // 2, head % 2
            lanes = slice(128 * pair, 128 * pair + 128)
            d_out = da_all[j, :, lanes].astype(F32)
            recip = rl_s[j, :, 32 * head : 32 * head + 1]
            delta = recip * jnp.sum(
                jnp.where(inside[par], d_out * att_loc[j, :, lanes].astype(F32), 0.0), axis=-1, keepdims=True
            )
            high = delta.astype(BF).astype(F32)
            ext = jnp.where(spare[par], -high, jnp.where(spare_lo[par], high - delta, 0.0))
            ext = jnp.where(inside[par], d_out * recip, ext).astype(BF)
            dox[head, j] = ext
            d_probs = nt(kx[head], ext).astype(BF)
            d_scores = pt[head, j] * d_probs
            wi[head, :, rows_at(j * width, width, width)] = d_scores[0:total]
            ds_pre[head, j] = d_scores[total:]
            grads.append(nn(vtx[head, 0:HEAD_DIM, :], d_scores))
        dq_s[j] = (jnp.concatenate(grads, axis=0).T * HEAD_DIM**-0.5).astype(BF)

    pl.loop(0, 2)(score_grads)
    serve_lo(0)
    serve_lo(1)
    serve_lo(2)
    pl.loop(2, 4)(score_grads)

    def key_side(left, right):
        halves = []
        for pair in range(2):
            sides = []
            for par in range(2):
                head = 2 * pair + par
                value = nn(left(head, 0), right(head, 0, pair))
                for j in range(1, 4):
                    value += nn(left(head, j), right(head, j, pair))
                sides.append(value)
            halves.append(jnp.where(inside[0], sides[0], sides[1]))
        return jnp.concatenate(halves, axis=-1)

    def d_values(rows):
        return key_side(lambda head, j: pt[head, j, rows, :], lambda head, j, pair: dox[head, j])

    def d_keys(left):
        return key_side(left, lambda head, j, pair: q_s[j * width : (j + 1) * width, 128 * pair : 128 * pair + 128])

    def partial(i):
        rows = rows_at(i * width, width, width)
        dk = d_keys(lambda head, j: wi[head, rows, j * width : (j + 1) * width]).astype(BF)
        dv = d_values(rows).astype(BF)
        return nt(dq_s[i], wq[0]) + nt(dk, wq[1]) + nt(dv, wq[2])

    part_core = [
        remote(core_out.at[i], core_in.at[i], part_core_sem.at[0, i], part_core_sem.at[1, i], dev_core) for i in range(2)
    ]
    part_x = []
    for k, b in enumerate(blocks):
        rows = rows_at(b * piece, piece)
        part_x.append(remote(x_out.at[rows], x_in.at[rows], part_x_sem.at[0, k], part_x_sem.at[1, k], dev_x))

    core_out[0] = partial(hd_).astype(BF)
    part_core[0].start()
    mine = partial(hx)
    part_core[0].wait_recv()
    x_out[...] = (mine + core_in[0].astype(F32)).astype(BF)
    for copy in part_x:
        copy.start()

    pre_part[0] = d_keys(lambda head, j: ds_pre[head, j])
    pre_part[1] = d_values(pl.ds(total, slots))
    few = slots // 8
    mine_rows = rows_at(group * few, few, few)
    pre_copies, pre_back = [], []
    for d, g in enumerate(others):
        device = (g // 2, h, lax.rem(g, 2))
        pre_copies.append(
            remote(pre_part.at[:, rows_at(g * few, few, few)], pre_land.at[d], pre_sem.at[0, d], pre_sem.at[1, d], device)
        )
        pre_back.append(
            remote(pre_sum.at[:, mine_rows], pre_sum.at[:, mine_rows], pre2_sem.at[0, d], pre2_sem.at[1, d], device)
        )
    for copy in pre_copies:
        copy.start()
    for k in (3, 0, 1, 2):
        lo_x[k].wait_recv()
        lo_across[k].start()

    core_out[1] = partial(hc).astype(BF)
    part_core[1].start()
    acc[...] += partial(h)
    part_core[1].wait_recv()
    acc[...] += core_in[1].astype(F32)

    igz, igx, igc, igcx = [], [], [], []
    for k, b in enumerate(blocks):
        rows = rows_at(b * piece, piece)
        source = ig_all.at[b, my_piece]
        if k < 3:
            igz.append(remote(fin.at[rows], ig_all.at[z, my_piece], igz_sem.at[0, k], igz_sem.at[1, k], (b, h, y)))
        else:
            source = fin.at[rows]
        igx.append(remote(source, ig_all.at[b, my_piece], igx_sem.at[0, k], igx_sem.at[1, k], dev_x))
        igc.append(remote(source, ig_all.at[b, my_piece], igc_sem.at[0, k], igc_sem.at[1, k], dev_core))
        igcx.append(
            remote(ig_all.at[b, x_piece], ig_all.at[b, x_piece], igcx_sem.at[0, k], igcx_sem.at[1, k], dev_core)
        )
    ig_own = pltpu.make_async_copy(fin.at[rows_at(z * piece, piece)], ig_all.at[z, my_piece], out_sem.at[1])
    for k, b in enumerate(blocks):
        rows = rows_at(b * piece, piece)
        part_x[k].wait_recv()
        fin[rows, :] = (acc[rows, :] + x_in[rows, :].astype(F32)).astype(BF)
        if k < 3:
            igz[k].start()
        else:
            ig_own.start()
            igx[3].start()
            igc[3].start()
        if k == 1:
            for copy in pre_copies:
                copy.wait_recv()
            for i in range(2):
                term = pre_part[i, mine_rows, :]
                for d in range(7):
                    term += pre_land[d, i]
                pre_sum[i, mine_rows, :] = term
            for copy in pre_back:
                copy.start()
    for copy in lo_core + lo_across:
        copy.wait_recv()
    lo_own.wait()
    for k in range(3):
        igz[k].wait_recv()
        igx[k].start()
        igc[k].start()
    for copy in pre_back:
        copy.wait_recv()
    pre_o[...] = pre_sum[...]
    for k in (3, 0, 1, 2):
        igx[k].wait_recv()
        igcx[k].start()
    for copy in igc + igcx:
        copy.wait_recv()
    ig_own.wait()
    sent = tok_copies + tok_forwards + x_queue + core_weights + bias_copies + fb_copies + cot_copies + att_copies
    sent += lo_z + lo_x + lo_core + lo_across + list(da_copies.values()) + part_core + part_x
    for copy in sent + igz + igx + igc + igcx + pre_copies + pre_back:
        copy.wait_send()


def layer(tokens, cot, w_qkv, w_out, w_in, w_down, prefix, proj_bias, ffn_bias, gains, shifts, lengths, key_mask):
    seqs, width, model = tokens.shape
    local = w_qkv.shape[2]
    hidden = w_in.shape[1]
    slots = prefix.shape[1]
    total = seqs * width
    keys = total + slots
    dma = pltpu.SemaphoreType.DMA
    hbm = pl.BlockSpec(memory_space=pl.ANY)
    vmem = pl.BlockSpec(memory_space=pltpu.VMEM)
    shape = jax.ShapeDtypeStruct
    return pl.pallas_call(
        layer_kernel,
        name="layer",
        out_shape=(
            pltpu.VMEM((4, width, model), BF),
            pltpu.VMEM((4, width, model), BF),
            shape((2, slots, local), F32),
        ),
        in_specs=[hbm] * 6 + [vmem] * 5 + [pl.BlockSpec(memory_space=pltpu.SMEM), vmem],
        out_specs=(vmem, vmem, vmem),
        scratch_shapes=[
            pltpu.VMEM((4, width, model), BF),
            pltpu.VMEM((4, width // 4, model), BF),
            pltpu.VMEM((4, 8, width), F32),
            pltpu.VMEM((4, 8, width), F32),
            pltpu.VMEM((3, model, local), BF),
            pltpu.VMEM((4, local, model), BF),
            pltpu.VMEM((4, model, hidden), BF),
            pltpu.VMEM((4, hidden, model), BF),
            pltpu.VMEM((4, 8, hidden), F32),
            pltpu.VMEM((total, local), BF),
            pltpu.VMEM((keys, local), BF),
            pltpu.VMEM((keys, local), BF),
            pltpu.VMEM((4, keys, 128), BF),
            pltpu.VMEM((4, HEAD_DIM + 16, keys), BF),
            pltpu.VMEM((4, 4, keys, width), BF),
            pltpu.VMEM((4, width, local), BF),
            pltpu.VMEM((4, width, local), BF),
            pltpu.VMEM((4, width, 128), F32),
            pltpu.VMEM((width, model), F32),
            pltpu.VMEM((width, model), F32),
            pltpu.VMEM((width, model), BF),
            pltpu.VMEM((width, model), F32),
            pltpu.VMEM((4, width, hidden), BF),
            pltpu.VMEM((4, width, hidden), F32),
            pltpu.VMEM((width, model), BF),
            pltpu.VMEM((4, width, local), BF),
            pltpu.VMEM((4, width, local), BF),
            pltpu.VMEM((4, 4, slots, width), BF),
            pltpu.VMEM((4, 4, width, 128), BF),
            pltpu.VMEM((4, width, local), BF),
            pltpu.VMEM((2, width, model), BF),
            pltpu.VMEM((2, width, model), BF),
            pltpu.VMEM((width, model), BF),
            pltpu.VMEM((width, model), BF),
            pltpu.VMEM((width, model), BF),
            pltpu.VMEM((2, slots, local), F32),
            pltpu.VMEM((7, 2, slots // 8, local), F32),
            pltpu.VMEM((2, slots, local), F32),
            dma((6,)),
            dma((4,)),
            dma((4, 3)),
            dma((2, 3)),
            dma((2, 3)),
            dma((2, 3)),
            dma((2, 4)),
            dma((2, 3)),
            dma((2, 9)),
            dma((2, 9)),
            dma((2, 9)),
            dma((2, 9)),
            dma((4, 3)),
            dma((2, 3)),
            dma((2, 4)),
            dma((2, 4)),
            dma((2, 4)),
            dma((2, 4)),
            dma((2, 2)),
            dma((2, 4)),
            dma((2, 3)),
            dma((2, 4)),
            dma((2, 4)),
            dma((2, 4)),
            dma((2, 7)),
            dma((2, 7)),
        ],
        compiler_params=pltpu.CompilerParams(
            collective_id=0, has_side_effects=True, vmem_limit_bytes=58 * 2**20
        ),
        cost_estimate=pl.CostEstimate(flops=15 * 10**9, bytes_accessed=40 * 2**20, transcendentals=6 * 10**6),
    )(tokens, cot, w_qkv, w_out, w_in, w_down, prefix, proj_bias, ffn_bias, gains, shifts, lengths, key_mask)


def finish_kernel(lo, ig, grad, prefix, first, second, lo_o, ig_o, grad_o, new_o, first_o, second_o, lo_f, ig_f, sem):
    seqs = lo.shape[0]
    copies = []
    for i in range(seqs):
        for k, (src, mid, dst) in enumerate(((lo, lo_f, lo_o), (ig, ig_f, ig_o))):
            mid[i] = src[i].astype(F32)
            copy = pltpu.make_async_copy(mid.at[i], dst.at[i], sem.at[k, i])
            copy.start()
            copies.append(copy)
    slope = grad[...]
    grad_o[...] = slope
    new_first = BETA_ONE * first[...] + (1.0 - BETA_ONE) * slope
    new_second = BETA_TWO * second[...] + (1.0 - BETA_TWO) * slope * slope
    first_hat = new_first / (1.0 - BETA_ONE**STEP)
    second_hat = new_second / (1.0 - BETA_TWO**STEP)
    value = prefix[...]
    new_o[...] = value - LEARN_RATE * (first_hat / (jnp.sqrt(second_hat) + ADAM_EPSILON) + WEIGHT_DECAY * value)
    first_o[...] = new_first
    second_o[...] = new_second
    for copy in copies:
        copy.wait()


def finish(lo, ig, grad, prefix, first, second):
    hbm = pl.BlockSpec(memory_space=pl.ANY)
    vmem = pl.BlockSpec(memory_space=pltpu.VMEM)
    shape = jax.ShapeDtypeStruct
    whole, little = shape(lo.shape, F32), shape(prefix.shape, F32)
    return pl.pallas_call(
        finish_kernel,
        name="finish",
        out_shape=(whole, whole, little, little, little, little),
        in_specs=[vmem] * 6,
        out_specs=(hbm, hbm, vmem, vmem, vmem, vmem),
        scratch_shapes=[
            pltpu.VMEM(lo.shape, F32),
            pltpu.VMEM(lo.shape, F32),
            pltpu.SemaphoreType.DMA((2, lo.shape[0])),
        ],
        compiler_params=pltpu.CompilerParams(vmem_limit_bytes=40 * 2**20),
    )(lo, ig, grad, prefix, first, second)


def body(*args):
    (tokens, cotangent, prefix, first_moment, second_moment, w_qkv, proj_bias, w_out, w_in, ffn_bias) = args[:10]
    w_down, gains, shifts, lengths, key_mask = args[10:]
    fits = (
        lax.axis_size("seq") == 4
        and lax.axis_size("head") == 4
        and lax.axis_size("batch") == 2
        and tokens.shape == (4, 256, 1024)
        and w_qkv.shape == (3, 1024, 256)
        and w_in.shape == (1024, 1024)
        and prefix.shape[1] == 64
    )
    if not fits:
        return general_body(*args)
    layer_out, input_grad, prefix_grad = layer(
        tokens, cotangent, w_qkv, w_out, w_in, w_down, prefix, proj_bias, ffn_bias.reshape(1, -1), gains, shifts,
        lengths, key_mask,
    )
    layer_out, input_grad, prefix_grad, new_prefix, new_first, new_second = finish(
        layer_out, input_grad, prefix_grad, prefix, first_moment, second_moment
    )
    return layer_out, input_grad, prefix_grad, new_prefix, new_first, new_second


def solution(mesh):
    placed = (
        P("batch", "seq", None),
        P("batch", "seq", None),
        P(None, None, "head"),
        P(None, None, "head"),
        P(None, None, "head"),
        P(None, None, "head"),
        P(None, "head"),
        P("head", None),
        P(None, "head"),
        P("head"),
        P("head", None),
        P(),
        P(),
        P("batch"),
        P("batch", "seq"),
    )
    return jax.shard_map(
        body,
        mesh=mesh,
        in_specs=placed,
        out_specs=(
            P("batch", "seq", None),
            P("batch", "seq", None),
            P(None, None, "head"),
            P(None, None, "head"),
            P(None, None, "head"),
            P(None, None, "head"),
        ),
        check_vma=False,
    )
```

```python
import jax
import jax.numpy as jnp
from jax import lax
from jax.experimental import pallas as pl
from jax.experimental.pallas import tpu as pltpu
from jax.sharding import PartitionSpec as P

HEAD_DIM = 64
STEP = 10


NEG_FILL = -1e30
NORM_EPSILON = 1e-05
BETA_ONE = 0.9
BETA_TWO = 0.95
LEARN_RATE = 0.8
WEIGHT_DECAY = 0.01
ADAM_EPSILON = 1e-08


def shifted(value, axis, steps):
    count = lax.axis_size(axis)
    pairs = [(source, (source + steps) % count) for source in range(count)]
    return lax.ppermute(value, axis, pairs)


def layer_norm(values_in, gain_row, shift_row):
    row_mean = jnp.mean(values_in, axis=-1, keepdims=True)
    centred = values_in - row_mean
    spread = jnp.mean(centred * centred, axis=-1, keepdims=True)
    return centred * lax.rsqrt(spread + NORM_EPSILON) * gain_row + shift_row


def exact_gelu(values_in):
    return jax.nn.gelu(values_in, approximate=False)


def block_scores(queries, block_keys, block_bias, score_scale):
    scores = (
        jnp.einsum("shqd,shkd->shqk", queries, block_keys, preferred_element_type=jnp.float32)
        * score_scale
    )
    return scores + block_bias.astype(jnp.float32)[:, None, None, :]


def absorb(softmax_state, queries, block_keys, block_values, block_bias, score_scale):
    row_max, row_sum, weighted = softmax_state
    scores = block_scores(queries, block_keys, block_bias, score_scale)
    new_max = jnp.maximum(row_max, jnp.max(scores, axis=-1))
    fade_factor = jnp.exp(row_max - new_max)
    exp_scores = jnp.exp(scores - new_max[..., None])
    row_sum = row_sum * fade_factor + jnp.sum(exp_scores, axis=-1)
    weighted = weighted * fade_factor[..., None] + jnp.einsum(
        "shqk,shkd->shqd",
        exp_scores.astype(jnp.bfloat16),
        block_values,
        preferred_element_type=jnp.float32,
    )
    return (new_max, row_sum, weighted)


def back_block(
    queries, grad_att, log_total, row_delta, block_keys, block_values, block_bias, score_scale
):
    scores = block_scores(queries, block_keys, block_bias, score_scale)
    probabilities = jnp.exp(scores - log_total[..., None])
    grad_probs = jnp.einsum(
        "shqd,shkd->shqk", grad_att, block_values, preferred_element_type=jnp.float32
    )
    grad_scores = (probabilities * (grad_probs - row_delta[..., None])).astype(jnp.bfloat16)
    grad_queries = (
        jnp.einsum("shqk,shkd->shqd", grad_scores, block_keys, preferred_element_type=jnp.float32)
        * score_scale
    )
    grad_keys = (
        jnp.einsum("shqk,shqd->shkd", grad_scores, queries, preferred_element_type=jnp.float32)
        * score_scale
    )
    grad_values = jnp.einsum(
        "shqk,shqd->shkd",
        probabilities.astype(jnp.bfloat16),
        grad_att,
        preferred_element_type=jnp.float32,
    )
    return (grad_queries, grad_keys, grad_values)


def general_body(
    tokens,
    cotangent,
    prefix,
    first_moment,
    second_moment,
    w_qkv,
    proj_bias,
    w_out,
    w_in,
    ffn_bias,
    w_down,
    gains,
    shifts,
    lengths,
    key_mask,
):
    seqs_dev, shard_len, model_width = tokens.shape
    row_count = seqs_dev * shard_len
    local_width = w_qkv.shape[2]
    heads_dev = local_width // HEAD_DIM
    prefix_slots = prefix.shape[1]
    score_scale = HEAD_DIM ** (-0.5)
    cycle_size = lax.axis_size("seq")
    cycle_place = lax.axis_index("seq")
    flat_tokens = tokens.reshape(row_count, model_width)
    projected = (
        jnp.einsum("td,ide->ite", flat_tokens, w_qkv, preferred_element_type=jnp.float32)
        + proj_bias[:, None, :]
    )
    by_head = (
        projected.astype(jnp.bfloat16)
        .reshape(3, seqs_dev, shard_len, heads_dev, HEAD_DIM)
        .transpose(0, 1, 3, 2, 4)
    )
    queries = by_head[0]
    own_keys = by_head[1]
    own_values = by_head[2]
    positions = cycle_place * shard_len + lax.broadcasted_iota(jnp.int32, (seqs_dev, shard_len), 1)
    live_keys = (key_mask == 1) & (positions < lengths[:, None])
    own_bias = jnp.where(live_keys, 0.0, NEG_FILL).astype(jnp.bfloat16)
    prefix_low = (
        prefix.astype(jnp.bfloat16)
        .reshape(2, prefix_slots, heads_dev, HEAD_DIM)
        .transpose(0, 2, 1, 3)
    )
    pre_scores = (
        jnp.einsum("shqd,hpd->shqp", queries, prefix_low[0], preferred_element_type=jnp.float32)
        * score_scale
    )
    row_max = jnp.max(pre_scores, axis=-1)
    exp_prefix = jnp.exp(pre_scores - row_max[..., None])
    row_sum = jnp.sum(exp_prefix, axis=-1)
    weighted = jnp.einsum(
        "shqp,hpd->shqd",
        exp_prefix.astype(jnp.bfloat16),
        prefix_low[1],
        preferred_element_type=jnp.float32,
    )

    def visit_keys(softmax_state, block_keys, block_values, block_bias):
        return absorb(softmax_state, queries, block_keys, block_values, block_bias, score_scale)

    def forward_turn(turn_index, carried):
        softmax_state, block_keys, block_values, block_bias = carried
        softmax_state = visit_keys(softmax_state, block_keys, block_values, block_bias)
        block_keys, block_values, block_bias = shifted(
            (block_keys, block_values, block_bias), "seq", 1
        )
        return (softmax_state, block_keys, block_values, block_bias)

    carried = lax.fori_loop(
        0,
        cycle_size - 1,
        forward_turn,
        ((row_max, row_sum, weighted), own_keys, own_values, own_bias),
    )
    row_max, row_sum, weighted = visit_keys(carried[0], carried[1], carried[2], carried[3])
    log_total = row_max + jnp.log(row_sum)
    attended = weighted / row_sum[..., None]
    merged = attended.astype(jnp.bfloat16).transpose(0, 2, 1, 3).reshape(row_count, local_width)
    attention = (
        lax.psum(jnp.dot(merged, w_out, preferred_element_type=jnp.float32), "head") + shifts[0]
    )
    resid_one = flat_tokens.astype(jnp.float32) + attention
    normed, norm_one_back = jax.vjp(
        lambda values_in: layer_norm(values_in, gains[0], shifts[1]), resid_one
    )
    inner_sum = (
        jnp.dot(normed.astype(jnp.bfloat16), w_in, preferred_element_type=jnp.float32) + ffn_bias
    )
    activated, gelu_back = jax.vjp(exact_gelu, inner_sum)
    feed_forward = (
        lax.psum(
            jnp.dot(activated.astype(jnp.bfloat16), w_down, preferred_element_type=jnp.float32),
            "head",
        )
        + shifts[2]
    )
    layer_value, norm_two_back = jax.vjp(
        lambda values_in: layer_norm(values_in, gains[1], shifts[3]), normed + feed_forward
    )
    contract_last = (((1,), (1,)), ((), ()))
    (grad_two,) = norm_two_back(cotangent.reshape(row_count, model_width).astype(jnp.float32))
    grad_act = lax.dot_general(
        grad_two.astype(jnp.bfloat16), w_down, contract_last, preferred_element_type=jnp.float32
    )
    (grad_inner,) = gelu_back(grad_act)
    hidden_part = lax.dot_general(
        grad_inner.astype(jnp.bfloat16), w_in, contract_last, preferred_element_type=jnp.float32
    )
    grad_normed = grad_two + lax.psum(hidden_part, "head")
    (grad_one,) = norm_one_back(grad_normed)
    grad_merged = lax.dot_general(
        grad_one.astype(jnp.bfloat16), w_out, contract_last, preferred_element_type=jnp.float32
    )
    grad_att = (
        grad_merged.astype(jnp.bfloat16)
        .reshape(seqs_dev, shard_len, heads_dev, HEAD_DIM)
        .transpose(0, 2, 1, 3)
    )
    row_delta = jnp.sum(grad_att.astype(jnp.float32) * attended, axis=-1)
    pre_probs = jnp.exp(pre_scores - log_total[..., None])
    grad_pre_probs = jnp.einsum(
        "shqd,hpd->shqp", grad_att, prefix_low[1], preferred_element_type=jnp.float32
    )
    grad_pre_scores = (pre_probs * (grad_pre_probs - row_delta[..., None])).astype(jnp.bfloat16)
    grad_query_pre = (
        jnp.einsum(
            "shqp,hpd->shqd", grad_pre_scores, prefix_low[0], preferred_element_type=jnp.float32
        )
        * score_scale
    )
    grad_pre_keys = (
        jnp.einsum("shqp,shqd->hpd", grad_pre_scores, queries, preferred_element_type=jnp.float32)
        * score_scale
    )
    grad_pre_values = jnp.einsum(
        "shqp,shqd->hpd",
        pre_probs.astype(jnp.bfloat16),
        grad_att,
        preferred_element_type=jnp.float32,
    )
    prefix_terms = (
        jnp.stack([grad_pre_keys, grad_pre_values])
        .transpose(0, 2, 1, 3)
        .reshape(2, prefix_slots, local_width)
    )
    empty_grad = jnp.zeros(queries.shape, jnp.float32)

    def back_visit(query_side, key_side):
        return back_block(
            query_side[0],
            query_side[1],
            query_side[2],
            query_side[3],
            key_side[0],
            key_side[1],
            key_side[2],
            score_scale,
        )

    own_key_side = (own_keys, own_values, own_bias)

    def query_turn(turn_index, carried):
        grad_keys, grad_values, visit_queries, visit_grad, visit_total, visit_delta, visit_sum = (
            carried
        )
        turn_queries, turn_keys, turn_values = back_visit(
            (visit_queries, visit_grad, visit_total, visit_delta), own_key_side
        )
        moved = (
            shifted(visit_queries.astype(jnp.float32), "seq", 1).astype(visit_queries.dtype),
            shifted(visit_grad.astype(jnp.float32), "seq", 1).astype(visit_grad.dtype),
            shifted(visit_total, "seq", 1),
            shifted(visit_delta, "seq", 1),
            shifted(visit_sum + turn_queries, "seq", 1),
        )
        return (grad_keys + turn_keys, grad_values + turn_values) + moved

    carried = lax.fori_loop(
        0,
        cycle_size - 1,
        query_turn,
        (empty_grad, empty_grad, queries, grad_att, log_total, row_delta, grad_query_pre),
    )
    grad_keys, grad_values, visit_queries, visit_grad, visit_total, visit_delta, visit_sum = carried
    turn_queries, turn_keys, turn_values = back_visit(
        (visit_queries, visit_grad, visit_total, visit_delta), own_key_side
    )
    grad_keys = grad_keys + turn_keys
    grad_values = grad_values + turn_values
    grad_queries = shifted(visit_sum + turn_queries, "seq", 1)
    grad_rows = (
        jnp.stack([grad_queries, grad_keys, grad_values])
        .astype(jnp.bfloat16)
        .transpose(0, 1, 3, 2, 4)
        .reshape(3, row_count, local_width)
    )
    input_part = jnp.einsum("ite,ide->td", grad_rows, w_qkv, preferred_element_type=jnp.float32)
    input_grad = grad_one + lax.psum(input_part, "head")
    prefix_grad = lax.psum(prefix_terms, ("seq", "batch"))
    new_first = BETA_ONE * first_moment + (1.0 - BETA_ONE) * prefix_grad
    new_second = BETA_TWO * second_moment + (1.0 - BETA_TWO) * prefix_grad * prefix_grad
    first_hat = new_first / (1.0 - BETA_ONE**STEP)
    second_hat = new_second / (1.0 - BETA_TWO**STEP)
    new_prefix = prefix - LEARN_RATE * (
        first_hat / (jnp.sqrt(second_hat) + ADAM_EPSILON) + WEIGHT_DECAY * prefix
    )
    layer_out = layer_value.reshape(seqs_dev, shard_len, model_width)
    return (
        layer_out,
        input_grad.reshape(seqs_dev, shard_len, model_width),
        prefix_grad,
        new_prefix,
        new_first,
        new_second,
    )


BF = jnp.bfloat16
F32 = jnp.float32
MESH = pl.DeviceIdType.MESH
AHEAD = 2


def nn(left, right):
    return jnp.dot(left, right, preferred_element_type=F32)


def nt(left, right):
    return lax.dot_general(
        left, right, (((1,), (1,)), ((), ())), preferred_element_type=F32
    )


def remote(src, dst, send, recv, device):
    return pltpu.make_async_remote_copy(
        src, dst, send, recv, device_id=device, device_id_type=MESH
    )


def rows_at(start, size, step=64):
    return pl.ds(pl.multiple_of(start, step), size)


def places():
    z = lax.axis_index("seq")
    h = lax.axis_index("head")
    y = lax.axis_index("batch")
    return z, h, y


def member(h, u):
    chip, core = h // 2, lax.rem(h, 2)
    return 2 * lax.rem(chip + u // 2, 2) + lax.rem(core + u % 2, 2)


def z_peers(z):
    return [z + 1 - 2 * lax.rem(z, 2), 3 - z, lax.rem(z + 2, 4)]


def greet(devices):
    barrier = pltpu.get_barrier_semaphore()
    for device in devices:
        pl.semaphore_signal(barrier, inc=1, device_id=device, device_id_type=MESH)
    pl.semaphore_wait(barrier, len(devices))


def lane_masks():
    lane = lax.broadcasted_iota(jnp.int32, (1, 128), 1)
    inside = [lane < HEAD_DIM, lane >= HEAD_DIM]
    spare = [lane == HEAD_DIM, lane == 0]
    return inside, spare


def layer_kernel(
    tokens,
    cot,
    w_qkv,
    w_out,
    w_in,
    w_down,
    prefix,
    proj_bias,
    ffn_bias,
    gains,
    shifts,
    lengths,
    key_mask,
    lo_all,
    ig_all,
    pre_o,
    tok,
    cotg,
    bias_s,
    bias_g,
    wq,
    wo,
    wi,
    wd,
    fb,
    q_s,
    k_s,
    v_s,
    kx,
    vtx,
    pt,
    att_loc,
    att_all,
    rl_s,
    normed_s,
    xhat_s,
    nb_s,
    acc,
    act,
    gp,
    lo_s,
    da_s,
    da_all,
    ds_pre,
    dox,
    dq_s,
    core_out,
    core_in,
    x_out,
    x_in,
    fin,
    pre_part,
    pre_land,
    pre_sum,
    loc_sem,
    out_sem,
    tok_sem,
    cot_sem,
    bias_sem,
    fb_sem,
    att_sem,
    core_sem,
    x_sem,
    y_sem,
    c1_sem,
    c2_sem,
    lower_sem,
    lo_sem,
    lox_sem,
    loc_lo_sem,
    lox_core_sem,
    da_sem,
    part_core_sem,
    part_x_sem,
    igz_sem,
    igx_sem,
    igc_sem,
    igcx_sem,
    pre_sem,
    pre2_sem,
):
    z, h, y = places()
    core = lax.rem(h, 2)
    hc, hx, hd_ = member(h, 1), member(h, 2), member(h, 3)
    dev_core, dev_x, dev_diag, dev_y = (z, hc, y), (z, hx, y), (z, hd_, y), (z, h, 1 - y)
    zs = z_peers(z)
    width = tok.shape[1]
    piece = width // 4
    slots = prefix.shape[1]
    total = 4 * width
    group = 2 * z + y
    others = [lax.rem(group + d, 8) for d in range(1, 8)]
    greet([dev_core, dev_x, dev_diag] + [(g // 2, h, lax.rem(g, 2)) for g in others])

    half = width // 2
    my_half = rows_at(core * half, half)
    tok_copies, tok_forwards = [], []
    for k, zp in enumerate(zs):
        tok_copies.append(
            remote(tokens.at[zp, my_half], tok.at[z, my_half], tok_sem.at[0, k], tok_sem.at[1, k], (zp, h, y))
        )
        tok_forwards.append(
            remote(tok.at[zp, my_half], tok.at[zp, my_half], tok_sem.at[2, k], tok_sem.at[3, k], dev_core)
        )
    for copy in tok_copies:
        copy.start()
    tok_own = pltpu.make_async_copy(tokens.at[z], tok.at[z], loc_sem.at[0])
    tok_own.start()
    wq_own = pltpu.make_async_copy(w_qkv, wq, loc_sem.at[1])
    wq_own.start()

    chunks = [(w_out, wo, w_out.shape[0] // 2, 0, w_out.shape[0] // 2)]
    deep = w_in.shape[0] // 2
    for i in range(4):
        chunks.append((w_in, wi, deep, i * (deep // 4), deep // 4))
    deep = w_down.shape[0] // 4
    for i in range(4):
        chunks.append((w_down, wd, deep, i * (deep // 4), deep // 4))
    over_x, over_y, core_x, core_y = [], [], [], []
    for i, (src, dst, deep, offset, size) in enumerate(chunks):
        mine = rows_at(y * deep + offset, size)
        other = rows_at((1 - y) * deep + offset, size)
        over_x.append(remote(src.at[mine], dst.at[h, mine], x_sem.at[0, i], x_sem.at[1, i], dev_x))
        over_y.append(remote(dst.at[hx, mine], dst.at[hx, mine], y_sem.at[0, i], y_sem.at[1, i], dev_y))
        core_x.append(remote(dst.at[hx, mine], dst.at[hx, mine], c1_sem.at[0, i], c1_sem.at[1, i], dev_core))
        core_y.append(remote(dst.at[hx, other], dst.at[hx, other], c2_sem.at[0, i], c2_sem.at[1, i], dev_core))
    n_chunks = len(chunks)
    base, size = w_down.shape[0] // 2, w_down.shape[0] // 8
    lower = rows_at(base + z * size, size, 128)
    part = rows_at(base + z * size + y * (size // 2), size // 2)
    lower_x = remote(w_down.at[part], wd.at[h, part], x_sem.at[0, 9], x_sem.at[1, 9], dev_x)
    lower_y = remote(wd.at[hx, part], wd.at[hx, part], y_sem.at[0, 9], y_sem.at[1, 9], dev_y)
    lower_core = [remote(wd.at[hx, lower], wd.at[hx, lower], c1_sem.at[0, 9], c1_sem.at[1, 9], dev_core)]
    lower_z = []
    for k, zp in enumerate(zs):
        theirs = rows_at(base + zp * size, size, 128)
        lower_z.append(
            remote(wd.at[hx, lower], wd.at[hx, lower], lower_sem.at[0, k], lower_sem.at[1, k], (zp, h, y))
        )
        lower_core.append(
            remote(wd.at[hx, theirs], wd.at[hx, theirs], lower_sem.at[2, k], lower_sem.at[3, k], dev_core)
        )
    x_queue = [over_x[0], lower_x] + over_x[1:]
    for copy in x_queue[:AHEAD]:
        copy.start()

    def serve_x(place):
        x_queue[place].wait_recv()
        if place == 1:
            lower_y.start()
        else:
            i = place - 1 if place else 0
            over_y[i].start()
            core_x[i].start()
        if place + AHEAD < len(x_queue):
            x_queue[place + AHEAD].start()

    def serve_y(i):
        over_y[i].wait_recv()
        core_y[i].start()

    own_weights, core_weights = [], []
    for i, (src, dst) in enumerate(((w_out, wo), (w_in, wi), (w_down, wd))):
        own_weights.append(pltpu.make_async_copy(src, dst.at[h], loc_sem.at[2 + i]))
        core_weights.append(remote(src, dst.at[h], core_sem.at[0, i], core_sem.at[1, i], dev_core))

    spot = lax.broadcasted_iota(jnp.int32, (8, width), 1) + z * width
    for s in range(4):
        live = (jnp.broadcast_to(key_mask[s : s + 1, :], (8, width)) == 1) & (spot < lengths[s])
        bias_s[s] = jnp.where(live, 0.0, NEG_FILL)
    bias_g[z] = bias_s[z]
    bias_copies = [
        remote(bias_s.at[zp], bias_g.at[z], bias_sem.at[0, k], bias_sem.at[1, k], (zp, h, y))
        for k, zp in enumerate(zs)
    ]
    fb[h] = jnp.broadcast_to(ffn_bias[...], fb.shape[1:])
    fb_copies = [
        remote(fb.at[h], fb.at[h], fb_sem.at[0, k], fb_sem.at[1, k], device)
        for k, device in enumerate((dev_core, dev_x, dev_diag))
    ]
    for copy in bias_copies + fb_copies:
        copy.start()
    for copy in own_weights + core_weights:
        copy.start()

    my_piece = rows_at(h * piece, piece)
    cot_copies = [
        remote(cot.at[zp, my_piece], cotg.at[z], cot_sem.at[0, k], cot_sem.at[1, k], (zp, h, y))
        for k, zp in enumerate(zs)
    ]
    cot_own = pltpu.make_async_copy(cot.at[z, my_piece], cotg.at[z], loc_sem.at[5])
    cot_own.start()

    inside, spare = lane_masks()

    pk = prefix[0].astype(BF)
    pv = prefix[1].astype(BF)
    k_s[total : total + slots, :] = pk
    v_s[total : total + slots, :] = pv
    for head in range(4):
        pair, par = head // 2, head % 2
        part = pk[:, 128 * pair : 128 * pair + 128].astype(F32)
        kx[head, total : total + slots, :] = jnp.where(inside[par], part, 0.0).astype(BF)
        vtx[head, HEAD_DIM:, :] = jnp.ones((vtx.shape[1] - HEAD_DIM, vtx.shape[2]), BF)

    def project(block):
        rows = tok[block]
        for i, target in enumerate((q_s, k_s, v_s)):
            value = (nn(rows, wq[i]) + proj_bias[i : i + 1, :]).astype(BF)
            if i == 0:
                value = (value.astype(F32) * HEAD_DIM**-0.5).astype(BF)
            for j in range(4):
                target[rows_at(j * width + block * piece, piece), :] = value[piece * j : piece * j + piece]
            if i == 1:
                column = jnp.broadcast_to(bias_g[block][0:1, :], (128, width)).T
                for head in range(4):
                    pair, par = head // 2, head % 2
                    part = value[:, 128 * pair : 128 * pair + 128].astype(F32)
                    ext = jnp.where(inside[par], part, jnp.where(spare[par], column, 0.0)).astype(BF)
                    for j in range(4):
                        kx[head, rows_at(j * width + block * piece, piece), :] = ext[piece * j : piece * j + piece]

    tok_own.wait()
    wq_own.wait()
    project(z)
    serve_x(0)
    for k, zp in enumerate(zs):
        serve_x(k + 1)
        if k != 1:
            serve_y(k // 2)
        tok_copies[k].wait_recv()
        tok_forwards[k].start()
        bias_copies[k].wait_recv()
        if k == 2:
            lower_y.wait_recv()
            for copy in lower_core[:1] + lower_z + cot_copies:
                copy.start()
        tok_forwards[k].wait_recv()
        project(zp)

    for i in range(4):
        flipped = v_s[i * width : (i + 1) * width, :].astype(F32).T.astype(BF)
        for head in range(4):
            vtx[head, 0:HEAD_DIM, i * width : (i + 1) * width] = flipped[HEAD_DIM * head : HEAD_DIM * (head + 1)]
    flipped = v_s[total : total + slots, :].astype(F32).T.astype(BF)
    for head in range(4):
        vtx[head, 0:HEAD_DIM, total : total + slots] = flipped[HEAD_DIM * head : HEAD_DIM * (head + 1)]

    def att_copy(u):
        j = member(h, u)
        return remote(att_loc.at[j], att_all.at[h], att_sem.at[0, u], att_sem.at[1, u], (z, j, y))

    def attend(step):
        u = 3 - step
        j = member(h, u)
        outs, recips = [], []
        for head in range(4):
            pair, par = head // 2, head % 2
            part = q_s[rows_at(j * width, width, width), 128 * pair : 128 * pair + 128].astype(F32)
            ext = jnp.where(inside[par], part, jnp.where(spare[par], 1.0, 0.0)).astype(BF)
            scores = nt(kx[head], ext)
            top = jnp.max(scores, axis=0, keepdims=True)
            weight = jnp.exp(scores - top).astype(BF)
            pt[head, j] = weight
            summed = nn(vtx[head], weight)
            recip = 1.0 / summed[HEAD_DIM : HEAD_DIM + 1]
            outs.append(summed[0:HEAD_DIM] * recip)
            recips.append(jnp.broadcast_to(recip, (32, width)))
        att_loc[j] = jnp.concatenate(outs, axis=0).T.astype(BF)
        rl_s[j] = jnp.concatenate(recips, axis=0).T

        @pl.when(u > 0)
        def _():
            att_copy(u).start()

        @pl.when(u == 0)
        def _():
            att_all[h] = att_loc[h]

    pl.loop(0, 2)(attend)
    serve_x(4)
    serve_y(2)
    pl.loop(2, 4)(attend)
    serve_x(5)
    serve_y(3)
    att_copies = [att_copy(u) for u in (1, 2, 3)]

    lane = lax.broadcasted_iota(jnp.int32, (1, 128), 1)
    spare_lo = [lane == HEAD_DIM + 1, lane == 1]
    for head in range(4):
        pair, par = head // 2, head % 2
        part = v_s[:, 128 * pair : 128 * pair + 128].astype(F32)
        ones = jnp.where(spare[par] | spare_lo[par], 1.0, 0.0)
        kx[head] = jnp.where(inside[par], part, ones).astype(BF)
    for i in range(5):
        low, size = i * width, width if i < 4 else slots
        flipped = k_s[low : low + size, :].astype(F32).T.astype(BF)
        for head in range(4):
            vtx[head, 0:HEAD_DIM, low : low + size] = flipped[HEAD_DIM * head : HEAD_DIM * (head + 1)]

    serve_x(6)

    own_weights[0].wait()
    core_weights[0].wait_recv()
    core_x[0].wait_recv()
    core_y[0].wait_recv()
    for copy in att_copies:
        copy.wait_recv()
    attention = nn(att_all[0], wo[0])
    for j in range(1, 4):
        attention += nn(att_all[j], wo[j])
    mine = jnp.concatenate([tok[b, my_piece, :] for b in range(4)], axis=0).astype(F32)
    resid = mine + attention + shifts[0:1, :]
    centred = resid - jnp.mean(resid, axis=-1, keepdims=True)
    inverse_one = lax.rsqrt(jnp.mean(centred * centred, axis=-1, keepdims=True) + NORM_EPSILON)
    xhat = centred * inverse_one
    xhat_s[...] = xhat
    normed = xhat * gains[0:1, :] + shifts[1:2, :]
    normed_s[...] = normed
    nb_s[...] = normed.astype(BF)

    tile = 256
    tiles = wi.shape[2] // tile

    def ffn_in(quarter):
        @pl.loop(0, tiles, unroll=4)
        def _(n):
            cols = rows_at(n * tile, tile, tile)
            inner = nn(nb_s[...], wi[quarter, :, cols]) + fb[quarter, 0:1, cols]
            cdf = 0.5 * (1.0 + lax.erf(inner * 0.7071067811865476))
            act[quarter, :, cols] = (inner * cdf).astype(BF)
            gp[quarter, :, cols] = cdf + inner * (jnp.exp(-0.5 * inner * inner) * 0.3989422804014327)

    for copy in fb_copies:
        copy.wait_recv()
    own_weights[1].wait()
    core_weights[1].wait_recv()
    ffn_in(h)
    serve_x(7)
    ffn_in(hc)
    serve_y(4)
    serve_x(8)
    for i in range(1, 5):
        core_x[i].wait_recv()
        core_y[i].wait_recv()
    ffn_in(hx)
    ffn_in(hd_)

    acc[...] = jnp.zeros(acc.shape, F32)

    def ffn_out(quarter, start, deep):
        span = rows_at(start, deep, deep)

        @pl.loop(0, tiles, unroll=4)
        def _(n):
            cols = rows_at(n * tile, tile, tile)
            acc[:, cols] += nn(act[quarter, :, span], wd[quarter, span, cols])

    own_weights[2].wait()
    core_weights[2].wait_recv()
    deep = wd.shape[1]
    for k in range(3):
        lower_z[k].wait_recv()
        lower_core[k + 1].start()
    ffn_out(h, 0, deep)
    serve_x(9)
    serve_y(5)
    serve_y(6)
    ffn_out(hc, 0, deep)
    serve_y(7)
    ffn_out(hx, base, deep // 2)
    for copy in lower_core:
        copy.wait_recv()
    ffn_out(hd_, base, deep // 2)
    for i in range(5, 9):
        core_x[i].wait_recv()
    ffn_out(hx, y * (deep // 4), deep // 4)
    ffn_out(hd_, y * (deep // 4), deep // 4)
    serve_y(8)
    ffn_out(hx, (1 - y) * (deep // 4), deep // 4)
    for i in range(5, 9):
        core_y[i].wait_recv()
    ffn_out(hd_, (1 - y) * (deep // 4), deep // 4)

    resid = normed_s[...] + acc[...] + shifts[2:3, :]
    centred = resid - jnp.mean(resid, axis=-1, keepdims=True)
    inverse = lax.rsqrt(jnp.mean(centred * centred, axis=-1, keepdims=True) + NORM_EPSILON)
    xhat = centred * inverse
    lo_s[...] = (xhat * gains[1:2, :] + shifts[3:4, :]).astype(BF)
    x_piece = rows_at(hx * piece, piece)
    lo_z, lo_x, lo_core, lo_across = [], [], [], []
    blocks = zs + [z]
    for k, b in enumerate(blocks):
        rows = rows_at(b * piece, piece)
        source = lo_all.at[b, my_piece]
        if k < 3:
            lo_z.append(remote(lo_s.at[rows], lo_all.at[z, my_piece], lo_sem.at[0, k], lo_sem.at[1, k], (b, h, y)))
        else:
            source = lo_s.at[rows]
        lo_x.append(remote(source, lo_all.at[b, my_piece], lox_sem.at[0, k], lox_sem.at[1, k], dev_x))
        lo_core.append(remote(source, lo_all.at[b, my_piece], loc_lo_sem.at[0, k], loc_lo_sem.at[1, k], dev_core))
        lo_across.append(
            remote(lo_all.at[b, x_piece], lo_all.at[b, x_piece], lox_core_sem.at[0, k], lox_core_sem.at[1, k], dev_core)
        )
    lo_own = pltpu.make_async_copy(lo_s.at[rows_at(z * piece, piece)], lo_all.at[z, my_piece], out_sem.at[0])
    for copy in lo_z + [lo_x[3], lo_core[3], lo_own]:
        copy.start()

    def serve_lo(k):
        lo_z[k].wait_recv()
        lo_x[k].start()
        lo_core[k].start()

    cot_own.wait()
    for copy in cot_copies:
        copy.wait_recv()
    dy = jnp.concatenate([cotg[b] for b in range(4)], axis=0).astype(F32) * gains[1:2, :]
    g_two = inverse * (
        dy - jnp.mean(dy, axis=-1, keepdims=True) - xhat * jnp.mean(dy * xhat, axis=-1, keepdims=True)
    )
    acc[...] = g_two
    nb_s[...] = g_two.astype(BF)

    @pl.loop(0, 4)
    def _(quarter):
        @pl.loop(0, tiles, unroll=4)
        def _(n):
            cols = rows_at(n * tile, tile, tile)
            d_act = nt(nb_s[...], wd[quarter, cols, :])
            act[quarter, :, cols] = (d_act * gp[quarter, :, cols]).astype(BF)

    @pl.loop(0, 4)
    def _(quarter):
        @pl.loop(0, tiles, unroll=4)
        def _(n):
            cols = rows_at(n * tile, tile, tile)
            acc[:, cols] += nt(act[quarter], wi[quarter, cols, :])

    dy = acc[...] * gains[0:1, :]
    xhat = xhat_s[...]
    g_one = inverse_one * (
        dy - jnp.mean(dy, axis=-1, keepdims=True) - xhat * jnp.mean(dy * xhat, axis=-1, keepdims=True)
    )
    acc[...] = g_one
    low = g_one.astype(BF)
    da_copies = {}
    for u in (2, 3, 1):
        j = member(h, u)
        da_s[j] = nt(low, wo[j]).astype(BF)
        da_copies[u] = remote(da_s.at[j], da_all.at[h], da_sem.at[0, u], da_sem.at[1, u], (z, j, y))
        da_copies[u].start()
    da_all[h] = nt(low, wo[h]).astype(BF)
    for copy in over_y + [lower_y] + core_x + core_y + lower_z + lower_core:
        copy.wait_send()

    def score_grads(u):
        j = member(h, u)

        @pl.when(u > 0)
        def _():
            remote(da_s.at[j], da_all.at[h], da_sem.at[0, u], da_sem.at[1, u], (z, j, y)).wait_recv()

        grads = []
        for head in range(4):
            pair, par = head // 2, head % 2
            lanes = slice(128 * pair, 128 * pair + 128)
            d_out = da_all[j, :, lanes].astype(F32)
            recip = rl_s[j, :, 32 * head : 32 * head + 1]
            delta = recip * jnp.sum(
                jnp.where(inside[par], d_out * att_loc[j, :, lanes].astype(F32), 0.0), axis=-1, keepdims=True
            )
            high = delta.astype(BF).astype(F32)
            ext = jnp.where(spare[par], -high, jnp.where(spare_lo[par], high - delta, 0.0))
            ext = jnp.where(inside[par], d_out * recip, ext).astype(BF)
            dox[head, j] = ext
            d_probs = nt(kx[head], ext).astype(BF)
            d_scores = pt[head, j] * d_probs
            wi[head, :, rows_at(j * width, width, width)] = d_scores[0:total]
            ds_pre[head, j] = d_scores[total:]
            grads.append(nn(vtx[head, 0:HEAD_DIM, :], d_scores))
        dq_s[j] = (jnp.concatenate(grads, axis=0).T * HEAD_DIM**-0.5).astype(BF)

    pl.loop(0, 2)(score_grads)
    serve_lo(0)
    serve_lo(1)
    serve_lo(2)
    pl.loop(2, 4)(score_grads)

    def key_side(left, right):
        halves = []
        for pair in range(2):
            sides = []
            for par in range(2):
                head = 2 * pair + par
                value = nn(left(head, 0), right(head, 0, pair))
                for j in range(1, 4):
                    value += nn(left(head, j), right(head, j, pair))
                sides.append(value)
            halves.append(jnp.where(inside[0], sides[0], sides[1]))
        return jnp.concatenate(halves, axis=-1)

    def d_values(rows):
        return key_side(lambda head, j: pt[head, j, rows, :], lambda head, j, pair: dox[head, j])

    def d_keys(left):
        return key_side(left, lambda head, j, pair: q_s[j * width : (j + 1) * width, 128 * pair : 128 * pair + 128])

    def partial(i):
        rows = rows_at(i * width, width, width)
        dk = d_keys(lambda head, j: wi[head, rows, j * width : (j + 1) * width]).astype(BF)
        dv = d_values(rows).astype(BF)
        return nt(dq_s[i], wq[0]) + nt(dk, wq[1]) + nt(dv, wq[2])

    part_core = [
        remote(core_out.at[i], core_in.at[i], part_core_sem.at[0, i], part_core_sem.at[1, i], dev_core) for i in range(2)
    ]
    part_x = []
    for k, b in enumerate(blocks):
        rows = rows_at(b * piece, piece)
        part_x.append(remote(x_out.at[rows], x_in.at[rows], part_x_sem.at[0, k], part_x_sem.at[1, k], dev_x))

    core_out[0] = partial(hd_).astype(BF)
    part_core[0].start()
    mine = partial(hx)
    part_core[0].wait_recv()
    x_out[...] = (mine + core_in[0].astype(F32)).astype(BF)
    for copy in part_x:
        copy.start()

    pre_part[0] = d_keys(lambda head, j: ds_pre[head, j])
    pre_part[1] = d_values(pl.ds(total, slots))
    few = slots // 8
    mine_rows = rows_at(group * few, few, few)
    pre_copies, pre_back = [], []
    for d, g in enumerate(others):
        device = (g // 2, h, lax.rem(g, 2))
        pre_copies.append(
            remote(pre_part.at[:, rows_at(g * few, few, few)], pre_land.at[d], pre_sem.at[0, d], pre_sem.at[1, d], device)
        )
        pre_back.append(
            remote(pre_sum.at[:, mine_rows], pre_sum.at[:, mine_rows], pre2_sem.at[0, d], pre2_sem.at[1, d], device)
        )
    for copy in pre_copies:
        copy.start()
    for k in (3, 0, 1, 2):
        lo_x[k].wait_recv()
        lo_across[k].start()

    core_out[1] = partial(hc).astype(BF)
    part_core[1].start()
    acc[...] += partial(h)
    part_core[1].wait_recv()
    acc[...] += core_in[1].astype(F32)

    igz, igx, igc, igcx = [], [], [], []
    for k, b in enumerate(blocks):
        rows = rows_at(b * piece, piece)
        source = ig_all.at[b, my_piece]
        if k < 3:
            igz.append(remote(fin.at[rows], ig_all.at[z, my_piece], igz_sem.at[0, k], igz_sem.at[1, k], (b, h, y)))
        else:
            source = fin.at[rows]
        igx.append(remote(source, ig_all.at[b, my_piece], igx_sem.at[0, k], igx_sem.at[1, k], dev_x))
        igc.append(remote(source, ig_all.at[b, my_piece], igc_sem.at[0, k], igc_sem.at[1, k], dev_core))
        igcx.append(
            remote(ig_all.at[b, x_piece], ig_all.at[b, x_piece], igcx_sem.at[0, k], igcx_sem.at[1, k], dev_core)
        )
    ig_own = pltpu.make_async_copy(fin.at[rows_at(z * piece, piece)], ig_all.at[z, my_piece], out_sem.at[1])
    for k, b in enumerate(blocks):
        rows = rows_at(b * piece, piece)
        part_x[k].wait_recv()
        fin[rows, :] = (acc[rows, :] + x_in[rows, :].astype(F32)).astype(BF)
        if k < 3:
            igz[k].start()
        else:
            ig_own.start()
            igx[3].start()
            igc[3].start()
        if k == 1:
            for copy in pre_copies:
                copy.wait_recv()
            for i in range(2):
                term = pre_part[i, mine_rows, :]
                for d in range(7):
                    term += pre_land[d, i]
                pre_sum[i, mine_rows, :] = term
            for copy in pre_back:
                copy.start()
    for copy in lo_core + lo_across:
        copy.wait_recv()
    lo_own.wait()
    for k in range(3):
        igz[k].wait_recv()
        igx[k].start()
        igc[k].start()
    for copy in pre_back:
        copy.wait_recv()
    pre_o[...] = pre_sum[...]
    for k in (3, 0, 1, 2):
        igx[k].wait_recv()
        igcx[k].start()
    for copy in igc + igcx:
        copy.wait_recv()
    ig_own.wait()
    sent = tok_copies + tok_forwards + x_queue + core_weights + bias_copies + fb_copies + cot_copies + att_copies
    sent += lo_z + lo_x + lo_core + lo_across + list(da_copies.values()) + part_core + part_x
    for copy in sent + igz + igx + igc + igcx + pre_copies + pre_back:
        copy.wait_send()


def layer(tokens, cot, w_qkv, w_out, w_in, w_down, prefix, proj_bias, ffn_bias, gains, shifts, lengths, key_mask):
    seqs, width, model = tokens.shape
    local = w_qkv.shape[2]
    hidden = w_in.shape[1]
    slots = prefix.shape[1]
    total = seqs * width
    keys = total + slots
    dma = pltpu.SemaphoreType.DMA
    hbm = pl.BlockSpec(memory_space=pl.ANY)
    vmem = pl.BlockSpec(memory_space=pltpu.VMEM)
    shape = jax.ShapeDtypeStruct
    return pl.pallas_call(
        layer_kernel,
        name="layer",
        out_shape=(
            pltpu.VMEM((4, width, model), BF),
            pltpu.VMEM((4, width, model), BF),
            pltpu.VMEM((2, slots, local), F32),
        ),
        in_specs=[hbm] * 6 + [vmem] * 5 + [pl.BlockSpec(memory_space=pltpu.SMEM), vmem],
        out_specs=(vmem, vmem, vmem),
        scratch_shapes=[
            pltpu.VMEM((4, width, model), BF),
            pltpu.VMEM((4, width // 4, model), BF),
            pltpu.VMEM((4, 8, width), F32),
            pltpu.VMEM((4, 8, width), F32),
            pltpu.VMEM((3, model, local), BF),
            pltpu.VMEM((4, local, model), BF),
            pltpu.VMEM((4, model, hidden), BF),
            pltpu.VMEM((4, hidden, model), BF),
            pltpu.VMEM((4, 8, hidden), F32),
            pltpu.VMEM((total, local), BF),
            pltpu.VMEM((keys, local), BF),
            pltpu.VMEM((keys, local), BF),
            pltpu.VMEM((4, keys, 128), BF),
            pltpu.VMEM((4, HEAD_DIM + 16, keys), BF),
            pltpu.VMEM((4, 4, keys, width), BF),
            pltpu.VMEM((4, width, local), BF),
            pltpu.VMEM((4, width, local), BF),
            pltpu.VMEM((4, width, 128), F32),
            pltpu.VMEM((width, model), F32),
            pltpu.VMEM((width, model), F32),
            pltpu.VMEM((width, model), BF),
            pltpu.VMEM((width, model), F32),
            pltpu.VMEM((4, width, hidden), BF),
            pltpu.VMEM((4, width, hidden), F32),
            pltpu.VMEM((width, model), BF),
            pltpu.VMEM((4, width, local), BF),
            pltpu.VMEM((4, width, local), BF),
            pltpu.VMEM((4, 4, slots, width), BF),
            pltpu.VMEM((4, 4, width, 128), BF),
            pltpu.VMEM((4, width, local), BF),
            pltpu.VMEM((2, width, model), BF),
            pltpu.VMEM((2, width, model), BF),
            pltpu.VMEM((width, model), BF),
            pltpu.VMEM((width, model), BF),
            pltpu.VMEM((width, model), BF),
            pltpu.VMEM((2, slots, local), F32),
            pltpu.VMEM((7, 2, slots // 8, local), F32),
            pltpu.VMEM((2, slots, local), F32),
            dma((6,)),
            dma((4,)),
            dma((4, 3)),
            dma((2, 3)),
            dma((2, 3)),
            dma((2, 3)),
            dma((2, 4)),
            dma((2, 3)),
            dma((2, 10)),
            dma((2, 10)),
            dma((2, 10)),
            dma((2, 10)),
            dma((4, 3)),
            dma((2, 3)),
            dma((2, 4)),
            dma((2, 4)),
            dma((2, 4)),
            dma((2, 4)),
            dma((2, 2)),
            dma((2, 4)),
            dma((2, 3)),
            dma((2, 4)),
            dma((2, 4)),
            dma((2, 4)),
            dma((2, 7)),
            dma((2, 7)),
        ],
        compiler_params=pltpu.CompilerParams(
            collective_id=0, has_side_effects=True, vmem_limit_bytes=58 * 2**20
        ),
        cost_estimate=pl.CostEstimate(flops=15 * 10**9, bytes_accessed=40 * 2**20, transcendentals=6 * 10**6),
    )(tokens, cot, w_qkv, w_out, w_in, w_down, prefix, proj_bias, ffn_bias, gains, shifts, lengths, key_mask)


def finish_kernel(lo, ig, grad, prefix, first, second, lo_o, ig_o, grad_o, new_o, first_o, second_o, lo_f, ig_f, sem):
    seqs = lo.shape[0]
    copies = []
    for i in range(seqs):
        for k, (src, mid, dst) in enumerate(((lo, lo_f, lo_o), (ig, ig_f, ig_o))):
            mid[i] = src[i].astype(F32)
            copy = pltpu.make_async_copy(mid.at[i], dst.at[i], sem.at[k, i])
            copy.start()
            copies.append(copy)
    slope = grad[...]
    grad_o[...] = slope
    new_first = BETA_ONE * first[...] + (1.0 - BETA_ONE) * slope
    new_second = BETA_TWO * second[...] + (1.0 - BETA_TWO) * slope * slope
    first_hat = new_first / (1.0 - BETA_ONE**STEP)
    second_hat = new_second / (1.0 - BETA_TWO**STEP)
    value = prefix[...]
    new_o[...] = value - LEARN_RATE * (first_hat / (jnp.sqrt(second_hat) + ADAM_EPSILON) + WEIGHT_DECAY * value)
    first_o[...] = new_first
    second_o[...] = new_second
    for copy in copies:
        copy.wait()


def finish(lo, ig, grad, prefix, first, second):
    hbm = pl.BlockSpec(memory_space=pl.ANY)
    vmem = pl.BlockSpec(memory_space=pltpu.VMEM)
    shape = jax.ShapeDtypeStruct
    whole, little = shape(lo.shape, F32), shape(prefix.shape, F32)
    return pl.pallas_call(
        finish_kernel,
        name="finish",
        out_shape=(whole, whole, little, little, little, little),
        in_specs=[vmem] * 6,
        out_specs=(hbm, hbm, vmem, vmem, vmem, vmem),
        scratch_shapes=[
            pltpu.VMEM(lo.shape, F32),
            pltpu.VMEM(lo.shape, F32),
            pltpu.SemaphoreType.DMA((2, lo.shape[0])),
        ],
        compiler_params=pltpu.CompilerParams(vmem_limit_bytes=40 * 2**20),
    )(lo, ig, grad, prefix, first, second)


def body(*args):
    (tokens, cotangent, prefix, first_moment, second_moment, w_qkv, proj_bias, w_out, w_in, ffn_bias) = args[:10]
    w_down, gains, shifts, lengths, key_mask = args[10:]
    fits = (
        lax.axis_size("seq") == 4
        and lax.axis_size("head") == 4
        and lax.axis_size("batch") == 2
        and tokens.shape == (4, 256, 1024)
        and w_qkv.shape == (3, 1024, 256)
        and w_in.shape == (1024, 1024)
        and prefix.shape[1] == 64
    )
    if not fits:
        return general_body(*args)
    layer_out, input_grad, prefix_grad = layer(
        tokens, cotangent, w_qkv, w_out, w_in, w_down, prefix, proj_bias, ffn_bias.reshape(1, -1), gains, shifts,
        lengths, key_mask,
    )
    layer_out, input_grad, prefix_grad, new_prefix, new_first, new_second = finish(
        layer_out, input_grad, prefix_grad, prefix, first_moment, second_moment
    )
    return layer_out, input_grad, prefix_grad, new_prefix, new_first, new_second


def solution(mesh):
    placed = (
        P("batch", "seq", None),
        P("batch", "seq", None),
        P(None, None, "head"),
        P(None, None, "head"),
        P(None, None, "head"),
        P(None, None, "head"),
        P(None, "head"),
        P("head", None),
        P(None, "head"),
        P("head"),
        P("head", None),
        P(),
        P(),
        P("batch"),
        P("batch", "seq"),
    )
    return jax.shard_map(
        body,
        mesh=mesh,
        in_specs=placed,
        out_specs=(
            P("batch", "seq", None),
            P("batch", "seq", None),
            P(None, None, "head"),
            P(None, None, "head"),
            P(None, None, "head"),
            P(None, None, "head"),
        ),
        check_vma=False,
    )
```

```python
import jax
import jax.numpy as jnp
from jax import lax
from jax.experimental import pallas as pl
from jax.experimental.pallas import tpu as pltpu
from jax.sharding import PartitionSpec as P

HEAD_DIM = 64
STEP = 10


NEG_FILL = -1e30
NORM_EPSILON = 1e-05
BETA_ONE = 0.9
BETA_TWO = 0.95
LEARN_RATE = 0.8
WEIGHT_DECAY = 0.01
ADAM_EPSILON = 1e-08


def shifted(value, axis, steps):
    count = lax.axis_size(axis)
    pairs = [(source, (source + steps) % count) for source in range(count)]
    return lax.ppermute(value, axis, pairs)


def layer_norm(values_in, gain_row, shift_row):
    row_mean = jnp.mean(values_in, axis=-1, keepdims=True)
    centred = values_in - row_mean
    spread = jnp.mean(centred * centred, axis=-1, keepdims=True)
    return centred * lax.rsqrt(spread + NORM_EPSILON) * gain_row + shift_row


def exact_gelu(values_in):
    return jax.nn.gelu(values_in, approximate=False)


def block_scores(queries, block_keys, block_bias, score_scale):
    scores = (
        jnp.einsum("shqd,shkd->shqk", queries, block_keys, preferred_element_type=jnp.float32)
        * score_scale
    )
    return scores + block_bias.astype(jnp.float32)[:, None, None, :]


def absorb(softmax_state, queries, block_keys, block_values, block_bias, score_scale):
    row_max, row_sum, weighted = softmax_state
    scores = block_scores(queries, block_keys, block_bias, score_scale)
    new_max = jnp.maximum(row_max, jnp.max(scores, axis=-1))
    fade_factor = jnp.exp(row_max - new_max)
    exp_scores = jnp.exp(scores - new_max[..., None])
    row_sum = row_sum * fade_factor + jnp.sum(exp_scores, axis=-1)
    weighted = weighted * fade_factor[..., None] + jnp.einsum(
        "shqk,shkd->shqd",
        exp_scores.astype(jnp.bfloat16),
        block_values,
        preferred_element_type=jnp.float32,
    )
    return (new_max, row_sum, weighted)


def back_block(
    queries, grad_att, log_total, row_delta, block_keys, block_values, block_bias, score_scale
):
    scores = block_scores(queries, block_keys, block_bias, score_scale)
    probabilities = jnp.exp(scores - log_total[..., None])
    grad_probs = jnp.einsum(
        "shqd,shkd->shqk", grad_att, block_values, preferred_element_type=jnp.float32
    )
    grad_scores = (probabilities * (grad_probs - row_delta[..., None])).astype(jnp.bfloat16)
    grad_queries = (
        jnp.einsum("shqk,shkd->shqd", grad_scores, block_keys, preferred_element_type=jnp.float32)
        * score_scale
    )
    grad_keys = (
        jnp.einsum("shqk,shqd->shkd", grad_scores, queries, preferred_element_type=jnp.float32)
        * score_scale
    )
    grad_values = jnp.einsum(
        "shqk,shqd->shkd",
        probabilities.astype(jnp.bfloat16),
        grad_att,
        preferred_element_type=jnp.float32,
    )
    return (grad_queries, grad_keys, grad_values)


def general_body(
    tokens,
    cotangent,
    prefix,
    first_moment,
    second_moment,
    w_qkv,
    proj_bias,
    w_out,
    w_in,
    ffn_bias,
    w_down,
    gains,
    shifts,
    lengths,
    key_mask,
):
    seqs_dev, shard_len, model_width = tokens.shape
    row_count = seqs_dev * shard_len
    local_width = w_qkv.shape[2]
    heads_dev = local_width // HEAD_DIM
    prefix_slots = prefix.shape[1]
    score_scale = HEAD_DIM ** (-0.5)
    cycle_size = lax.axis_size("seq")
    cycle_place = lax.axis_index("seq")
    flat_tokens = tokens.reshape(row_count, model_width)
    projected = (
        jnp.einsum("td,ide->ite", flat_tokens, w_qkv, preferred_element_type=jnp.float32)
        + proj_bias[:, None, :]
    )
    by_head = (
        projected.astype(jnp.bfloat16)
        .reshape(3, seqs_dev, shard_len, heads_dev, HEAD_DIM)
        .transpose(0, 1, 3, 2, 4)
    )
    queries = by_head[0]
    own_keys = by_head[1]
    own_values = by_head[2]
    positions = cycle_place * shard_len + lax.broadcasted_iota(jnp.int32, (seqs_dev, shard_len), 1)
    live_keys = (key_mask == 1) & (positions < lengths[:, None])
    own_bias = jnp.where(live_keys, 0.0, NEG_FILL).astype(jnp.bfloat16)
    prefix_low = (
        prefix.astype(jnp.bfloat16)
        .reshape(2, prefix_slots, heads_dev, HEAD_DIM)
        .transpose(0, 2, 1, 3)
    )
    pre_scores = (
        jnp.einsum("shqd,hpd->shqp", queries, prefix_low[0], preferred_element_type=jnp.float32)
        * score_scale
    )
    row_max = jnp.max(pre_scores, axis=-1)
    exp_prefix = jnp.exp(pre_scores - row_max[..., None])
    row_sum = jnp.sum(exp_prefix, axis=-1)
    weighted = jnp.einsum(
        "shqp,hpd->shqd",
        exp_prefix.astype(jnp.bfloat16),
        prefix_low[1],
        preferred_element_type=jnp.float32,
    )

    def visit_keys(softmax_state, block_keys, block_values, block_bias):
        return absorb(softmax_state, queries, block_keys, block_values, block_bias, score_scale)

    def forward_turn(turn_index, carried):
        softmax_state, block_keys, block_values, block_bias = carried
        softmax_state = visit_keys(softmax_state, block_keys, block_values, block_bias)
        block_keys, block_values, block_bias = shifted(
            (block_keys, block_values, block_bias), "seq", 1
        )
        return (softmax_state, block_keys, block_values, block_bias)

    carried = lax.fori_loop(
        0,
        cycle_size - 1,
        forward_turn,
        ((row_max, row_sum, weighted), own_keys, own_values, own_bias),
    )
    row_max, row_sum, weighted = visit_keys(carried[0], carried[1], carried[2], carried[3])
    log_total = row_max + jnp.log(row_sum)
    attended = weighted / row_sum[..., None]
    merged = attended.astype(jnp.bfloat16).transpose(0, 2, 1, 3).reshape(row_count, local_width)
    attention = (
        lax.psum(jnp.dot(merged, w_out, preferred_element_type=jnp.float32), "head") + shifts[0]
    )
    resid_one = flat_tokens.astype(jnp.float32) + attention
    normed, norm_one_back = jax.vjp(
        lambda values_in: layer_norm(values_in, gains[0], shifts[1]), resid_one
    )
    inner_sum = (
        jnp.dot(normed.astype(jnp.bfloat16), w_in, preferred_element_type=jnp.float32) + ffn_bias
    )
    activated, gelu_back = jax.vjp(exact_gelu, inner_sum)
    feed_forward = (
        lax.psum(
            jnp.dot(activated.astype(jnp.bfloat16), w_down, preferred_element_type=jnp.float32),
            "head",
        )
        + shifts[2]
    )
    layer_value, norm_two_back = jax.vjp(
        lambda values_in: layer_norm(values_in, gains[1], shifts[3]), normed + feed_forward
    )
    contract_last = (((1,), (1,)), ((), ()))
    (grad_two,) = norm_two_back(cotangent.reshape(row_count, model_width).astype(jnp.float32))
    grad_act = lax.dot_general(
        grad_two.astype(jnp.bfloat16), w_down, contract_last, preferred_element_type=jnp.float32
    )
    (grad_inner,) = gelu_back(grad_act)
    hidden_part = lax.dot_general(
        grad_inner.astype(jnp.bfloat16), w_in, contract_last, preferred_element_type=jnp.float32
    )
    grad_normed = grad_two + lax.psum(hidden_part, "head")
    (grad_one,) = norm_one_back(grad_normed)
    grad_merged = lax.dot_general(
        grad_one.astype(jnp.bfloat16), w_out, contract_last, preferred_element_type=jnp.float32
    )
    grad_att = (
        grad_merged.astype(jnp.bfloat16)
        .reshape(seqs_dev, shard_len, heads_dev, HEAD_DIM)
        .transpose(0, 2, 1, 3)
    )
    row_delta = jnp.sum(grad_att.astype(jnp.float32) * attended, axis=-1)
    pre_probs = jnp.exp(pre_scores - log_total[..., None])
    grad_pre_probs = jnp.einsum(
        "shqd,hpd->shqp", grad_att, prefix_low[1], preferred_element_type=jnp.float32
    )
    grad_pre_scores = (pre_probs * (grad_pre_probs - row_delta[..., None])).astype(jnp.bfloat16)
    grad_query_pre = (
        jnp.einsum(
            "shqp,hpd->shqd", grad_pre_scores, prefix_low[0], preferred_element_type=jnp.float32
        )
        * score_scale
    )
    grad_pre_keys = (
        jnp.einsum("shqp,shqd->hpd", grad_pre_scores, queries, preferred_element_type=jnp.float32)
        * score_scale
    )
    grad_pre_values = jnp.einsum(
        "shqp,shqd->hpd",
        pre_probs.astype(jnp.bfloat16),
        grad_att,
        preferred_element_type=jnp.float32,
    )
    prefix_terms = (
        jnp.stack([grad_pre_keys, grad_pre_values])
        .transpose(0, 2, 1, 3)
        .reshape(2, prefix_slots, local_width)
    )
    empty_grad = jnp.zeros(queries.shape, jnp.float32)

    def back_visit(query_side, key_side):
        return back_block(
            query_side[0],
            query_side[1],
            query_side[2],
            query_side[3],
            key_side[0],
            key_side[1],
            key_side[2],
            score_scale,
        )

    own_key_side = (own_keys, own_values, own_bias)

    def query_turn(turn_index, carried):
        grad_keys, grad_values, visit_queries, visit_grad, visit_total, visit_delta, visit_sum = (
            carried
        )
        turn_queries, turn_keys, turn_values = back_visit(
            (visit_queries, visit_grad, visit_total, visit_delta), own_key_side
        )
        moved = (
            shifted(visit_queries.astype(jnp.float32), "seq", 1).astype(visit_queries.dtype),
            shifted(visit_grad.astype(jnp.float32), "seq", 1).astype(visit_grad.dtype),
            shifted(visit_total, "seq", 1),
            shifted(visit_delta, "seq", 1),
            shifted(visit_sum + turn_queries, "seq", 1),
        )
        return (grad_keys + turn_keys, grad_values + turn_values) + moved

    carried = lax.fori_loop(
        0,
        cycle_size - 1,
        query_turn,
        (empty_grad, empty_grad, queries, grad_att, log_total, row_delta, grad_query_pre),
    )
    grad_keys, grad_values, visit_queries, visit_grad, visit_total, visit_delta, visit_sum = carried
    turn_queries, turn_keys, turn_values = back_visit(
        (visit_queries, visit_grad, visit_total, visit_delta), own_key_side
    )
    grad_keys = grad_keys + turn_keys
    grad_values = grad_values + turn_values
    grad_queries = shifted(visit_sum + turn_queries, "seq", 1)
    grad_rows = (
        jnp.stack([grad_queries, grad_keys, grad_values])
        .astype(jnp.bfloat16)
        .transpose(0, 1, 3, 2, 4)
        .reshape(3, row_count, local_width)
    )
    input_part = jnp.einsum("ite,ide->td", grad_rows, w_qkv, preferred_element_type=jnp.float32)
    input_grad = grad_one + lax.psum(input_part, "head")
    prefix_grad = lax.psum(prefix_terms, ("seq", "batch"))
    new_first = BETA_ONE * first_moment + (1.0 - BETA_ONE) * prefix_grad
    new_second = BETA_TWO * second_moment + (1.0 - BETA_TWO) * prefix_grad * prefix_grad
    first_hat = new_first / (1.0 - BETA_ONE**STEP)
    second_hat = new_second / (1.0 - BETA_TWO**STEP)
    new_prefix = prefix - LEARN_RATE * (
        first_hat / (jnp.sqrt(second_hat) + ADAM_EPSILON) + WEIGHT_DECAY * prefix
    )
    layer_out = layer_value.reshape(seqs_dev, shard_len, model_width)
    return (
        layer_out,
        input_grad.reshape(seqs_dev, shard_len, model_width),
        prefix_grad,
        new_prefix,
        new_first,
        new_second,
    )


BF = jnp.bfloat16
F32 = jnp.float32
MESH = pl.DeviceIdType.MESH
AHEAD = 2


def nn(left, right):
    return jnp.dot(left, right, preferred_element_type=F32)


def nt(left, right):
    return lax.dot_general(
        left, right, (((1,), (1,)), ((), ())), preferred_element_type=F32
    )


def remote(src, dst, send, recv, device):
    return pltpu.make_async_remote_copy(
        src, dst, send, recv, device_id=device, device_id_type=MESH
    )


def rows_at(start, size, step=64):
    return pl.ds(pl.multiple_of(start, step), size)


def places():
    z = lax.axis_index("seq")
    h = lax.axis_index("head")
    y = lax.axis_index("batch")
    return z, h, y


def member(h, u):
    chip, core = h // 2, lax.rem(h, 2)
    return 2 * lax.rem(chip + u // 2, 2) + lax.rem(core + u % 2, 2)


def z_peers(z):
    return [z + 1 - 2 * lax.rem(z, 2), 3 - z, lax.rem(z + 2, 4)]


def greet(devices):
    barrier = pltpu.get_barrier_semaphore()
    for device in devices:
        pl.semaphore_signal(barrier, inc=1, device_id=device, device_id_type=MESH)
    pl.semaphore_wait(barrier, len(devices))


def lane_masks():
    lane = lax.broadcasted_iota(jnp.int32, (1, 128), 1)
    inside = [lane < HEAD_DIM, lane >= HEAD_DIM]
    spare = [lane == HEAD_DIM, lane == 0]
    return inside, spare


def layer_kernel(
    tokens,
    cot,
    w_qkv,
    w_out,
    w_in,
    w_down,
    prefix,
    proj_bias,
    ffn_bias,
    gains,
    shifts,
    lengths,
    key_mask,
    lo_all,
    ig_all,
    pre_o,
    tok,
    cotg,
    bias_s,
    bias_g,
    wq,
    wo,
    wi,
    wd,
    fb,
    q_s,
    k_s,
    v_s,
    kx,
    vtx,
    pt,
    att_loc,
    att_all,
    rl_s,
    normed_s,
    xhat_s,
    nb_s,
    acc,
    act,
    gp,
    lo_s,
    da_s,
    da_all,
    ds_pre,
    dox,
    dq_s,
    core_out,
    core_in,
    x_out,
    x_in,
    fin,
    pre_part,
    pre_land,
    pre_sum,
    loc_sem,
    out_sem,
    tok_sem,
    cot_sem,
    bias_sem,
    fb_sem,
    att_sem,
    core_sem,
    x_sem,
    y_sem,
    c1_sem,
    c2_sem,
    lower_sem,
    lo_sem,
    lox_sem,
    loc_lo_sem,
    lox_core_sem,
    da_sem,
    part_core_sem,
    part_x_sem,
    igz_sem,
    igx_sem,
    igc_sem,
    igcx_sem,
    pre_sem,
    pre2_sem,
):
    z, h, y = places()
    core = lax.rem(h, 2)
    hc, hx, hd_ = member(h, 1), member(h, 2), member(h, 3)
    dev_core, dev_x, dev_diag, dev_y = (z, hc, y), (z, hx, y), (z, hd_, y), (z, h, 1 - y)
    zs = z_peers(z)
    width = tok.shape[1]
    piece = width // 4
    slots = prefix.shape[1]
    total = 4 * width
    group = 2 * z + y
    others = [lax.rem(group + d, 8) for d in range(1, 8)]
    greet([dev_core, dev_x, dev_diag] + [(g // 2, h, lax.rem(g, 2)) for g in others])

    half = width // 2
    my_half = rows_at(core * half, half)
    tok_copies, tok_forwards = [], []
    for k, zp in enumerate(zs):
        tok_copies.append(
            remote(tokens.at[zp, my_half], tok.at[z, my_half], tok_sem.at[0, k], tok_sem.at[1, k], (zp, h, y))
        )
        tok_forwards.append(
            remote(tok.at[zp, my_half], tok.at[zp, my_half], tok_sem.at[2, k], tok_sem.at[3, k], dev_core)
        )
    for copy in tok_copies:
        copy.start()
    tok_own = pltpu.make_async_copy(tokens.at[z], tok.at[z], loc_sem.at[0])
    tok_own.start()
    wq_own = pltpu.make_async_copy(w_qkv, wq, loc_sem.at[1])
    wq_own.start()

    chunks = [(w_out, wo, w_out.shape[0] // 2, 0, w_out.shape[0] // 2)]
    deep = w_in.shape[0] // 2
    for i in range(4):
        chunks.append((w_in, wi, deep, i * (deep // 4), deep // 4))
    deep = w_down.shape[0] // 4
    for i in range(4):
        chunks.append((w_down, wd, deep, i * (deep // 4), deep // 4))
    over_x, over_y, core_x, core_y = [], [], [], []
    for i, (src, dst, deep, offset, size) in enumerate(chunks):
        mine = rows_at(y * deep + offset, size)
        other = rows_at((1 - y) * deep + offset, size)
        over_x.append(remote(src.at[mine], dst.at[h, mine], x_sem.at[0, i], x_sem.at[1, i], dev_x))
        over_y.append(remote(dst.at[hx, mine], dst.at[hx, mine], y_sem.at[0, i], y_sem.at[1, i], dev_y))
        core_x.append(remote(dst.at[hx, mine], dst.at[hx, mine], c1_sem.at[0, i], c1_sem.at[1, i], dev_core))
        core_y.append(remote(dst.at[hx, other], dst.at[hx, other], c2_sem.at[0, i], c2_sem.at[1, i], dev_core))
    n_chunks = len(chunks)
    base, size = w_down.shape[0] // 2, w_down.shape[0] // 8
    lower = rows_at(base + z * size, size, 128)
    part = rows_at(base + z * size + y * (size // 2), size // 2)
    lower_x = remote(w_down.at[part], wd.at[h, part], x_sem.at[0, 9], x_sem.at[1, 9], dev_x)
    lower_y = remote(wd.at[hx, part], wd.at[hx, part], y_sem.at[0, 9], y_sem.at[1, 9], dev_y)
    lower_core = [remote(wd.at[hx, lower], wd.at[hx, lower], c1_sem.at[0, 9], c1_sem.at[1, 9], dev_core)]
    lower_z = []
    for k, zp in enumerate(zs):
        theirs = rows_at(base + zp * size, size, 128)
        lower_z.append(
            remote(wd.at[hx, lower], wd.at[hx, lower], lower_sem.at[0, k], lower_sem.at[1, k], (zp, h, y))
        )
        lower_core.append(
            remote(wd.at[hx, theirs], wd.at[hx, theirs], lower_sem.at[2, k], lower_sem.at[3, k], dev_core)
        )
    x_queue = [over_x[0], lower_x] + over_x[1:]
    for copy in x_queue[:AHEAD]:
        copy.start()

    def serve_x(place):
        x_queue[place].wait_recv()
        if place == 1:
            lower_y.start()
        else:
            i = place - 1 if place else 0
            over_y[i].start()
            core_x[i].start()
        if place + AHEAD < len(x_queue):
            x_queue[place + AHEAD].start()

    def serve_y(i):
        over_y[i].wait_recv()
        core_y[i].start()

    own_weights, core_weights = [], []
    for i, (src, dst) in enumerate(((w_out, wo), (w_in, wi), (w_down, wd))):
        own_weights.append(pltpu.make_async_copy(src, dst.at[h], loc_sem.at[2 + i]))
        core_weights.append(remote(src, dst.at[h], core_sem.at[0, i], core_sem.at[1, i], dev_core))

    spot = lax.broadcasted_iota(jnp.int32, (8, width), 1) + z * width
    for s in range(4):
        live = (jnp.broadcast_to(key_mask[s : s + 1, :], (8, width)) == 1) & (spot < lengths[s])
        bias_s[s] = jnp.where(live, 0.0, NEG_FILL)
    bias_g[z] = bias_s[z]
    bias_copies = [
        remote(bias_s.at[zp], bias_g.at[z], bias_sem.at[0, k], bias_sem.at[1, k], (zp, h, y))
        for k, zp in enumerate(zs)
    ]
    fb[h] = jnp.broadcast_to(ffn_bias[...], fb.shape[1:])
    fb_copies = [
        remote(fb.at[h], fb.at[h], fb_sem.at[0, k], fb_sem.at[1, k], device)
        for k, device in enumerate((dev_core, dev_x, dev_diag))
    ]
    for copy in bias_copies + fb_copies:
        copy.start()
    for copy in own_weights + core_weights:
        copy.start()

    my_piece = rows_at(h * piece, piece)
    cot_copies = [
        remote(cot.at[zp, my_piece], cotg.at[z], cot_sem.at[0, k], cot_sem.at[1, k], (zp, h, y))
        for k, zp in enumerate(zs)
    ]
    cot_own = pltpu.make_async_copy(cot.at[z, my_piece], cotg.at[z], loc_sem.at[5])
    cot_own.start()

    inside, spare = lane_masks()

    pk = prefix[0].astype(BF)
    pv = prefix[1].astype(BF)
    k_s[total : total + slots, :] = pk
    v_s[total : total + slots, :] = pv
    for head in range(4):
        pair, par = head // 2, head % 2
        part = pk[:, 128 * pair : 128 * pair + 128].astype(F32)
        kx[head, total : total + slots, :] = jnp.where(inside[par], part, 0.0).astype(BF)
        vtx[head, HEAD_DIM:, :] = jnp.ones((vtx.shape[1] - HEAD_DIM, vtx.shape[2]), BF)

    def project(block):
        rows = tok[block]
        for i, target in enumerate((q_s, k_s, v_s)):
            value = (nn(rows, wq[i]) + proj_bias[i : i + 1, :]).astype(BF)
            if i == 0:
                value = (value.astype(F32) * HEAD_DIM**-0.5).astype(BF)
            for j in range(4):
                target[rows_at(j * width + block * piece, piece), :] = value[piece * j : piece * j + piece]
            if i == 1:
                column = jnp.broadcast_to(bias_g[block][0:1, :], (128, width)).T
                for head in range(4):
                    pair, par = head // 2, head % 2
                    part = value[:, 128 * pair : 128 * pair + 128].astype(F32)
                    ext = jnp.where(inside[par], part, jnp.where(spare[par], column, 0.0)).astype(BF)
                    for j in range(4):
                        kx[head, rows_at(j * width + block * piece, piece), :] = ext[piece * j : piece * j + piece]

    tok_own.wait()
    wq_own.wait()
    project(z)
    serve_x(0)
    for k, zp in enumerate(zs):
        serve_x(k + 1)
        if k != 1:
            serve_y(k // 2)
        tok_copies[k].wait_recv()
        tok_forwards[k].start()
        bias_copies[k].wait_recv()
        if k == 2:
            lower_y.wait_recv()
            for copy in lower_core[:1] + lower_z + cot_copies:
                copy.start()
        tok_forwards[k].wait_recv()
        project(zp)

    for i in range(4):
        flipped = v_s[i * width : (i + 1) * width, :].astype(F32).T.astype(BF)
        for head in range(4):
            vtx[head, 0:HEAD_DIM, i * width : (i + 1) * width] = flipped[HEAD_DIM * head : HEAD_DIM * (head + 1)]
    flipped = v_s[total : total + slots, :].astype(F32).T.astype(BF)
    for head in range(4):
        vtx[head, 0:HEAD_DIM, total : total + slots] = flipped[HEAD_DIM * head : HEAD_DIM * (head + 1)]

    def att_copy(u):
        j = member(h, u)
        return remote(att_loc.at[j], att_all.at[h], att_sem.at[0, u], att_sem.at[1, u], (z, j, y))

    def attend(step):
        u = 3 - step
        j = member(h, u)
        outs, recips = [], []
        for head in range(4):
            pair, par = head // 2, head % 2
            part = q_s[rows_at(j * width, width, width), 128 * pair : 128 * pair + 128].astype(F32)
            ext = jnp.where(inside[par], part, jnp.where(spare[par], 1.0, 0.0)).astype(BF)
            scores = nt(kx[head], ext)
            top = jnp.max(scores, axis=0, keepdims=True)
            weight = jnp.exp(scores - top).astype(BF)
            pt[head, j] = weight
            summed = nn(vtx[head], weight)
            recip = 1.0 / summed[HEAD_DIM : HEAD_DIM + 1]
            outs.append(summed[0:HEAD_DIM] * recip)
            recips.append(jnp.broadcast_to(recip, (32, width)))
        att_loc[j] = jnp.concatenate(outs, axis=0).T.astype(BF)
        rl_s[j] = jnp.concatenate(recips, axis=0).T

        @pl.when(u > 0)
        def _():
            att_copy(u).start()

        @pl.when(u == 0)
        def _():
            att_all[h] = att_loc[h]

    pl.loop(0, 2)(attend)
    serve_x(4)
    serve_y(2)
    pl.loop(2, 4)(attend)
    serve_x(5)
    serve_y(3)
    att_copies = [att_copy(u) for u in (1, 2, 3)]

    lane = lax.broadcasted_iota(jnp.int32, (1, 128), 1)
    spare_lo = [lane == HEAD_DIM + 1, lane == 1]
    for head in range(4):
        pair, par = head // 2, head % 2
        part = v_s[:, 128 * pair : 128 * pair + 128].astype(F32)
        ones = jnp.where(spare[par] | spare_lo[par], 1.0, 0.0)
        kx[head] = jnp.where(inside[par], part, ones).astype(BF)
    for i in range(5):
        low, size = i * width, width if i < 4 else slots
        flipped = k_s[low : low + size, :].astype(F32).T.astype(BF)
        for head in range(4):
            vtx[head, 0:HEAD_DIM, low : low + size] = flipped[HEAD_DIM * head : HEAD_DIM * (head + 1)]

    serve_x(6)

    own_weights[0].wait()
    core_weights[0].wait_recv()
    core_x[0].wait_recv()
    core_y[0].wait_recv()
    for copy in att_copies:
        copy.wait_recv()
    attention = nn(att_all[0], wo[0])
    for j in range(1, 4):
        attention += nn(att_all[j], wo[j])
    mine = jnp.concatenate([tok[b, my_piece, :] for b in range(4)], axis=0).astype(F32)
    resid = mine + attention + shifts[0:1, :]
    centred = resid - jnp.mean(resid, axis=-1, keepdims=True)
    inverse_one = lax.rsqrt(jnp.mean(centred * centred, axis=-1, keepdims=True) + NORM_EPSILON)
    xhat = centred * inverse_one
    xhat_s[...] = xhat
    normed = xhat * gains[0:1, :] + shifts[1:2, :]
    normed_s[...] = normed
    nb_s[...] = normed.astype(BF)

    tile = 256
    tiles = wi.shape[2] // tile

    def ffn_in(quarter):
        @pl.loop(0, tiles, unroll=4)
        def _(n):
            cols = rows_at(n * tile, tile, tile)
            inner = nn(nb_s[...], wi[quarter, :, cols]) + fb[quarter, 0:1, cols]
            cdf = 0.5 * (1.0 + lax.erf(inner * 0.7071067811865476))
            act[quarter, :, cols] = (inner * cdf).astype(BF)
            gp[quarter, :, cols] = cdf + inner * (jnp.exp(-0.5 * inner * inner) * 0.3989422804014327)

    for copy in fb_copies:
        copy.wait_recv()
    own_weights[1].wait()
    core_weights[1].wait_recv()
    ffn_in(h)
    serve_x(7)
    ffn_in(hc)
    serve_y(4)
    serve_x(8)
    for i in range(1, 5):
        core_x[i].wait_recv()
        core_y[i].wait_recv()
    ffn_in(hx)
    ffn_in(hd_)

    acc[...] = jnp.zeros(acc.shape, F32)

    def ffn_out(quarter, start, deep):
        span = rows_at(start, deep, deep)

        @pl.loop(0, tiles, unroll=4)
        def _(n):
            cols = rows_at(n * tile, tile, tile)
            acc[:, cols] += nn(act[quarter, :, span], wd[quarter, span, cols])

    own_weights[2].wait()
    core_weights[2].wait_recv()
    deep = wd.shape[1]
    for k in range(3):
        lower_z[k].wait_recv()
        lower_core[k + 1].start()
    ffn_out(h, 0, deep)
    serve_x(9)
    serve_y(5)
    serve_y(6)
    ffn_out(hc, 0, deep)
    serve_y(7)
    ffn_out(hx, base, deep // 2)
    for copy in lower_core:
        copy.wait_recv()
    ffn_out(hd_, base, deep // 2)
    for i in range(5, 9):
        core_x[i].wait_recv()
    ffn_out(hx, y * (deep // 4), deep // 4)
    ffn_out(hd_, y * (deep // 4), deep // 4)
    serve_y(8)
    ffn_out(hx, (1 - y) * (deep // 4), deep // 4)
    for i in range(5, 9):
        core_y[i].wait_recv()
    ffn_out(hd_, (1 - y) * (deep // 4), deep // 4)

    resid = normed_s[...] + acc[...] + shifts[2:3, :]
    centred = resid - jnp.mean(resid, axis=-1, keepdims=True)
    inverse = lax.rsqrt(jnp.mean(centred * centred, axis=-1, keepdims=True) + NORM_EPSILON)
    xhat = centred * inverse
    lo_s[...] = (xhat * gains[1:2, :] + shifts[3:4, :]).astype(BF)
    x_piece = rows_at(hx * piece, piece)
    lo_z, lo_x, lo_core, lo_across = [], [], [], []
    blocks = zs + [z]
    for k, b in enumerate(blocks):
        rows = rows_at(b * piece, piece)
        source = lo_all.at[b, my_piece]
        if k < 3:
            lo_z.append(remote(lo_s.at[rows], lo_all.at[z, my_piece], lo_sem.at[0, k], lo_sem.at[1, k], (b, h, y)))
        else:
            source = lo_s.at[rows]
        lo_x.append(remote(source, lo_all.at[b, my_piece], lox_sem.at[0, k], lox_sem.at[1, k], dev_x))
        lo_core.append(remote(source, lo_all.at[b, my_piece], loc_lo_sem.at[0, k], loc_lo_sem.at[1, k], dev_core))
        lo_across.append(
            remote(lo_all.at[b, x_piece], lo_all.at[b, x_piece], lox_core_sem.at[0, k], lox_core_sem.at[1, k], dev_core)
        )
    lo_own = pltpu.make_async_copy(lo_s.at[rows_at(z * piece, piece)], lo_all.at[z, my_piece], out_sem.at[0])
    for copy in lo_z + [lo_x[3], lo_core[3], lo_own]:
        copy.start()

    def serve_lo(k):
        lo_z[k].wait_recv()
        lo_x[k].start()
        lo_core[k].start()

    cot_own.wait()
    for copy in cot_copies:
        copy.wait_recv()
    dy = jnp.concatenate([cotg[b] for b in range(4)], axis=0).astype(F32) * gains[1:2, :]
    g_two = inverse * (
        dy - jnp.mean(dy, axis=-1, keepdims=True) - xhat * jnp.mean(dy * xhat, axis=-1, keepdims=True)
    )
    acc[...] = g_two
    nb_s[...] = g_two.astype(BF)

    @pl.loop(0, 4, unroll=4)
    def _(quarter):
        @pl.loop(0, tiles, unroll=4)
        def _(n):
            cols = rows_at(n * tile, tile, tile)
            d_act = nt(nb_s[...], wd[quarter, cols, :])
            act[quarter, :, cols] = (d_act * gp[quarter, :, cols]).astype(BF)

    @pl.loop(0, 4, unroll=4)
    def _(quarter):
        @pl.loop(0, tiles, unroll=4)
        def _(n):
            cols = rows_at(n * tile, tile, tile)
            acc[:, cols] += nt(act[quarter], wi[quarter, cols, :])

    dy = acc[...] * gains[0:1, :]
    xhat = xhat_s[...]
    g_one = inverse_one * (
        dy - jnp.mean(dy, axis=-1, keepdims=True) - xhat * jnp.mean(dy * xhat, axis=-1, keepdims=True)
    )
    acc[...] = g_one
    low = g_one.astype(BF)
    da_copies = {}
    for u in (2, 3, 1):
        j = member(h, u)
        da_s[j] = nt(low, wo[j]).astype(BF)
        da_copies[u] = remote(da_s.at[j], da_all.at[h], da_sem.at[0, u], da_sem.at[1, u], (z, j, y))
        da_copies[u].start()
    da_all[h] = nt(low, wo[h]).astype(BF)
    for copy in over_y + [lower_y] + core_x + core_y + lower_z + lower_core:
        copy.wait_send()

    def score_grads(u):
        j = member(h, u)

        @pl.when(u > 0)
        def _():
            remote(da_s.at[j], da_all.at[h], da_sem.at[0, u], da_sem.at[1, u], (z, j, y)).wait_recv()

        grads = []
        for head in range(4):
            pair, par = head // 2, head % 2
            lanes = slice(128 * pair, 128 * pair + 128)
            d_out = da_all[j, :, lanes].astype(F32)
            recip = rl_s[j, :, 32 * head : 32 * head + 1]
            delta = recip * jnp.sum(
                jnp.where(inside[par], d_out * att_loc[j, :, lanes].astype(F32), 0.0), axis=-1, keepdims=True
            )
            high = delta.astype(BF).astype(F32)
            ext = jnp.where(spare[par], -high, jnp.where(spare_lo[par], high - delta, 0.0))
            ext = jnp.where(inside[par], d_out * recip, ext).astype(BF)
            dox[head, j] = ext
            d_probs = nt(kx[head], ext).astype(BF)
            d_scores = pt[head, j] * d_probs
            wi[head, :, rows_at(j * width, width, width)] = d_scores[0:total]
            ds_pre[head, j] = d_scores[total:]
            grads.append(nn(vtx[head, 0:HEAD_DIM, :], d_scores))
        dq_s[j] = (jnp.concatenate(grads, axis=0).T * HEAD_DIM**-0.5).astype(BF)

    pl.loop(0, 2)(score_grads)
    serve_lo(0)
    serve_lo(1)
    serve_lo(2)
    pl.loop(2, 4)(score_grads)

    def key_side(left, right):
        halves = []
        for pair in range(2):
            sides = []
            for par in range(2):
                head = 2 * pair + par
                value = nn(left(head, 0), right(head, 0, pair))
                for j in range(1, 4):
                    value += nn(left(head, j), right(head, j, pair))
                sides.append(value)
            halves.append(jnp.where(inside[0], sides[0], sides[1]))
        return jnp.concatenate(halves, axis=-1)

    def d_values(rows):
        return key_side(lambda head, j: pt[head, j, rows, :], lambda head, j, pair: dox[head, j])

    def d_keys(left):
        return key_side(left, lambda head, j, pair: q_s[j * width : (j + 1) * width, 128 * pair : 128 * pair + 128])

    def partial(i):
        rows = rows_at(i * width, width, width)
        dk = d_keys(lambda head, j: wi[head, rows, j * width : (j + 1) * width]).astype(BF)
        dv = d_values(rows).astype(BF)
        return nt(dq_s[i], wq[0]) + nt(dk, wq[1]) + nt(dv, wq[2])

    part_core = [
        remote(core_out.at[i], core_in.at[i], part_core_sem.at[0, i], part_core_sem.at[1, i], dev_core) for i in range(2)
    ]
    part_x = []
    for k, b in enumerate(blocks):
        rows = rows_at(b * piece, piece)
        part_x.append(remote(x_out.at[rows], x_in.at[rows], part_x_sem.at[0, k], part_x_sem.at[1, k], dev_x))

    core_out[0] = partial(hd_).astype(BF)
    part_core[0].start()
    mine = partial(hx)
    part_core[0].wait_recv()
    x_out[...] = (mine + core_in[0].astype(F32)).astype(BF)
    for copy in part_x:
        copy.start()

    pre_part[0] = d_keys(lambda head, j: ds_pre[head, j])
    pre_part[1] = d_values(pl.ds(total, slots))
    few = slots // 8
    mine_rows = rows_at(group * few, few, few)
    pre_copies, pre_back = [], []
    for d, g in enumerate(others):
        device = (g // 2, h, lax.rem(g, 2))
        pre_copies.append(
            remote(pre_part.at[:, rows_at(g * few, few, few)], pre_land.at[d], pre_sem.at[0, d], pre_sem.at[1, d], device)
        )
        pre_back.append(
            remote(pre_sum.at[:, mine_rows], pre_sum.at[:, mine_rows], pre2_sem.at[0, d], pre2_sem.at[1, d], device)
        )
    for copy in pre_copies:
        copy.start()
    for k in (3, 0, 1, 2):
        lo_x[k].wait_recv()
        lo_across[k].start()

    core_out[1] = partial(hc).astype(BF)
    part_core[1].start()
    acc[...] += partial(h)
    part_core[1].wait_recv()
    acc[...] += core_in[1].astype(F32)

    igz, igx, igc, igcx = [], [], [], []
    for k, b in enumerate(blocks):
        rows = rows_at(b * piece, piece)
        source = ig_all.at[b, my_piece]
        if k < 3:
            igz.append(remote(fin.at[rows], ig_all.at[z, my_piece], igz_sem.at[0, k], igz_sem.at[1, k], (b, h, y)))
        else:
            source = fin.at[rows]
        igx.append(remote(source, ig_all.at[b, my_piece], igx_sem.at[0, k], igx_sem.at[1, k], dev_x))
        igc.append(remote(source, ig_all.at[b, my_piece], igc_sem.at[0, k], igc_sem.at[1, k], dev_core))
        igcx.append(
            remote(ig_all.at[b, x_piece], ig_all.at[b, x_piece], igcx_sem.at[0, k], igcx_sem.at[1, k], dev_core)
        )
    ig_own = pltpu.make_async_copy(fin.at[rows_at(z * piece, piece)], ig_all.at[z, my_piece], out_sem.at[1])
    for k, b in enumerate(blocks):
        rows = rows_at(b * piece, piece)
        part_x[k].wait_recv()
        fin[rows, :] = (acc[rows, :] + x_in[rows, :].astype(F32)).astype(BF)
        if k < 3:
            igz[k].start()
        else:
            ig_own.start()
            igx[3].start()
            igc[3].start()
        if k == 1:
            for copy in pre_copies:
                copy.wait_recv()
            for i in range(2):
                term = pre_part[i, mine_rows, :]
                for d in range(7):
                    term += pre_land[d, i]
                pre_sum[i, mine_rows, :] = term
            for copy in pre_back:
                copy.start()
    for copy in lo_core + lo_across:
        copy.wait_recv()
    lo_own.wait()
    for k in range(3):
        igz[k].wait_recv()
        igx[k].start()
        igc[k].start()
    for copy in pre_back:
        copy.wait_recv()
    pre_o[...] = pre_sum[...]
    for k in (3, 0, 1, 2):
        igx[k].wait_recv()
        igcx[k].start()
    for copy in igc + igcx:
        copy.wait_recv()
    ig_own.wait()
    sent = tok_copies + tok_forwards + x_queue + core_weights + bias_copies + fb_copies + cot_copies + att_copies
    sent += lo_z + lo_x + lo_core + lo_across + list(da_copies.values()) + part_core + part_x
    for copy in sent + igz + igx + igc + igcx + pre_copies + pre_back:
        copy.wait_send()


def layer(tokens, cot, w_qkv, w_out, w_in, w_down, prefix, proj_bias, ffn_bias, gains, shifts, lengths, key_mask):
    seqs, width, model = tokens.shape
    local = w_qkv.shape[2]
    hidden = w_in.shape[1]
    slots = prefix.shape[1]
    total = seqs * width
    keys = total + slots
    dma = pltpu.SemaphoreType.DMA
    hbm = pl.BlockSpec(memory_space=pl.ANY)
    vmem = pl.BlockSpec(memory_space=pltpu.VMEM)
    shape = jax.ShapeDtypeStruct
    return pl.pallas_call(
        layer_kernel,
        name="layer",
        out_shape=(
            pltpu.VMEM((4, width, model), BF),
            pltpu.VMEM((4, width, model), BF),
            pltpu.VMEM((2, slots, local), F32),
        ),
        in_specs=[hbm] * 6 + [vmem] * 5 + [pl.BlockSpec(memory_space=pltpu.SMEM), vmem],
        out_specs=(vmem, vmem, vmem),
        scratch_shapes=[
            pltpu.VMEM((4, width, model), BF),
            pltpu.VMEM((4, width // 4, model), BF),
            pltpu.VMEM((4, 8, width), F32),
            pltpu.VMEM((4, 8, width), F32),
            pltpu.VMEM((3, model, local), BF),
            pltpu.VMEM((4, local, model), BF),
            pltpu.VMEM((4, model, hidden), BF),
            pltpu.VMEM((4, hidden, model), BF),
            pltpu.VMEM((4, 8, hidden), F32),
            pltpu.VMEM((total, local), BF),
            pltpu.VMEM((keys, local), BF),
            pltpu.VMEM((keys, local), BF),
            pltpu.VMEM((4, keys, 128), BF),
            pltpu.VMEM((4, HEAD_DIM + 16, keys), BF),
            pltpu.VMEM((4, 4, keys, width), BF),
            pltpu.VMEM((4, width, local), BF),
            pltpu.VMEM((4, width, local), BF),
            pltpu.VMEM((4, width, 128), F32),
            pltpu.VMEM((width, model), F32),
            pltpu.VMEM((width, model), F32),
            pltpu.VMEM((width, model), BF),
            pltpu.VMEM((width, model), F32),
            pltpu.VMEM((4, width, hidden), BF),
            pltpu.VMEM((4, width, hidden), F32),
            pltpu.VMEM((width, model), BF),
            pltpu.VMEM((4, width, local), BF),
            pltpu.VMEM((4, width, local), BF),
            pltpu.VMEM((4, 4, slots, width), BF),
            pltpu.VMEM((4, 4, width, 128), BF),
            pltpu.VMEM((4, width, local), BF),
            pltpu.VMEM((2, width, model), BF),
            pltpu.VMEM((2, width, model), BF),
            pltpu.VMEM((width, model), BF),
            pltpu.VMEM((width, model), BF),
            pltpu.VMEM((width, model), BF),
            pltpu.VMEM((2, slots, local), F32),
            pltpu.VMEM((7, 2, slots // 8, local), F32),
            pltpu.VMEM((2, slots, local), F32),
            dma((6,)),
            dma((4,)),
            dma((4, 3)),
            dma((2, 3)),
            dma((2, 3)),
            dma((2, 3)),
            dma((2, 4)),
            dma((2, 3)),
            dma((2, 10)),
            dma((2, 10)),
            dma((2, 10)),
            dma((2, 10)),
            dma((4, 3)),
            dma((2, 3)),
            dma((2, 4)),
            dma((2, 4)),
            dma((2, 4)),
            dma((2, 4)),
            dma((2, 2)),
            dma((2, 4)),
            dma((2, 3)),
            dma((2, 4)),
            dma((2, 4)),
            dma((2, 4)),
            dma((2, 7)),
            dma((2, 7)),
        ],
        compiler_params=pltpu.CompilerParams(
            collective_id=0, has_side_effects=True, vmem_limit_bytes=58 * 2**20
        ),
        cost_estimate=pl.CostEstimate(flops=15 * 10**9, bytes_accessed=40 * 2**20, transcendentals=6 * 10**6),
    )(tokens, cot, w_qkv, w_out, w_in, w_down, prefix, proj_bias, ffn_bias, gains, shifts, lengths, key_mask)


def finish_kernel(lo, ig, grad, prefix, first, second, lo_o, ig_o, grad_o, new_o, first_o, second_o, lo_f, ig_f, sem):
    seqs = lo.shape[0]
    copies = []
    for i in range(seqs):
        for k, (src, mid, dst) in enumerate(((lo, lo_f, lo_o), (ig, ig_f, ig_o))):
            mid[i] = src[i].astype(F32)
            copy = pltpu.make_async_copy(mid.at[i], dst.at[i], sem.at[k, i])
            copy.start()
            copies.append(copy)
    slope = grad[...]
    grad_o[...] = slope
    new_first = BETA_ONE * first[...] + (1.0 - BETA_ONE) * slope
    new_second = BETA_TWO * second[...] + (1.0 - BETA_TWO) * slope * slope
    first_hat = new_first / (1.0 - BETA_ONE**STEP)
    second_hat = new_second / (1.0 - BETA_TWO**STEP)
    value = prefix[...]
    new_o[...] = value - LEARN_RATE * (first_hat / (jnp.sqrt(second_hat) + ADAM_EPSILON) + WEIGHT_DECAY * value)
    first_o[...] = new_first
    second_o[...] = new_second
    for copy in copies:
        copy.wait()


def finish(lo, ig, grad, prefix, first, second):
    hbm = pl.BlockSpec(memory_space=pl.ANY)
    vmem = pl.BlockSpec(memory_space=pltpu.VMEM)
    shape = jax.ShapeDtypeStruct
    whole, little = shape(lo.shape, F32), shape(prefix.shape, F32)
    return pl.pallas_call(
        finish_kernel,
        name="finish",
        out_shape=(whole, whole, little, little, little, little),
        in_specs=[vmem] * 6,
        out_specs=(hbm, hbm, vmem, vmem, vmem, vmem),
        scratch_shapes=[
            pltpu.VMEM(lo.shape, F32),
            pltpu.VMEM(lo.shape, F32),
            pltpu.SemaphoreType.DMA((2, lo.shape[0])),
        ],
        compiler_params=pltpu.CompilerParams(vmem_limit_bytes=40 * 2**20),
    )(lo, ig, grad, prefix, first, second)


def body(*args):
    (tokens, cotangent, prefix, first_moment, second_moment, w_qkv, proj_bias, w_out, w_in, ffn_bias) = args[:10]
    w_down, gains, shifts, lengths, key_mask = args[10:]
    fits = (
        lax.axis_size("seq") == 4
        and lax.axis_size("head") == 4
        and lax.axis_size("batch") == 2
        and tokens.shape == (4, 256, 1024)
        and w_qkv.shape == (3, 1024, 256)
        and w_in.shape == (1024, 1024)
        and prefix.shape[1] == 64
    )
    if not fits:
        return general_body(*args)
    layer_out, input_grad, prefix_grad = layer(
        tokens, cotangent, w_qkv, w_out, w_in, w_down, prefix, proj_bias, ffn_bias.reshape(1, -1), gains, shifts,
        lengths, key_mask,
    )
    layer_out, input_grad, prefix_grad, new_prefix, new_first, new_second = finish(
        layer_out, input_grad, prefix_grad, prefix, first_moment, second_moment
    )
    return layer_out, input_grad, prefix_grad, new_prefix, new_first, new_second


def solution(mesh):
    placed = (
        P("batch", "seq", None),
        P("batch", "seq", None),
        P(None, None, "head"),
        P(None, None, "head"),
        P(None, None, "head"),
        P(None, None, "head"),
        P(None, "head"),
        P("head", None),
        P(None, "head"),
        P("head"),
        P("head", None),
        P(),
        P(),
        P("batch"),
        P("batch", "seq"),
    )
    return jax.shard_map(
        body,
        mesh=mesh,
        in_specs=placed,
        out_specs=(
            P("batch", "seq", None),
            P("batch", "seq", None),
            P(None, None, "head"),
            P(None, None, "head"),
            P(None, None, "head"),
            P(None, None, "head"),
        ),
        check_vma=False,
    )
```
